32 devices in a mesh: cell: 16 (over z, y, x), gene: 2 (over core).
Axes of the slice: x: 2, y: 2, z: 4, core: 2. Of those that a mesh axis runs over, the one named last changes fastest.
Arguments:
- gene_in: bfloat16 [64, 2048, 256], P('cell', 'gene'), may hold values from -6 to 6
- class_in: bfloat16 [64, 8, 256], P('cell'), may hold values from -6 to 6
- expressed: int32 [64], P('cell'), may hold values from 256 to 2048, as said below
- ln1_gain: float32 [256], replicated, may hold values from 0.1 to 1.9
- ln1_bias: float32 [256], replicated, may hold values from -1.75 to 1.75
- w_qkv: bfloat16 [256, 768], replicated, may hold values from -0.375 to 0.375
- w_out: bfloat16 [256, 256], replicated, may hold values from -10 to 10
- ln2_gain: float32 [256], replicated, may hold values from 0.1 to 1.9
- ln2_bias: float32 [256], replicated, may hold values from -1.75 to 1.75
- w_up: bfloat16 [256, 1024], replicated, may hold values from -0.375 to 0.375
- b_up: float32 [1024], replicated, may hold values from -1.75 to 1.75
- w_down: bfloat16 [1024, 256], replicated, may hold values from -0.1875 to 0.1875
- b_down: float32 [256], replicated, may hold values from -1.75 to 1.75
- gene_cot: bfloat16 [64, 2048, 256], P('cell', 'gene'), may hold values from -6 to 6
- class_cot: bfloat16 [64, 8, 256], P('cell'), may hold values from -6 to 6
Outputs:
- gene_out: bfloat16 [64, 2048, 256], P('cell', 'gene')
- class_out: bfloat16 [64, 8, 256], P('cell')
- gene_grad: bfloat16 [64, 2048, 256], P('cell', 'gene')
- class_grad: bfloat16 [64, 8, 256], P('cell')
- grad_ln1_gain: float32 [256], replicated
- grad_ln1_bias: float32 [256], replicated
- grad_qkv: float32 [256, 768], replicated
- grad_out: float32 [256, 256], replicated
- grad_ln2_gain: float32 [256], replicated
- grad_ln2_bias: float32 [256], replicated
- grad_up: float32 [256, 1024], replicated
- grad_up_bias: float32 [1024], replicated
- grad_down: float32 [1024, 256], replicated
- grad_down_bias: float32 [256], replicated
The draws below stay inside these ranges and needn't reach their ends.
Inputs may be any that keep to these rules, and one draw needn't show every extreme that they name: Each cell's gene tokens at positions below its count are expressed, the others are padding. In each aligned block of 4 cells (the cells of one index of the cell axis) one cell has all 2048 and another has 256.
All inputs are finite; a program needn't handle non-finite values.
Results may differ from the reference program's by a relative error of at most 0.015.
Values may be sent and summed in bfloat16 or wider, within the bound.
A program may use at most 256 MiB of HBM per device.

```python
import jax
import jax.numpy as jnp
from jax import lax

D = 256
HEADS = 4
HEAD = 64
FF = 1024
CLS = 8
GENES = 2048
C_DEV = 4
CELLS = 64


def draw_expressed(key, part):
    key = jax.random.fold_in(key, 11)
    tail_key, pick_key = jax.random.split(key)
    floor_length = GENES // 8
    random_base = jax.random.randint(tail_key, (CELLS,), 0, 256)
    lengths = floor_length + (GENES - floor_length) * random_base * random_base // 65536
    chosen = jnp.repeat(jax.random.randint(pick_key, (CELLS // C_DEV,), 0, C_DEV), C_DEV)
    slot_index = jnp.arange(CELLS) % C_DEV
    lengths = jnp.where(slot_index == (chosen + 1) % C_DEV, floor_length, lengths)
    return jnp.where(slot_index == chosen, GENES, lengths).astype(jnp.int32)


def block_scale(rng, shape, cuts, smallest, largest):
    level = 1.0
    for position, blocks in cuts:
        steps = jax.random.uniform(jax.random.fold_in(jax.random.fold_in(rng, 6), position), (blocks,), jnp.float32, smallest / len(cuts), largest / len(cuts))
        level = level * jnp.repeat(jnp.exp(steps), shape[position] // blocks).reshape((-1,) + (1,) * (len(shape) - 1 - position))
    return level


def scatter_about(own_key, extent, width, most, shards=(), held_as=jnp.bfloat16):
    factor_of = block_scale(own_key, extent, shards, -0.22, 0.18) if shards else 1.0
    entries = jax.random.normal(own_key, extent, jnp.float32) * width * factor_of
    return jnp.minimum(jnp.maximum(entries, -most), most).astype(held_as)


def setup_inputs(seed: int = 0) -> dict:
    arg_keys = jax.random.split(jax.random.key(seed), 16)
    gene_in = scatter_about(arg_keys[0], (CELLS, GENES, D), 1.0, 6.0, ((0, 16), (1, 2)))
    class_in = scatter_about(arg_keys[1], (CELLS, CLS, D), 1.0, 6.0, ((0, 16),))
    expressed = draw_expressed(jax.random.fold_in(arg_keys[15], 71), 0)
    ln1_gain = jnp.clip(1.0 + 0.18 * jax.random.normal(arg_keys[3], (D,), jnp.float32), 0.1, 1.9)
    ln1_bias = scatter_about(arg_keys[4], (D,), 0.3, 1.75, (), jnp.float32)
    w_qkv = scatter_about(arg_keys[5], (D, 3 * D), D ** -0.5, 0.375)
    w_out = scatter_about(arg_keys[6], (D, D), 1.6, 10.0)
    ln2_gain = jnp.clip(1.0 + 0.18 * jax.random.normal(arg_keys[7], (D,), jnp.float32), 0.1, 1.9)
    ln2_bias = scatter_about(arg_keys[8], (D,), 0.3, 1.75, (), jnp.float32)
    w_up = scatter_about(arg_keys[9], (D, FF), D ** -0.5, 0.375)
    b_up = scatter_about(arg_keys[10], (FF,), 0.3, 1.75, (), jnp.float32)
    w_down = scatter_about(arg_keys[11], (FF, D), FF ** -0.5, 0.1875)
    b_down = scatter_about(arg_keys[12], (D,), 0.3, 1.75, (), jnp.float32)
    gene_cot = scatter_about(arg_keys[13], (CELLS, GENES, D), 1.0, 6.0, ((0, 16), (1, 2)))
    class_cot = scatter_about(arg_keys[14], (CELLS, CLS, D), 1.0, 6.0, ((0, 16),))
    return {"gene_in": gene_in, "class_in": class_in, "expressed": expressed, "ln1_gain": ln1_gain, "ln1_bias": ln1_bias, "w_qkv": w_qkv, "w_out": w_out, "ln2_gain": ln2_gain, "ln2_bias": ln2_bias, "w_up": w_up, "b_up": b_up, "w_down": w_down, "b_down": b_down, "gene_cot": gene_cot, "class_cot": class_cot}


@jax.custom_vjp
def low(v):
    return lax.optimization_barrier(v.astype(jnp.bfloat16)).astype(jnp.float32)

@jax.custom_vjp
def low_back(v):
    return v

def low_keep(v):
    return (low(v), None)

def low_pass(kept, grad):
    return (grad,)

def back_keep(v):
    return (v, None)

def back_low(kept, grad):
    return (low(grad),)
low.defvjp(low_keep, low_pass)
low_back.defvjp(back_keep, back_low)
EPS = 1e-05
NEG = -1e+30

def product(left, right):
    return jnp.dot(left, right, precision=lax.Precision.HIGHEST, preferred_element_type=jnp.float32)

def normalize(values, gain, bias):
    average = lax.optimization_barrier(jnp.mean(values, -1, keepdims=True))
    centered = values - average
    spread = lax.optimization_barrier(jnp.mean(centered * centered, -1, keepdims=True))
    return centered * lax.rsqrt(spread + EPS) * gain + bias

def cell_layer(params, tokens, length):
    ln1_gain, ln1_bias, w_qkv, w_out, ln2_gain, ln2_bias, w_up, b_up, w_down, b_down = params
    row_count = tokens.shape[0]
    hidden = low(normalize(tokens, ln1_gain, ln1_bias))
    packed = low_back(low(product(hidden, w_qkv)))
    queries = packed[:, :D].reshape(row_count, HEADS, HEAD)
    key_heads = packed[:, D:2 * D].reshape(row_count, HEADS, HEAD)
    values = packed[:, 2 * D:].reshape(row_count, HEADS, HEAD)
    scores = jnp.einsum('qhd,khd->hqk', queries, key_heads, precision=lax.Precision.HIGHEST) * HEAD ** (-0.5)
    scores = low_back(scores)
    positions = jnp.arange(row_count, dtype=jnp.int32)
    key_valid = (positions < CLS) | (positions - CLS < length)
    scores = jnp.where(key_valid[None, None, :], scores, NEG)
    weights = low(jax.nn.softmax(scores, axis=-1))
    attended = jnp.einsum('hqk,khd->qhd', weights, values, precision=lax.Precision.HIGHEST).reshape(row_count, D)
    attended = low(low_back(attended))
    middle = tokens + low_back(product(attended, w_out))
    second_hidden = low(normalize(middle, ln2_gain, ln2_bias))
    up_proj = low_back(product(second_hidden, w_up) + b_up)
    activated = low(jax.nn.gelu(up_proj, approximate=False))
    return middle + product(activated, w_down) + b_down

def reference(gene_in, class_in, expressed, ln1_gain, ln1_bias, w_qkv, w_out, ln2_gain, ln2_bias, w_up, b_up, w_down, b_down, gene_cot, class_cot):
    params = tuple((entry.astype(jnp.float32) for entry in (ln1_gain, ln1_bias, w_qkv, w_out, ln2_gain, ln2_bias, w_up, b_up, w_down, b_down)))
    tokens = jnp.concatenate([class_in, gene_in], axis=1).astype(jnp.float32)
    cotangent = jnp.concatenate([class_cot, gene_cot], axis=1).astype(jnp.float32)

    def forward(weights, inputs):
        cell_step = jax.checkpoint(cell_layer)

        def visit_cell(carried, entry_pair):
            return (carried, cell_step(weights, entry_pair[0], entry_pair[1]))
        return lax.scan(visit_cell, jnp.zeros((), jnp.float32), (inputs, expressed))[1]
    result, pullback = jax.vjp(forward, params, tokens)
    weight_grads, token_grads = pullback(cotangent)
    return (result[:, CLS:].astype(jnp.bfloat16), result[:, :CLS].astype(jnp.bfloat16), token_grads[:, CLS:].astype(jnp.bfloat16), token_grads[:, :CLS].astype(jnp.bfloat16), weight_grads[0], weight_grads[1], weight_grads[2], weight_grads[3], weight_grads[4], weight_grads[5], weight_grads[6], weight_grads[7], weight_grads[8], weight_grads[9])
```

```python
import functools

import jax
import jax.numpy as jnp
from jax import lax
from jax.experimental import pallas as pl
from jax.experimental.pallas import tpu as pltpu
from jax.sharding import PartitionSpec as P

HEADS = 4
EPS = 1e-05
LOG2E = 1.4426950408889634
SAFE = 40.0
KB = 256
VMEM = 63 * 2**20
F32 = jnp.float32
BF16 = jnp.bfloat16


def dot(left, right):
    return jnp.dot(left, right, preferred_element_type=F32)


def dot_nt(left, right):
    return lax.dot_general(left, right, (((1,), (1,)), ((), ())), preferred_element_type=F32)


def dot_tn(left, right):
    return lax.dot_general(left, right, (((0,), (0,)), ((), ())), preferred_element_type=F32)


def spread_column(row):
    return jnp.broadcast_to(row, (128, row.shape[1])).T


def widen(column, lanes):
    return jnp.concatenate([column] * (lanes // 128), axis=1)


def fold_lanes(values):
    total = values[:, :128]
    for start in range(128, values.shape[1], 128):
        total = total + values[:, start : start + 128]
    return total


def norm_rows(values):
    centered = values - jnp.mean(values, -1, keepdims=True)
    inverse = lax.rsqrt(jnp.mean(centered * centered, -1, keepdims=True) + EPS)
    return centered * inverse, inverse


def norm_columns(values):
    scale = 1.0 / values.shape[0]
    centered = values - jnp.sum(values, 0, keepdims=True) * scale
    inverse = lax.rsqrt(jnp.sum(centered * centered, 0, keepdims=True) * scale + EPS)
    return centered * inverse, inverse


def project_kernel(
    counts, place, x, xc, gain, bias, w, qt, qr, kr, vr, kt, va, stat, pc, w_t, gain_c, bias_c
):
    cell, half = pl.program_id(0), pl.program_id(1)
    genes, width = x.shape[1:]
    head = width // HEADS

    @pl.when((cell == 0) & (half == 0))
    def _():
        w_t[...] = w[...].T
        gain_c[...] = spread_column(gain[...])
        bias_c[...] = spread_column(bias[...])

    stat[...] = jnp.zeros_like(stat)
    own = half == place[0]
    needed = half * genes < counts[cell]

    def low_rows():
        unit, _ = norm_columns(x[0].T.astype(F32))
        return unit * widen(gain_c[...], genes) + widen(bias_c[...], genes)

    def norms(columns, first):
        for h in range(HEADS):
            part = columns[h * head : (h + 1) * head]
            size = jnp.sum(part * part, 0, keepdims=True)
            best = size[:, :128]
            for start in range(128, genes, 128):
                best = jnp.maximum(best, size[:, start : start + 128])
            stat[0, 0, first + h : first + h + 1, :] = best

    @pl.when(needed)
    def _():
        spot = half * genes + lax.broadcasted_iota(jnp.int32, (1, genes), 1)
        valid = spot < counts[cell]
        low = jnp.where(valid, low_rows(), 0.0).astype(BF16)
        low_r = low.T
        packed_t = dot(w_t[width:, :], low)
        kt[0] = packed_t[:width].astype(BF16)
        mark = jnp.where(
            (lax.broadcasted_iota(jnp.int32, (16, genes), 0) == 0) & valid, 1.0, 0.0
        ).astype(BF16)
        for h in range(HEADS):
            va[0, h, :head, :] = packed_t[width + h * head : width + (h + 1) * head].astype(BF16)
            va[0, h, head:, :] = mark
        packed = dot(low_r, w[:, width:])
        kr[0] = packed[:, :width].astype(BF16)
        vr[0] = packed[:, width:].astype(BF16)
        norms(packed_t[:width], 0)

    @pl.when(own)
    def _():
        low = low_rows().astype(BF16)
        query_t = dot(w_t[:width, :], low).astype(BF16) * (head**-0.5)
        qt[0] = query_t
        qr[0] = query_t.T
        norms(query_t.astype(F32), HEADS)

    @pl.when(half == 0)
    def _():
        unit, _ = norm_rows(xc[0].astype(F32))
        low = (unit * gain[...] + bias[...]).astype(BF16)
        pc[0] = dot(low, w[...]).astype(BF16).astype(F32)


def project(counts, place, x_all, xc, gain, bias, w):
    cells, total, width = x_all.shape
    genes = total // 2
    classes = xc.shape[1]
    head = width // HEADS
    whole = lambda shape: pl.BlockSpec(shape, lambda c, h, *_: (0,) * len(shape))
    rows = pl.BlockSpec((1, genes, width), lambda c, h, *_: (c, h, 0))
    columns = pl.BlockSpec((1, width, genes), lambda c, h, *_: (c, 0, h))
    own_rows = pl.BlockSpec((1, genes, width), lambda c, h, *_: (c, 0, 0))
    own_columns = pl.BlockSpec((1, width, genes), lambda c, h, *_: (c, 0, 0))
    per_cell = lambda shape: pl.BlockSpec((1,) + shape, lambda c, h, *_: (c,) + (0,) * len(shape))
    out = lambda shape, kind=BF16: jax.ShapeDtypeStruct(shape, kind)
    return pl.pallas_call(
        project_kernel,
        grid_spec=pltpu.PrefetchScalarGridSpec(
            num_scalar_prefetch=2,
            grid=(cells, 2),
            in_specs=[
                rows,
                per_cell((classes, width)),
                whole((1, width)),
                whole((1, width)),
                whole((width, 3 * width)),
            ],
            out_specs=[
                own_columns,
                own_rows,
                rows,
                rows,
                columns,
                pl.BlockSpec((1, HEADS, head + 16, genes), lambda c, h, *_: (c, 0, 0, h)),
                pl.BlockSpec((1, 1, 8, 128), lambda c, h, *_: (c, h, 0, 0)),
                per_cell((classes, 3 * width)),
            ],
            scratch_shapes=[
                pltpu.VMEM((3 * width, width), BF16),
                pltpu.VMEM((width, 128), F32),
                pltpu.VMEM((width, 128), F32),
            ],
        ),
        out_shape=[
            out((cells, width, genes)),
            out((cells, genes, width)),
            out((cells, total, width)),
            out((cells, total, width)),
            out((cells, width, total)),
            out((cells, HEADS, head + 16, total)),
            out((cells, 2, 8, 128), F32),
            out((cells, classes, 3 * width), F32),
        ],
        compiler_params=pltpu.CompilerParams(vmem_limit_bytes=VMEM),
        name="project",
    )(counts, place, x_all, xc, gain, bias, w)


def gelu_parts(u):
    root = 0.7071067811865476
    t = pl.reciprocal(1.0 + (0.3275911 * root) * jnp.abs(u), approx=True)
    bell = jnp.exp2((-0.5 * LOG2E) * (u * u))
    poly = t * (
        0.127414796
        + t * (-0.142248368 + t * (0.7107068705 + t * (-0.7265760135 + t * 0.5307027145)))
    )
    tail = poly * bell
    phi = jnp.where(u >= 0.0, 1.0 - tail, tail)
    return u * phi, phi + (u * 0.3989422804014327) * bell


def layer_kernel(
    counts,
    qt,
    qr,
    kr,
    vr,
    kt,
    va,
    stat,
    pc,
    x,
    xc,
    cot,
    cotc,
    w_out,
    gain,
    bias,
    w_up,
    b_up,
    w_down,
    b_down,
    y,
    yc,
    dq,
    dqc,
    dk,
    dv,
    dkvc,
    gm,
    gmc,
    g_up,
    g_down,
    g_out,
    g_vec,
    w_out_t,
    w_up_t,
    w_down_t,
    gain_c,
    bias_c,
    b_up_c,
    b_down_c,
    probs,
    probs_ck,
    probs_cq,
    mix,
    shift,
    shift_q,
    inv_sum,
    qz,
    qn,
    dz,
    dn,
    delta,
    att,
    datt,
    x_t,
    dq_t,
    up_acc,
    up_bias_acc,
    gain_acc,
    bias_acc,
    down_bias_acc,
):
    cell = pl.program_id(0)
    cells = pl.num_programs(0)
    genes, width = x.shape[1:]
    classes = xc.shape[1]
    head = width // HEADS
    ff = w_up.shape[1]
    stack = HEADS * classes
    factor = head**-0.5
    count = counts[cell]
    blocks = (count + (KB - 1)) // KB
    total_blocks = kr.shape[1] // KB

    @pl.when(cell == 0)
    def _():
        w_out_t[...] = w_out[...].T
        w_up_t[...] = w_up[...].T
        w_down_t[...] = w_down[...].T
        gain_c[...] = spread_column(gain[...])
        bias_c[...] = spread_column(bias[...])
        b_up_c[...] = spread_column(b_up[...])
        b_down_c[...] = spread_column(b_down[...])
        up_acc[...] = jnp.zeros_like(up_acc)
        up_bias_acc[...] = jnp.zeros_like(up_bias_acc)
        gain_acc[...] = jnp.zeros_like(gain_acc)
        bias_acc[...] = jnp.zeros_like(bias_acc)
        down_bias_acc[...] = jnp.zeros_like(down_bias_acc)
        g_down[...] = jnp.zeros_like(g_down)
        g_out[...] = jnp.zeros_like(g_out)

    head_mask = lax.broadcasted_iota(jnp.int32, (stack, width), 1) // head == (
        lax.broadcasted_iota(jnp.int32, (stack, width), 0) // classes
    )
    pair_mask = lax.broadcasted_iota(jnp.int32, (stack, stack), 1) // classes == (
        lax.broadcasted_iota(jnp.int32, (stack, stack), 0) // classes
    )

    def by_head(rows):
        return jnp.where(head_mask, jnp.concatenate([rows] * HEADS, 0), 0.0)

    def from_heads(rows):
        kept = jnp.where(head_mask, rows, 0.0)
        total = kept[:classes]
        for h in range(1, HEADS):
            total = total + kept[h * classes : (h + 1) * classes]
        return total

    packed_c = pc[0]
    query_c = by_head(packed_c[:, :width] * factor)
    key_c = by_head(packed_c[:, width : 2 * width])
    value_c = by_head(packed_c[:, 2 * width :])
    key_c_t = key_c.T.astype(BF16)
    value_c_t = value_c.T.astype(BF16)
    query_cb, key_cb, value_cb = query_c.astype(BF16), key_c.astype(BF16), value_c.astype(BF16)

    half_rows = lax.broadcasted_iota(jnp.int32, (2 * head, genes), 0) // head
    half_lanes = lax.broadcasted_iota(jnp.int32, (genes, 2 * head), 1) // head
    for h in range(HEADS):
        pair = slice((h // 2) * 2 * head, (h // 2 + 1) * 2 * head)
        qz[h] = jnp.where(half_rows == h % 2, qt[0, pair, :].astype(F32), 0.0).astype(BF16)
        qn[h] = jnp.where(half_lanes == h % 2, qr[0, :, pair].astype(F32), 0.0).astype(BF16)

    size_k = jnp.max(jnp.maximum(stat[0, 0, :HEADS], stat[0, 1, :HEADS]))
    size_q = jnp.max(jnp.maximum(stat[0, 0, HEADS:], stat[0, 1, HEADS:]))
    size_k = jnp.maximum(size_k, jnp.max(jnp.sum(key_c * key_c, -1, keepdims=True)))
    size_q = jnp.maximum(size_q, jnp.max(jnp.sum(query_c * query_c, -1, keepdims=True)))
    safe = size_k * size_q < SAFE * SAFE

    def key_mask(start, shape, axis):
        return start + lax.broadcasted_iota(jnp.int32, shape, axis) < count

    shift[...] = jnp.zeros_like(shift)
    shift_q[...] = jnp.zeros_like(shift_q)

    @pl.when(jnp.logical_not(safe))
    def _():
        class_scores = dot(key_cb, qt[0])
        for h in range(HEADS):
            shift[h] = jnp.max(class_scores[h * classes : (h + 1) * classes], 0, keepdims=True)
        own_scores = jnp.where(pair_mask, dot(query_cb, key_c_t), -1e30)
        shift_q[...] = jnp.broadcast_to(jnp.max(own_scores, -1, keepdims=True), shift_q.shape)

        @pl.loop(0, blocks)
        def _(block):
            start = pl.multiple_of(block * KB, KB)
            for h in range(HEADS):
                scores = dot(
                    kr[0, pl.ds(start, KB), (h // 2) * 2 * head : (h // 2 + 1) * 2 * head], qz[h]
                )
                scores = jnp.where(key_mask(start, scores.shape, 0), scores, -1e30)
                shift[h] = jnp.maximum(shift[h], jnp.max(scores, 0, keepdims=True))
            scores = dot(query_cb, kt[0, :, pl.ds(start, KB)])
            scores = jnp.where(key_mask(start, scores.shape, 1), scores, -1e30)
            shift_q[...] = jnp.maximum(shift_q[...], jnp.max(scores, -1, keepdims=True))

        shift[...] = shift[...] * LOG2E
        shift_q[...] = shift_q[...] * LOG2E

    class_scores = dot(key_cb, qt[0])
    shift_rows = jnp.concatenate(
        [jnp.broadcast_to(shift[h], (classes, genes)) for h in range(HEADS)], 0
    )
    class_exp = jnp.exp2(class_scores * LOG2E - shift_rows).astype(BF16)
    probs_ck[...] = class_exp
    class_mix = dot(value_c_t, class_exp)
    for h in range(HEADS):
        mix[h, :head, :] = class_mix[h * head : (h + 1) * head]
        sums = jnp.sum(
            class_exp[h * classes : (h + 1) * classes].astype(F32), 0, keepdims=True
        )
        mix[h, head:, :] = jnp.where(
            lax.broadcasted_iota(jnp.int32, (16, genes), 0) == 0, sums, 0.0
        )
    shift_qc = shift_q[:, :1]
    own_exp = jnp.where(
        pair_mask, jnp.exp2(dot(query_cb, key_c_t) * LOG2E - shift_qc), 0.0
    ).astype(BF16)
    own_mix = dot(own_exp, value_cb)
    own_sum = jnp.sum(own_exp.astype(F32), -1, keepdims=True)

    def forward_block(block, carried, shifted):
        class_total, class_sum = carried
        start = pl.multiple_of(block * KB, KB)
        keys = pl.ds(start, KB)
        scores = [
            dot(kr[0, keys, (h // 2) * 2 * head : (h // 2 + 1) * 2 * head], qz[h])
            for h in range(1)
        ]
        class_scores = dot(query_cb, kt[0, :, keys]) * LOG2E - shift_qc
        for h in range(HEADS):
            if h + 1 < HEADS:
                g = h + 1
                scores.append(
                    dot(kr[0, keys, (g // 2) * 2 * head : (g // 2 + 1) * 2 * head], qz[g])
                )
            scaled = scores[h] * LOG2E
            if shifted:
                scaled = jnp.minimum(scaled - shift[h], 60.0)
            exps = jnp.exp2(scaled).astype(BF16)
            probs[h, keys, :] = exps
            mix[h] += dot(va[0, h, :, keys], exps)
        class_exp = jnp.where(
            key_mask(start, class_scores.shape, 1), jnp.exp2(class_scores), 0.0
        ).astype(BF16)
        probs_cq[:, keys] = class_exp
        class_total = class_total + dot(class_exp, vr[0, keys, :])
        class_sum = class_sum + jnp.sum(class_exp.astype(F32), -1, keepdims=True)
        return class_total, class_sum

    carried = lax.cond(
        safe,
        lambda: lax.fori_loop(
            0, blocks, functools.partial(forward_block, shifted=False), (own_mix, own_sum)
        ),
        lambda: lax.fori_loop(
            0, blocks, functools.partial(forward_block, shifted=True), (own_mix, own_sum)
        ),
    )
    class_total, class_sum = carried
    class_inv = 1.0 / class_sum
    class_att = from_heads(class_total * class_inv)
    for h in range(HEADS):
        inverse = 1.0 / mix[h, head : head + 1, :]
        inv_sum[h] = inverse
        att[h * head : (h + 1) * head, :genes] = (mix[h, :head, :] * inverse).astype(BF16)

    def pad_rows(rows):
        return jnp.concatenate([rows, jnp.zeros((128 - rows.shape[0], width), F32)], 0)

    x_t[:, :genes] = x[0].T.astype(F32)
    x_t[:, genes:] = pad_rows(xc[0].astype(F32)).T
    att[:, genes:] = pad_rows(class_att).T.astype(BF16)

    def feed(start, columns, with_class):
        lanes = columns + (128 if with_class else 0)
        span = pl.ds(start, lanes)
        wide_gain, wide_bias = widen(gain_c[...], lanes), widen(bias_c[...], lanes)
        cot_r = cot[0, pl.ds(start, columns), :]
        cot_t = cot_r.T
        if with_class:
            padded = pad_rows(cotc[0].astype(F32))
            cot_t = jnp.concatenate([cot_t, padded.T.astype(BF16)], 1)
            cot_r = jnp.concatenate([cot_r, (padded * 0.5).astype(BF16)], 0)
            share = jnp.where(
                lax.broadcasted_iota(jnp.int32, (1, lanes), 1) < columns, 1.0, 0.5
            )
            weigh = lambda values: values * share
            row_share = jnp.where(
                lax.broadcasted_iota(jnp.int32, (lanes, 1), 0) < columns, 1.0, 0.5
            )
            weigh_rows = lambda rows: (rows.astype(F32) * row_share).astype(BF16)
        else:
            weigh = lambda values: values
            weigh_rows = lambda rows: rows
        att_low = att[:, span]
        middle = x_t[:, span] + dot(w_out_t[...], att_low)
        grad_act = dot(w_down[...], cot_t)
        unit, inverse = norm_columns(middle)
        low = (unit * wide_gain + wide_bias).astype(BF16)
        up = dot(w_up_t[...], low) + widen(b_up_c[...], lanes)
        active, slope = gelu_parts(up)
        active = active.astype(BF16)
        grad_up = slope * grad_act
        up_bias_acc[...] += fold_lanes(weigh(grad_up))
        grad_up = grad_up.astype(BF16)
        result = middle + dot(w_down_t[...], active) + widen(b_down_c[...], lanes)
        back = dot(w_up[...], grad_up)
        scaled = back * wide_gain
        scale = 1.0 / width
        grad_middle = cot_t.astype(F32) + inverse * (
            scaled
            - jnp.sum(scaled, 0, keepdims=True) * scale
            - unit * (jnp.sum(scaled * unit, 0, keepdims=True) * scale)
        )
        grad_middle = grad_middle.astype(BF16)
        datt[:, span] = dot(w_out[...], grad_middle).astype(BF16)
        gain_acc[...] += fold_lanes(weigh(back * unit))
        bias_acc[...] += fold_lanes(weigh(back))
        middle_r = grad_middle.T
        g_down[...] += dot(active, cot_r)
        up_acc[...] += dot(grad_up, weigh_rows(low.T))
        g_out[...] += dot(att_low, weigh_rows(middle_r))
        cot_sum = jnp.sum(cot_r.astype(F32), 0, keepdims=True)
        down_bias_acc[...] += cot_sum
        result_r = result.T
        y[0, pl.ds(start, columns), :] = result_r[:columns].astype(BF16)
        gm[0, pl.ds(start, columns), :] = middle_r[:columns]
        if with_class:
            yc[0] = result_r[columns : columns + classes].astype(BF16)
            gmc[0] = middle_r[columns:].astype(F32)[:classes]

    feed_step = 256
    pieces = genes // feed_step

    @pl.loop(0, pieces - 1)
    def _(piece):
        feed(pl.multiple_of(piece * feed_step, feed_step), feed_step, False)

    feed((pieces - 1) * feed_step, feed_step, True)

    for h in range(HEADS):
        own = slice(h * head, (h + 1) * head)
        inverse = inv_sum[h]
        grad = (datt[own, :genes].astype(F32) * inverse).astype(BF16)
        delta[h] = jnp.sum(grad.astype(F32) * (mix[h, :head, :] * inverse), 0, keepdims=True)
        datt[own, :genes] = grad
        blank = jnp.zeros_like(grad)
        dz[h] = jnp.concatenate([grad, blank] if h % 2 == 0 else [blank, grad], 0)
    grad_r = datt[:, :genes].T
    for h in range(HEADS):
        pair = slice((h // 2) * 2 * head, (h // 2 + 1) * 2 * head)
        dn[h] = jnp.where(half_lanes == h % 2, grad_r[:, pair].astype(F32), 0.0).astype(BF16)

    class_grad = datt[:, genes:].astype(F32).T[:classes]
    class_grad = by_head(class_grad) * class_inv
    class_grad_b = class_grad.astype(BF16)
    class_grad_h = (class_grad * 0.5).astype(BF16)
    query_ch = (query_c * 0.5).astype(BF16)
    class_delta = jnp.sum(
        class_grad_b.astype(F32) * (class_total * class_inv), -1, keepdims=True
    )

    class_dprob = dot(value_cb, datt[:, :genes])
    delta_rows = jnp.concatenate(
        [jnp.broadcast_to(delta[h], (classes, genes)) for h in range(HEADS)], 0
    )
    class_probs = probs_ck[...]
    class_dscore = (class_probs.astype(F32) * (class_dprob - delta_rows)).astype(BF16)
    dq_t[...] = dot(key_c_t, class_dscore)
    class_dkey = dot(class_dscore, qr[0])
    class_dvalue = dot(class_probs, grad_r)
    own_dprob = dot(class_grad_b, value_c_t)
    own_dscore = (own_exp.astype(F32) * (own_dprob - class_delta)).astype(BF16)
    class_dquery = dot(own_dscore, key_cb)
    class_dkey = class_dkey + dot(own_dscore.astype(F32).T.astype(BF16), query_ch)
    class_dvalue = class_dvalue + dot(own_exp.astype(F32).T.astype(BF16), class_grad_h)

    def backward_block(block, class_dquery):
        start = pl.multiple_of(block * KB, KB)
        keys = pl.ds(start, KB)
        class_weights = probs_cq[:, keys]
        class_dprob = dot_nt(class_grad_b, vr[0, keys, :])
        dprobs = [dot(vr[0, keys, : 2 * head], dz[0])]
        class_dscore = (class_weights.astype(F32) * (class_dprob - class_delta)).astype(BF16)
        dkey = dot_tn(class_dscore, query_ch)
        dvalue = dot_tn(class_weights, class_grad_h)
        dkeys = [dkey[:, : 2 * head], dkey[:, 2 * head :]]
        dvalues = [dvalue[:, : 2 * head], dvalue[:, 2 * head :]]
        for h in range(HEADS):
            if h + 1 < HEADS:
                g = h + 1
                dprobs.append(
                    dot(vr[0, keys, (g // 2) * 2 * head : (g // 2 + 1) * 2 * head], dz[g])
                )
            weights = probs[h, keys, :]
            dscore = weights * (dprobs[h] - delta[h]).astype(BF16)
            own = slice(h * head, (h + 1) * head)
            dq_t[own, :] += dot(kt[0, own, keys], dscore)
            dkeys[h // 2] = dkeys[h // 2] + dot(dscore, qn[h])
            dvalues[h // 2] = dvalues[h // 2] + dot(weights, dn[h])
        valid = key_mask(start, (KB, width), 0)
        dk[0, keys, :] = jnp.where(valid, jnp.concatenate(dkeys, 1), 0.0).astype(BF16)
        dv[0, keys, :] = jnp.where(valid, jnp.concatenate(dvalues, 1), 0.0).astype(BF16)
        return class_dquery + dot(class_dscore, kr[0, keys, :])

    class_dquery = lax.fori_loop(0, blocks, backward_block, class_dquery)

    @pl.loop(blocks, total_blocks)
    def _(block):
        keys = pl.ds(pl.multiple_of(block * KB, KB), KB)
        dk[0, keys, :] = jnp.zeros((KB, width), BF16)
        dv[0, keys, :] = jnp.zeros((KB, width), BF16)

    dq[0] = (dq_t[...] * factor).astype(BF16).T
    dqc[0] = from_heads(class_dquery) * factor
    dkvc[0] = jnp.concatenate([from_heads(class_dkey), from_heads(class_dvalue)], 1)

    @pl.when(cell == cells - 1)
    def _():
        g_up[...] = up_acc[...].T
        g_vec[...] = jnp.zeros_like(g_vec)
        g_vec[0:1, :] = jnp.sum(up_bias_acc[...].T, 0, keepdims=True)
        g_vec[1:2, :width] = jnp.sum(gain_acc[...].T, 0, keepdims=True)
        g_vec[1:2, width : 2 * width] = jnp.sum(bias_acc[...].T, 0, keepdims=True)
        g_vec[1:2, 2 * width : 3 * width] = down_bias_acc[...]


def layer(
    counts, tables, x, xc, cot, cotc, w_out, gain, bias, w_up, b_up, w_down, b_down
):
    cells, genes, width = x.shape
    classes = xc.shape[1]
    total = tables[2].shape[1]
    head = width // HEADS
    ff = w_up.shape[1]
    stack = HEADS * classes
    whole = lambda shape: pl.BlockSpec(
        shape, lambda c, *_: (0,) * len(shape), pipeline_mode=pl.Buffered(1)
    )
    per_cell = lambda *shape: pl.BlockSpec((1,) + shape, lambda c, *_: (c,) + (0,) * len(shape))
    kept = lambda *shape: pl.BlockSpec(shape, lambda c, *_: (0,) * len(shape))
    out = lambda shape, kind=BF16: jax.ShapeDtypeStruct(shape, kind)
    vmem = lambda *shape, kind=BF16: pltpu.VMEM(shape, kind)
    f32 = functools.partial(vmem, kind=F32)
    return pl.pallas_call(
        layer_kernel,
        grid_spec=pltpu.PrefetchScalarGridSpec(
            num_scalar_prefetch=1,
            grid=(cells,),
            in_specs=[
                per_cell(width, genes),
                per_cell(genes, width),
                per_cell(total, width),
                per_cell(total, width),
                per_cell(width, total),
                per_cell(HEADS, head + 16, total),
                per_cell(2, 8, 128),
                per_cell(classes, 3 * width),
                per_cell(genes, width),
                per_cell(classes, width),
                per_cell(genes, width),
                per_cell(classes, width),
                whole((width, width)),
                whole((1, width)),
                whole((1, width)),
                whole((width, ff)),
                whole((1, ff)),
                whole((ff, width)),
                whole((1, width)),
            ],
            out_specs=[
                per_cell(genes, width),
                per_cell(classes, width),
                per_cell(genes, width),
                per_cell(classes, width),
                per_cell(total, width),
                per_cell(total, width),
                per_cell(classes, 2 * width),
                per_cell(genes, width),
                per_cell(classes, width),
                kept(width, ff),
                kept(ff, width),
                kept(width, width),
                kept(8, ff),
            ],
            scratch_shapes=[
                vmem(width, width),
                vmem(ff, width),
                vmem(width, ff),
                f32(width, 128),
                f32(width, 128),
                f32(ff, 128),
                f32(width, 128),
                vmem(HEADS, total, genes),
                vmem(stack, genes),
                vmem(stack, total),
                f32(HEADS, head + 16, genes),
                f32(HEADS, 1, genes),
                f32(stack, 128),
                f32(HEADS, 1, genes),
                vmem(HEADS, 2 * head, genes),
                vmem(HEADS, genes, 2 * head),
                vmem(HEADS, 2 * head, genes),
                vmem(HEADS, genes, 2 * head),
                f32(HEADS, 1, genes),
                vmem(width, genes + 128),
                vmem(width, genes + 128),
                f32(width, genes + 128),
                f32(width, genes),
                f32(ff, width),
                f32(ff, 128),
                f32(width, 128),
                f32(width, 128),
                f32(1, width),
            ],
        ),
        out_shape=[
            out((cells, genes, width)),
            out((cells, classes, width)),
            out((cells, genes, width)),
            out((cells, classes, width), F32),
            out((cells, total, width)),
            out((cells, total, width)),
            out((cells, classes, 2 * width), F32),
            out((cells, genes, width)),
            out((cells, classes, width), F32),
            out((width, ff), F32),
            out((ff, width), F32),
            out((width, width), F32),
            out((8, ff), F32),
        ],
        compiler_params=pltpu.CompilerParams(vmem_limit_bytes=VMEM),
        name="layer",
    )(counts, *tables, x, xc, cot, cotc, w_out, gain, bias, w_up, b_up, w_down, b_down)


def tokens_kernel(
    x, xc, gm, gmc, dq, dqc, dk, dv, dkvc, gain, bias, w, g_x, g_xc, g_qkv, g_vec, w_t
):
    cell = pl.program_id(0)
    genes, width = x.shape[1:]
    classes = xc.shape[1]

    @pl.when(cell == 0)
    def _():
        w_t[...] = w[...].T
        g_qkv[...] = jnp.zeros_like(g_qkv)
        g_vec[...] = jnp.zeros_like(g_vec)

    blank = jnp.zeros((16 - classes, width), F32)

    def joined(genes_part, class_part):
        return jnp.concatenate([genes_part.astype(F32), class_part.astype(F32), blank], 0)

    unit, inverse = norm_rows(joined(x[0], xc[0]))
    low = (unit * gain[...] + bias[...]).astype(BF16)
    rows = genes + 16
    spot = lax.broadcasted_iota(jnp.int32, (rows, 1), 0)
    share = jnp.where(spot < genes, 1.0, jnp.where(spot < genes + classes, 0.5, 0.0))
    class_grads = [dqc[0], dkvc[0][:, :width], dkvc[0][:, width:]]
    packed = jnp.concatenate(
        [
            jnp.concatenate([part, jnp.concatenate([class_part, blank], 0).astype(BF16)], 0)
            for part, class_part in zip((dq[0], dk[0], dv[0]), class_grads)
        ],
        1,
    )
    back = dot(packed, w_t[...])
    g_qkv[...] += dot_tn((low.astype(F32) * share).astype(BF16), packed)
    weighed = back * share
    g_vec[0:1, :] += jnp.sum(weighed * unit, 0, keepdims=True)
    g_vec[1:2, :] += jnp.sum(weighed, 0, keepdims=True)
    scaled = back * gain[...]
    result = joined(gm[0], gmc[0]) + inverse * (
        scaled
        - jnp.mean(scaled, -1, keepdims=True)
        - unit * jnp.mean(scaled * unit, -1, keepdims=True)
    )
    g_x[0] = result[:genes].astype(BF16)
    g_xc[0] = result[genes : genes + classes].astype(BF16)


def tokens(x, xc, gm, gmc, dq, dqc, dk, dv, dkvc, gain, bias, w):
    cells, genes, width = x.shape
    classes = xc.shape[1]
    whole = lambda shape: pl.BlockSpec(shape, lambda c: (0,) * len(shape))
    per_cell = lambda *shape: pl.BlockSpec((1,) + shape, lambda c: (c,) + (0,) * len(shape))
    out = lambda shape, kind=BF16: jax.ShapeDtypeStruct(shape, kind)
    return pl.pallas_call(
        tokens_kernel,
        grid=(cells,),
        in_specs=[
            per_cell(genes, width),
            per_cell(classes, width),
            per_cell(genes, width),
            per_cell(classes, width),
            per_cell(genes, width),
            per_cell(classes, width),
            per_cell(genes, width),
            per_cell(genes, width),
            per_cell(classes, 2 * width),
            whole((1, width)),
            whole((1, width)),
            whole((width, 3 * width)),
        ],
        out_specs=[
            per_cell(genes, width),
            per_cell(classes, width),
            whole((width, 3 * width)),
            whole((8, width)),
        ],
        out_shape=[
            out((cells, genes, width)),
            out((cells, classes, width)),
            out((width, 3 * width), F32),
            out((8, width), F32),
        ],
        scratch_shapes=[pltpu.VMEM((3 * width, width), BF16)],
        compiler_params=pltpu.CompilerParams(vmem_limit_bytes=VMEM),
        name="tokens",
    )(x, xc, gm, gmc, dq, dqc, dk, dv, dkvc, gain, bias, w)


def shards(
    gene_in,
    class_in,
    expressed,
    ln1_gain,
    ln1_bias,
    w_qkv,
    w_out,
    ln2_gain,
    ln2_bias,
    w_up,
    b_up,
    w_down,
    b_down,
    gene_cot,
    class_cot,
):
    width = gene_in.shape[-1]
    row = lambda vector: vector.reshape(1, -1)
    place = lax.axis_index("gene").reshape(1)
    everything = lax.all_gather(gene_in, "gene", axis=1, tiled=True)
    tables = project(
        expressed, place, everything, class_in, row(ln1_gain), row(ln1_bias), w_qkv
    )
    gene_out, class_out, dq, dqc, dk, dv, dkvc, gm, gmc, g_up, g_down, g_out, g_vec = layer(
        expressed,
        tables,
        gene_in,
        class_in,
        gene_cot,
        class_cot,
        w_out,
        row(ln2_gain),
        row(ln2_bias),
        w_up,
        row(b_up),
        w_down,
        row(b_down),
    )
    dk = lax.psum_scatter(dk, "gene", scatter_dimension=1, tiled=True)
    dv = lax.psum_scatter(dv, "gene", scatter_dimension=1, tiled=True)
    dkvc = lax.psum(dkvc, "gene")
    gene_grad, class_grad, g_qkv, g_vec1 = tokens(
        gene_in,
        class_in,
        gm,
        gmc,
        dq,
        dqc,
        dk,
        dv,
        dkvc,
        row(ln1_gain),
        row(ln1_bias),
        w_qkv,
    )
    g_up, g_down, g_out, g_vec, g_qkv, g_vec1 = lax.psum(
        (g_up, g_down, g_out, g_vec, g_qkv, g_vec1), ("cell", "gene")
    )
    return (
        gene_out,
        class_out,
        gene_grad,
        class_grad,
        g_vec1[0],
        g_vec1[1],
        g_qkv,
        g_out,
        g_vec[1, :width],
        g_vec[1, width : 2 * width],
        g_up,
        g_vec[0],
        g_down,
        g_vec[1, 2 * width : 3 * width],
    )


def solution(mesh):
    genes, cells, whole = P("cell", "gene", None), P("cell", None, None), P()
    return jax.shard_map(
        shards,
        mesh=mesh,
        in_specs=(genes, cells, P("cell")) + (whole,) * 10 + (genes, cells),
        out_specs=(genes, cells, genes, cells) + (whole,) * 10,
        check_vma=False,
    )
```

```python
import functools

import jax
import jax.numpy as jnp
from jax import lax
from jax.experimental import pallas as pl
from jax.experimental.pallas import tpu as pltpu
from jax.sharding import PartitionSpec as P

HEADS = 4
EPS = 1e-05
LOG2E = 1.4426950408889634
SAFE = 40.0
KB = 256
STREAMS = 3
VECTOR_ROWS = 32
VMEM = 63 * 2**20
F32 = jnp.float32
BF16 = jnp.bfloat16
MESH = pl.DeviceIdType.MESH


def dot(left, right):
    return jnp.dot(left, right, preferred_element_type=F32)


def dot_nt(left, right):
    return lax.dot_general(left, right, (((1,), (1,)), ((), ())), preferred_element_type=F32)


def dot_tn(left, right):
    return lax.dot_general(left, right, (((0,), (0,)), ((), ())), preferred_element_type=F32)


def spread_column(row):
    return jnp.broadcast_to(row, (128, row.shape[1])).T


def widen(column, lanes):
    return jnp.concatenate([column] * (lanes // 128), axis=1)


def fold_lanes(values):
    total = values[:, :128]
    for start in range(128, values.shape[1], 128):
        total = total + values[:, start : start + 128]
    return total


def norm_rows(values):
    centered = values - jnp.mean(values, -1, keepdims=True)
    inverse = lax.rsqrt(jnp.mean(centered * centered, -1, keepdims=True) + EPS)
    return centered * inverse, inverse


def norm_columns(values):
    scale = 1.0 / values.shape[0]
    centered = values - jnp.sum(values, 0, keepdims=True) * scale
    inverse = lax.rsqrt(jnp.sum(centered * centered, 0, keepdims=True) * scale + EPS)
    return centered * inverse, inverse


def flip(index, stride):
    return index + stride * (1 - 2 * ((index // stride) % 2))


def greet(partners):
    barrier = pltpu.get_barrier_semaphore()
    for partner in partners:
        pl.semaphore_signal(barrier, inc=1, device_id=partner, device_id_type=MESH)
    pl.semaphore_wait(barrier, len(partners))


def project_kernel(
    counts,
    x,
    x_hbm,
    xc,
    gain,
    bias,
    w,
    qt,
    kr,
    vr,
    kt,
    va,
    ut,
    stat,
    pc,
    w_t,
    gain_c,
    bias_c,
    other,
    sent,
    received,
):
    cell, half = pl.program_id(0), pl.program_id(1)
    cells = x_hbm.shape[0]
    genes, width = x.shape[1:]
    head = width // HEADS
    place = lax.axis_index("gene")
    partner = {"cell": lax.axis_index("cell"), "gene": 1 - place}

    def swap(index):
        return pltpu.make_async_remote_copy(
            src_ref=x_hbm.at[index],
            dst_ref=other.at[index],
            send_sem=sent.at[index],
            recv_sem=received.at[index],
            device_id=partner,
            device_id_type=MESH,
        )

    @pl.when((cell == 0) & (half == 0))
    def _():
        greet([partner])
        for index in range(cells):
            swap(index).start()
        w_t[...] = w[...].T
        gain_c[...] = spread_column(gain[...])
        bias_c[...] = spread_column(bias[...])

    def norms(columns, first):
        for h in range(HEADS):
            part = columns[h * head : (h + 1) * head]
            size = jnp.sum(part * part, 0, keepdims=True)
            best = size[:, :128]
            for start in range(128, genes, 128):
                best = jnp.maximum(best, size[:, start : start + 128])
            stat[0, 0, first + h : first + h + 1, :] = best

    def tables(values, origin):
        unit, _ = norm_columns(values.T.astype(F32))
        ut[0] = unit.astype(BF16)
        low = unit * widen(gain_c[...], genes) + widen(bias_c[...], genes)
        spot = origin + lax.broadcasted_iota(jnp.int32, (1, genes), 1)
        valid = spot < counts[cell]
        kept = jnp.where(valid, low, 0.0).astype(BF16)
        packed_t = dot(w_t[width:, :], kept)
        packed = dot(kept.T, w[:, width:])
        kt[0] = packed_t[:width].astype(BF16)
        mark = jnp.where(
            (lax.broadcasted_iota(jnp.int32, (16, genes), 0) == 0) & valid, 1.0, 0.0
        ).astype(BF16)
        for h in range(HEADS):
            va[0, h, :head, :] = packed_t[width + h * head : width + (h + 1) * head].astype(BF16)
            va[0, h, head:, :] = mark
        kr[0] = packed[:, :width].astype(BF16)
        vr[0] = packed[:, width:].astype(BF16)
        stat[...] = jnp.zeros_like(stat)
        norms(packed_t[:width], 0)
        return low

    @pl.when(half == 0)
    def _():
        low = tables(x[0], place * genes)
        query_t = dot(w_t[:width, :], low.astype(BF16)).astype(BF16) * (head**-0.5)
        qt[0] = query_t
        norms(query_t.astype(F32), HEADS)
        unit, _ = norm_rows(xc[0].astype(F32))
        class_low = (unit * gain[...] + bias[...]).astype(BF16)
        pc[0] = dot(class_low, w[...]).astype(BF16).astype(F32)

    @pl.when(half == 1)
    def _():
        swap(cell).wait_recv()
        tables(other[cell], (1 - place) * genes)

    @pl.when((cell == cells - 1) & (half == 1))
    def _():
        for index in range(cells):
            swap(index).wait_send()


def project(counts, x, xc, gain, bias, w):
    cells, genes, width = x.shape
    total = 2 * genes
    classes = xc.shape[1]
    head = width // HEADS
    whole = lambda shape: pl.BlockSpec(shape, lambda c, h: (0,) * len(shape))
    rows = pl.BlockSpec((1, genes, width), lambda c, h: (c, h, 0))
    columns = pl.BlockSpec((1, width, genes), lambda c, h: (c, 0, h))
    per_cell = lambda *shape: pl.BlockSpec((1,) + shape, lambda c, h: (c,) + (0,) * len(shape))
    out = lambda shape, kind=BF16: jax.ShapeDtypeStruct(shape, kind)
    return pl.pallas_call(
        project_kernel,
        grid=(cells, 2),
        in_specs=[
            pl.BlockSpec(memory_space=pltpu.SMEM),
            per_cell(genes, width),
            pl.BlockSpec(memory_space=pl.ANY),
            per_cell(classes, width),
            whole((1, width)),
            whole((1, width)),
            whole((width, 3 * width)),
        ],
        out_specs=[
            per_cell(width, genes),
            rows,
            rows,
            columns,
            pl.BlockSpec((1, HEADS, head + 16, genes), lambda c, h: (c, 0, 0, h)),
            columns,
            pl.BlockSpec((1, 1, 8, 128), lambda c, h: (c, h, 0, 0)),
            per_cell(classes, 3 * width),
        ],
        out_shape=[
            out((cells, width, genes)),
            out((cells, total, width)),
            out((cells, total, width)),
            out((cells, width, total)),
            out((cells, HEADS, head + 16, total)),
            out((cells, width, total)),
            out((cells, 2, 8, 128), F32),
            out((cells, classes, 3 * width), F32),
        ],
        scratch_shapes=[
            pltpu.VMEM((3 * width, width), BF16),
            pltpu.VMEM((width, 128), F32),
            pltpu.VMEM((width, 128), F32),
            pltpu.VMEM((cells, genes, width), BF16),
            pltpu.SemaphoreType.DMA((cells,)),
            pltpu.SemaphoreType.DMA((cells,)),
        ],
        compiler_params=pltpu.CompilerParams(
            vmem_limit_bytes=VMEM, collective_id=0, has_side_effects=True
        ),
        name="project",
    )(counts, x, x, xc, gain, bias, w)


def gelu_parts(u):
    root = 0.7071067811865476
    t = pl.reciprocal(1.0 + (0.3275911 * root) * jnp.abs(u), approx=True)
    bell = jnp.exp2((-0.5 * LOG2E) * (u * u))
    poly = t * (
        0.127414796
        + t * (-0.142248368 + t * (0.7107068705 + t * (-0.7265760135 + t * 0.5307027145)))
    )
    tail = poly * bell
    phi = jnp.where(u >= 0.0, 1.0 - tail, tail)
    return u * phi, phi + (u * 0.3989422804014327) * bell


def layer_kernel(
    counts,
    place,
    qt,
    kr,
    vr,
    kt,
    va,
    ut,
    stat,
    pc,
    x,
    xc,
    cot,
    cotc,
    w_out,
    gain,
    bias,
    w_up,
    b_up,
    w_down,
    b_down,
    y,
    yc,
    dq,
    dqc,
    dkv,
    dkvc,
    gm,
    gmc,
    slab,
    g_vec,
    w_out_t,
    w_up_t,
    w_down_t,
    gain_c,
    bias_c,
    b_up_c,
    b_down_c,
    probs,
    probs_ck,
    probs_cq,
    mix,
    shift,
    shift_q,
    inv_sum,
    qz,
    qn,
    dn,
    delta,
    att,
    datt,
    x_t,
    dq_t,
    up_acc,
    g_down,
    g_out,
    qkv_acc,
    up_bias_acc,
    gain_acc,
    bias_acc,
    down_bias_acc,
    packed_sum,
):
    cell = pl.program_id(0)
    cells = pl.num_programs(0)
    genes, width = x.shape[1:]
    classes = xc.shape[1]
    head = width // HEADS
    ff = w_up.shape[1]
    stack = HEADS * classes
    factor = head**-0.5
    count = counts[cell]
    own_count = jnp.clip(count - place[0] * genes, 0, genes)
    other_count = jnp.clip(count - (1 - place[0]) * genes, 0, genes)
    own_blocks = (own_count + (KB - 1)) // KB
    other_blocks = (other_count + (KB - 1)) // KB
    half_blocks = genes // KB
    blocks = own_blocks + other_blocks

    def nth_block(index):
        block = jnp.where(index < own_blocks, index, index - own_blocks + half_blocks)
        return pl.multiple_of(block * KB, KB)

    @pl.when(cell == 0)
    def _():
        w_out_t[...] = w_out[...].T
        w_up_t[...] = w_up[...].T
        w_down_t[...] = w_down[...].T
        gain_c[...] = spread_column(gain[...])
        bias_c[...] = spread_column(bias[...])
        b_up_c[...] = spread_column(b_up[...])
        b_down_c[...] = spread_column(b_down[...])
        up_acc[...] = jnp.zeros_like(up_acc)
        up_bias_acc[...] = jnp.zeros_like(up_bias_acc)
        gain_acc[...] = jnp.zeros_like(gain_acc)
        bias_acc[...] = jnp.zeros_like(bias_acc)
        down_bias_acc[...] = jnp.zeros_like(down_bias_acc)
        g_down[...] = jnp.zeros_like(g_down)
        g_out[...] = jnp.zeros_like(g_out)
        qkv_acc[...] = jnp.zeros_like(qkv_acc)
        packed_sum[...] = jnp.zeros_like(packed_sum)

    head_mask = lax.broadcasted_iota(jnp.int32, (stack, width), 1) // head == (
        lax.broadcasted_iota(jnp.int32, (stack, width), 0) // classes
    )
    pair_mask = lax.broadcasted_iota(jnp.int32, (stack, stack), 1) // classes == (
        lax.broadcasted_iota(jnp.int32, (stack, stack), 0) // classes
    )

    def by_head(rows):
        return jnp.where(head_mask, jnp.concatenate([rows] * HEADS, 0), 0.0)

    def from_heads(rows):
        kept = jnp.where(head_mask, rows, 0.0)
        total = kept[:classes]
        for h in range(1, HEADS):
            total = total + kept[h * classes : (h + 1) * classes]
        return total

    packed_c = pc[0]
    query_c = by_head(packed_c[:, :width] * factor)
    key_c = by_head(packed_c[:, width : 2 * width])
    value_c = by_head(packed_c[:, 2 * width :])
    key_c_t = key_c.T.astype(BF16)
    value_c_t = value_c.T.astype(BF16)
    query_cb, key_cb, value_cb = query_c.astype(BF16), key_c.astype(BF16), value_c.astype(BF16)

    half_rows = lax.broadcasted_iota(jnp.int32, (2 * head, genes), 0) // head
    half_lanes = lax.broadcasted_iota(jnp.int32, (genes, 2 * head), 1) // head
    query_r = qt[0].T
    for h in range(HEADS):
        pair = slice((h // 2) * 2 * head, (h // 2 + 1) * 2 * head)
        qz[h] = jnp.where(half_rows == h % 2, qt[0, pair, :].astype(F32), 0.0).astype(BF16)
        qn[h] = jnp.where(half_lanes == h % 2, query_r[:, pair].astype(F32), 0.0).astype(BF16)

    size_k = jnp.max(jnp.maximum(stat[0, 0, :HEADS], stat[0, 1, :HEADS]))
    size_q = jnp.max(jnp.maximum(stat[0, 0, HEADS:], stat[0, 1, HEADS:]))
    size_k = jnp.maximum(size_k, jnp.max(jnp.sum(key_c * key_c, -1, keepdims=True)))
    size_q = jnp.maximum(size_q, jnp.max(jnp.sum(query_c * query_c, -1, keepdims=True)))
    safe = size_k * size_q < SAFE * SAFE

    def key_mask(start, shape, axis):
        limit = jnp.where(start < genes, own_count, genes + other_count)
        return start + lax.broadcasted_iota(jnp.int32, shape, axis) < limit

    shift[...] = jnp.zeros_like(shift)
    shift_q[...] = jnp.zeros_like(shift_q)

    @pl.when(jnp.logical_not(safe))
    def _():
        class_scores = dot(key_cb, qt[0])
        for h in range(HEADS):
            shift[h] = jnp.max(class_scores[h * classes : (h + 1) * classes], 0, keepdims=True)
        own_scores = jnp.where(pair_mask, dot(query_cb, key_c_t), -1e30)
        shift_q[...] = jnp.broadcast_to(jnp.max(own_scores, -1, keepdims=True), shift_q.shape)

        @pl.loop(0, blocks)
        def _(block):
            start = nth_block(block)
            for h in range(HEADS):
                scores = dot(
                    kr[0, pl.ds(start, KB), (h // 2) * 2 * head : (h // 2 + 1) * 2 * head], qz[h]
                )
                scores = jnp.where(key_mask(start, scores.shape, 0), scores, -1e30)
                shift[h] = jnp.maximum(shift[h], jnp.max(scores, 0, keepdims=True))
            scores = dot(query_cb, kt[0, :, pl.ds(start, KB)])
            scores = jnp.where(key_mask(start, scores.shape, 1), scores, -1e30)
            shift_q[...] = jnp.maximum(shift_q[...], jnp.max(scores, -1, keepdims=True))

        shift[...] = shift[...] * LOG2E
        shift_q[...] = shift_q[...] * LOG2E

    class_scores = dot(key_cb, qt[0])
    shift_rows = jnp.concatenate(
        [jnp.broadcast_to(shift[h], (classes, genes)) for h in range(HEADS)], 0
    )
    class_exp = jnp.exp2(class_scores * LOG2E - shift_rows).astype(BF16)
    probs_ck[...] = class_exp
    class_mix = dot(value_c_t, class_exp)
    for h in range(HEADS):
        mix[h, :head, :] = class_mix[h * head : (h + 1) * head]
        sums = jnp.sum(
            class_exp[h * classes : (h + 1) * classes].astype(F32), 0, keepdims=True
        )
        mix[h, head:, :] = jnp.where(
            lax.broadcasted_iota(jnp.int32, (16, genes), 0) == 0, sums, 0.0
        )
    shift_qc = shift_q[:, :1]
    own_exp = jnp.where(
        pair_mask, jnp.exp2(dot(query_cb, key_c_t) * LOG2E - shift_qc), 0.0
    ).astype(BF16)
    own_mix = dot(own_exp, value_cb)
    own_sum = jnp.sum(own_exp.astype(F32), -1, keepdims=True)

    def forward_block(block, carried, shifted):
        class_total, class_sum = carried
        start = nth_block(block)
        keys = pl.ds(start, KB)
        scores = [
            dot(kr[0, keys, (h // 2) * 2 * head : (h // 2 + 1) * 2 * head], qz[h])
            for h in range(1)
        ]
        class_scores = dot(query_cb, kt[0, :, keys]) * LOG2E - shift_qc
        for h in range(HEADS):
            if h + 1 < HEADS:
                g = h + 1
                scores.append(
                    dot(kr[0, keys, (g // 2) * 2 * head : (g // 2 + 1) * 2 * head], qz[g])
                )
            scaled = scores[h] * LOG2E
            if shifted:
                scaled = jnp.minimum(scaled - shift[h], 60.0)
            exps = jnp.exp2(scaled).astype(BF16)
            probs[h, keys, :] = exps
            mix[h] += dot(va[0, h, :, keys], exps)
        class_exp = jnp.where(
            key_mask(start, class_scores.shape, 1), jnp.exp2(class_scores), 0.0
        ).astype(BF16)
        probs_cq[:, keys] = class_exp
        class_total = class_total + dot(class_exp, vr[0, keys, :])
        class_sum = class_sum + jnp.sum(class_exp.astype(F32), -1, keepdims=True)
        return class_total, class_sum

    carried = lax.cond(
        safe,
        lambda: lax.fori_loop(
            0, blocks, functools.partial(forward_block, shifted=False), (own_mix, own_sum)
        ),
        lambda: lax.fori_loop(
            0, blocks, functools.partial(forward_block, shifted=True), (own_mix, own_sum)
        ),
    )
    class_total, class_sum = carried
    class_inv = 1.0 / class_sum
    class_att = from_heads(class_total * class_inv)
    for h in range(HEADS):
        inverse = 1.0 / mix[h, head : head + 1, :]
        inv_sum[h] = inverse
        att[h * head : (h + 1) * head, :genes] = (mix[h, :head, :] * inverse).astype(BF16)

    def pad_rows(rows):
        return jnp.concatenate([rows, jnp.zeros((128 - rows.shape[0], width), F32)], 0)

    x_t[:, :genes] = x[0].T
    x_t[:, genes:] = pad_rows(xc[0].astype(F32)).T.astype(BF16)
    att[:, genes:] = pad_rows(class_att).T.astype(BF16)

    def feed(start, columns, with_class):
        lanes = columns + (128 if with_class else 0)
        span = pl.ds(start, lanes)
        wide_gain, wide_bias = widen(gain_c[...], lanes), widen(bias_c[...], lanes)
        cot_r = cot[0, pl.ds(start, columns), :]
        cot_t = cot_r.T
        if with_class:
            padded = pad_rows(cotc[0].astype(F32))
            cot_t = jnp.concatenate([cot_t, padded.T.astype(BF16)], 1)
            cot_r = jnp.concatenate([cot_r, (padded * 0.5).astype(BF16)], 0)
            share = jnp.where(
                lax.broadcasted_iota(jnp.int32, (1, lanes), 1) < columns, 1.0, 0.5
            )
            weigh = lambda values: values * share
            row_share = jnp.where(
                lax.broadcasted_iota(jnp.int32, (lanes, 1), 0) < columns, 1.0, 0.5
            )
            weigh_rows = lambda rows: (rows.astype(F32) * row_share).astype(BF16)
        else:
            weigh = lambda values: values
            weigh_rows = lambda rows: rows
        att_low = att[:, span]
        middle = x_t[:, span].astype(F32) + dot(w_out_t[...], att_low)
        grad_act = dot(w_down[...], cot_t)
        unit, inverse = norm_columns(middle)
        low = (unit * wide_gain + wide_bias).astype(BF16)
        up = dot(w_up_t[...], low) + widen(b_up_c[...], lanes)
        active, slope = gelu_parts(up)
        active = active.astype(BF16)
        grad_up = slope * grad_act
        up_bias_acc[...] += fold_lanes(weigh(grad_up))
        grad_up = grad_up.astype(BF16)
        result = middle + dot(w_down_t[...], active) + widen(b_down_c[...], lanes)
        back = dot(w_up[...], grad_up)
        scaled = back * wide_gain
        scale = 1.0 / width
        grad_middle = cot_t.astype(F32) + inverse * (
            scaled
            - jnp.sum(scaled, 0, keepdims=True) * scale
            - unit * (jnp.sum(scaled * unit, 0, keepdims=True) * scale)
        )
        grad_middle = grad_middle.astype(BF16)
        datt[:, span] = dot(w_out[...], grad_middle).astype(BF16)
        gain_acc[...] += fold_lanes(weigh(back * unit))
        bias_acc[...] += fold_lanes(weigh(back))
        middle_r = grad_middle.T
        g_down[...] += dot(active, cot_r)
        up_acc[...] += dot(grad_up, weigh_rows(low.T))
        g_out[...] += dot(att_low, weigh_rows(middle_r))
        cot_sum = jnp.sum(cot_r.astype(F32), 0, keepdims=True)
        down_bias_acc[...] += cot_sum
        result_r = result.T
        y[0, pl.ds(start, columns), :] = result_r[:columns].astype(BF16)
        gm[0, pl.ds(start, columns), :] = middle_r[:columns]
        if with_class:
            yc[0] = result_r[columns : columns + classes].astype(BF16)
            gmc[0] = middle_r[columns:].astype(F32)[:classes]

    feed_step = 256
    pieces = genes // feed_step

    @pl.loop(0, pieces - 1)
    def _(piece):
        feed(pl.multiple_of(piece * feed_step, feed_step), feed_step, False)

    feed((pieces - 1) * feed_step, feed_step, True)

    for h in range(HEADS):
        own = slice(h * head, (h + 1) * head)
        inverse = inv_sum[h]
        grad = (datt[own, :genes].astype(F32) * inverse).astype(BF16)
        delta[h] = jnp.sum(grad.astype(F32) * (mix[h, :head, :] * inverse), 0, keepdims=True)
        datt[own, :genes] = grad
        blank = jnp.zeros_like(grad)
        qz[h] = jnp.concatenate([grad, blank] if h % 2 == 0 else [blank, grad], 0)
    grad_r = datt[:, :genes].T
    for h in range(HEADS):
        pair = slice((h // 2) * 2 * head, (h // 2 + 1) * 2 * head)
        dn[h] = jnp.where(half_lanes == h % 2, grad_r[:, pair].astype(F32), 0.0).astype(BF16)

    class_grad = datt[:, genes:].astype(F32).T[:classes]
    class_grad = by_head(class_grad) * class_inv
    class_grad_b = class_grad.astype(BF16)
    class_grad_h = (class_grad * 0.5).astype(BF16)
    query_ch = (query_c * 0.5).astype(BF16)
    class_delta = jnp.sum(
        class_grad_b.astype(F32) * (class_total * class_inv), -1, keepdims=True
    )

    class_dprob = dot(value_cb, datt[:, :genes])
    delta_rows = jnp.concatenate(
        [jnp.broadcast_to(delta[h], (classes, genes)) for h in range(HEADS)], 0
    )
    class_probs = probs_ck[...]
    class_dscore = (class_probs.astype(F32) * (class_dprob - delta_rows)).astype(BF16)
    dq_t[...] = dot(key_c_t, class_dscore)
    class_dkey = dot_nt(class_dscore, qt[0])
    class_dvalue = dot(class_probs, grad_r)
    own_dprob = dot(class_grad_b, value_c_t)
    own_dscore = (own_exp.astype(F32) * (own_dprob - class_delta)).astype(BF16)
    class_dquery = dot(own_dscore, key_cb)
    class_dkey = class_dkey + dot(own_dscore.astype(F32).T.astype(BF16), query_ch)
    class_dvalue = class_dvalue + dot(own_exp.astype(F32).T.astype(BF16), class_grad_h)

    def backward_block(block, class_dquery):
        start = nth_block(block)
        keys = pl.ds(start, KB)
        class_weights = probs_cq[:, keys]
        class_dprob = dot_nt(class_grad_b, vr[0, keys, :])
        dprobs = [dot(vr[0, keys, : 2 * head], qz[0])]
        class_dscore = (class_weights.astype(F32) * (class_dprob - class_delta)).astype(BF16)
        dkey = dot_tn(class_dscore, query_ch)
        dvalue = dot_tn(class_weights, class_grad_h)
        dkeys = [dkey[:, : 2 * head], dkey[:, 2 * head :]]
        dvalues = [dvalue[:, : 2 * head], dvalue[:, 2 * head :]]
        for h in range(HEADS):
            if h + 1 < HEADS:
                g = h + 1
                dprobs.append(
                    dot(vr[0, keys, (g // 2) * 2 * head : (g // 2 + 1) * 2 * head], qz[g])
                )
            weights = probs[h, keys, :]
            dscore = weights * (dprobs[h] - delta[h]).astype(BF16)
            own = slice(h * head, (h + 1) * head)
            dq_t[own, :] += dot(kt[0, own, keys], dscore)
            dkeys[h // 2] = dkeys[h // 2] + dot(dscore, qn[h])
            dvalues[h // 2] = dvalues[h // 2] + dot(weights, dn[h])
        valid = key_mask(start, (KB, 2 * width), 0)
        grads = jnp.where(valid, jnp.concatenate(dkeys + dvalues, 1), 0.0)
        packed_sum[:, width:] += jnp.sum(grads, 0, keepdims=True)
        grads = grads.astype(BF16)
        dkv[0, keys, :] = grads
        qkv_acc[:, width:] += dot(ut[0, :, keys], grads)
        return class_dquery + dot(class_dscore, kr[0, keys, :])

    class_dquery = lax.fori_loop(0, blocks, backward_block, class_dquery)

    def blank_rows(block):
        dkv[0, pl.ds(pl.multiple_of(block * KB, KB), KB), :] = jnp.zeros((KB, 2 * width), BF16)

    pl.loop(own_blocks, half_blocks)(blank_rows)
    pl.loop(half_blocks + other_blocks, 2 * half_blocks)(blank_rows)

    dquery = dq_t[...] * factor
    dquery_r = dquery.astype(BF16).T
    dq[0] = dquery_r
    qkv_acc[:, :width] += dot(ut[0, :, :genes], dquery_r)
    class_dquery = from_heads(class_dquery) * factor
    class_dkv = jnp.concatenate([from_heads(class_dkey), from_heads(class_dvalue)], 1)
    dqc[0] = class_dquery
    dkvc[0] = class_dkv
    class_packed = jnp.concatenate([class_dquery * 0.5, class_dkv], 1)
    class_unit, _ = norm_rows(xc[0].astype(F32))
    pad = jnp.zeros((128 - classes, width), F32)
    class_unit_t = jnp.concatenate([class_unit, pad], 0).T.astype(BF16)
    class_packed_p = jnp.concatenate([class_packed] + [jnp.zeros((128 - classes, 3 * width), F32)], 0)
    qkv_acc[...] += dot(class_unit_t, class_packed_p.astype(BF16))
    packed_sum[:, :width] += jnp.sum(dquery_r.astype(F32), 0, keepdims=True)
    packed_sum[...] += jnp.sum(class_packed, 0, keepdims=True)

    @pl.when(cell == cells - 1)
    def _():
        first = 0

        def put(values):
            nonlocal first
            rows = values.shape[0]
            for start in range(0, values.shape[1], 128):
                slab[first : first + rows, :] = values[:, start : start + 128].astype(BF16)
                first += rows

        put(up_acc[...].T)
        put(g_down[...])
        put(g_out[...])
        put(qkv_acc[...])
        g_vec[...] = jnp.zeros_like(g_vec)
        line = 0
        for vector in (
            jnp.sum(up_bias_acc[...].T, 0, keepdims=True),
            jnp.sum(gain_acc[...].T, 0, keepdims=True),
            jnp.sum(bias_acc[...].T, 0, keepdims=True),
            down_bias_acc[...],
            packed_sum[...],
        ):
            for start in range(0, vector.shape[1], 128):
                g_vec[line : line + 1, :] = vector[:, start : start + 128]
                line += 1


def layer(
    counts, place, tables, x, xc, cot, cotc, w_out, gain, bias, w_up, b_up, w_down, b_down
):
    cells, genes, width = x.shape
    classes = xc.shape[1]
    total = tables[1].shape[1]
    head = width // HEADS
    ff = w_up.shape[1]
    stack = HEADS * classes
    slab_rows = (2 * ff + 4 * width) * width // 128
    whole = lambda shape: pl.BlockSpec(
        shape, lambda c, *_: (0,) * len(shape), pipeline_mode=pl.Buffered(1)
    )
    per_cell = lambda *shape: pl.BlockSpec((1,) + shape, lambda c, *_: (c,) + (0,) * len(shape))
    kept = lambda *shape: whole(shape)
    out = lambda shape, kind=BF16: jax.ShapeDtypeStruct(shape, kind)
    vmem = lambda *shape, kind=BF16: pltpu.VMEM(shape, kind)
    f32 = functools.partial(vmem, kind=F32)
    return pl.pallas_call(
        layer_kernel,
        grid_spec=pltpu.PrefetchScalarGridSpec(
            num_scalar_prefetch=2,
            grid=(cells,),
            in_specs=[
                per_cell(width, genes),
                per_cell(total, width),
                per_cell(total, width),
                per_cell(width, total),
                per_cell(HEADS, head + 16, total),
                per_cell(width, total),
                per_cell(2, 8, 128),
                per_cell(classes, 3 * width),
                per_cell(genes, width),
                per_cell(classes, width),
                per_cell(genes, width),
                per_cell(classes, width),
                whole((width, width)),
                whole((1, width)),
                whole((1, width)),
                whole((width, ff)),
                whole((1, ff)),
                whole((ff, width)),
                whole((1, width)),
            ],
            out_specs=[
                per_cell(genes, width),
                per_cell(classes, width),
                per_cell(genes, width),
                per_cell(classes, width),
                per_cell(total, 2 * width),
                per_cell(classes, 2 * width),
                per_cell(genes, width),
                per_cell(classes, width),
                kept(slab_rows, 128),
                kept(VECTOR_ROWS, 128),
            ],
            scratch_shapes=[
                vmem(width, width),
                vmem(ff, width),
                vmem(width, ff),
                f32(width, 128),
                f32(width, 128),
                f32(ff, 128),
                f32(width, 128),
                vmem(HEADS, total, genes),
                vmem(stack, genes),
                vmem(stack, total),
                f32(HEADS, head + 16, genes),
                f32(HEADS, 1, genes),
                f32(stack, 128),
                f32(HEADS, 1, genes),
                vmem(HEADS, 2 * head, genes),
                vmem(HEADS, genes, 2 * head),
                vmem(HEADS, genes, 2 * head),
                f32(HEADS, 1, genes),
                vmem(width, genes + 128),
                vmem(width, genes + 128),
                vmem(width, genes + 128),
                f32(width, genes),
                f32(ff, width),
                f32(ff, width),
                f32(width, width),
                f32(width, 3 * width),
                f32(ff, 128),
                f32(width, 128),
                f32(width, 128),
                f32(1, width),
                f32(1, 3 * width),
            ],
        ),
        out_shape=[
            out((cells, genes, width)),
            out((cells, classes, width)),
            out((cells, genes, width)),
            out((cells, classes, width), F32),
            out((cells, total, 2 * width)),
            out((cells, classes, 2 * width), F32),
            out((cells, genes, width)),
            out((cells, classes, width), F32),
            out((slab_rows, 128)),
            out((VECTOR_ROWS, 128), F32),
        ],
        compiler_params=pltpu.CompilerParams(vmem_limit_bytes=VMEM),
        name="layer",
    )(counts, place, *tables, x, xc, cot, cotc, w_out, gain, bias, w_up, b_up, w_down, b_down)


def finish_kernel(
    orders,
    slab,
    vec,
    x,
    gm,
    dq,
    dkv,
    dkv_hbm,
    xc,
    gmc,
    dqc,
    dkvc,
    gain,
    bias,
    w,
    g_x,
    g_xc,
    slab_out,
    vec_out,
    w_t,
    work,
    summed,
    inbox,
    vec_in,
    other,
    other_c,
    send_sems,
    recv_sems,
    vec_send,
    vec_recv,
    swap_send,
    swap_recv,
    class_send,
    class_recv,
):
    step, steps = pl.program_id(0), pl.num_programs(0)
    cells = dkv_hbm.shape[0]
    genes = dkv_hbm.shape[1] // 2
    rows, width = x.shape[1:]
    classes = xc.shape[1]
    per_cell = genes // rows
    me, place = lax.axis_index("cell"), lax.axis_index("gene")
    bits = len(orders[0])
    part = slab.shape[0] // STREAMS
    half = part // 2
    mate = {"cell": me, "gene": 1 - place}

    def peer(bit):
        return {"cell": flip(me, 1 << bit), "gene": place}

    def remote(source, target, send, receive, device):
        return pltpu.make_async_remote_copy(
            src_ref=source,
            dst_ref=target,
            send_sem=send,
            recv_sem=receive,
            device_id=device,
            device_id_type=MESH,
        )

    def swap(cell):
        return remote(
            dkv_hbm.at[cell, pl.ds(genes, genes), :],
            other.at[cell],
            swap_send.at[cell],
            swap_recv.at[cell],
            mate,
        )

    def swap_class():
        return remote(dkvc, other_c, class_send, class_recv, mate)

    def low(stream, level):
        start, size = 0, half
        for i in range(level - 1):
            size = size // 2
            start = start + ((me // (1 << orders[stream][i])) % 2) * size
        return pl.multiple_of(start, 16) if level > 1 else start

    def length(level):
        return part >> level

    def box(level):
        return half - (half >> (level - 1)) + half if level else 0

    def gather(stream, level):
        sems = send_sems.at[stream, level], recv_sems.at[stream, level]
        if level == 0:
            source = slab.at[pl.ds(pl.multiple_of(stream * part + (1 - place) * half, 16), half), :]
            return remote(source, inbox.at[stream, pl.ds(0, half), :], *sems, mate)
        size = length(level + 1)
        bit = orders[stream][level - 1]
        away = 1 - (me // (1 << bit)) % 2
        start = pl.multiple_of(low(stream, level) + away * size, 16)
        return remote(
            work.at[stream, pl.ds(start, size), :],
            inbox.at[stream, pl.ds(box(level), size), :],
            *sems,
            peer(bit),
        )

    def add(stream, level):
        size = length(level + 1)
        if level == 0:
            mine = slab[pl.ds(pl.multiple_of(stream * part + place * half, 16), half), :]
            start = 0
        else:
            start = low(stream, level + 1)
            mine = work[stream, pl.ds(start, size), :]
        total = mine.astype(F32) + inbox[stream, pl.ds(box(level), size), :].astype(F32)
        total = total.astype(BF16)
        if level == bits:
            summed[pl.ds(pl.multiple_of(stream * part + place * half + start, 16), size), :] = total
        else:
            work[stream, pl.ds(start, size), :] = total

    def spread(stream, level):
        sems = send_sems.at[stream, 2 * bits + 1 - level], recv_sems.at[stream, 2 * bits + 1 - level]
        size = length(level + 1)
        start = low(stream, level + 1) if level else 0
        span = pl.ds(pl.multiple_of(stream * part + place * half + start, 16), size)
        device = peer(orders[stream][level - 1]) if level else mate
        return remote(summed.at[span, :], summed.at[span, :], *sems, device)

    def vector(level):
        device = peer(orders[0][level - 1]) if level else mate
        return remote(
            vec if level == 0 else vec_out,
            vec_in.at[level],
            vec_send.at[level],
            vec_recv.at[level],
            device,
        )

    def stage(index):
        if index > 0:
            if index - 1 <= bits:
                for stream in range(STREAMS):
                    gather(stream, index - 1).wait()
                    add(stream, index - 1)
                vector(index - 1).wait()
                before = vec[...] if index == 1 else vec_out[...]
                vec_out[...] = before + vec_in[index - 1]
            else:
                for stream in range(STREAMS):
                    spread(stream, 2 * bits + 2 - index).wait()
        if index <= bits:
            for stream in range(STREAMS):
                gather(stream, index).start()
            vector(index).start()
        elif index < 2 * bits + 2:
            for stream in range(STREAMS):
                spread(stream, 2 * bits + 1 - index).start()

    def rows_back(values, grads, packed):
        unit, inverse = norm_rows(values)
        scaled = dot(packed, w_t[...]) * gain[...]
        return grads + inverse * (
            scaled
            - jnp.mean(scaled, -1, keepdims=True)
            - unit * jnp.mean(scaled * unit, -1, keepdims=True)
        )

    stages = 2 * bits + 3
    last = cells * per_cell - 1
    for index in range(min(stages, last + 1)):

        @pl.when(step == index)
        def _(index=index):
            if index == 0:
                greet([mate] + [peer(bit) for bit in range(bits)])
            stage(index)
            if index == 0:
                for cell in range(cells):
                    swap(cell).start()
                swap_class().start()
                w_t[...] = w[...].T

    cell = step // per_cell

    @pl.when(step % per_cell == 0)
    def _():
        swap(cell).wait()

    grads = dkv[0].astype(F32) + other[
        cell, pl.ds(pl.multiple_of((step % per_cell) * rows, 16), rows), :
    ].astype(F32)
    packed = jnp.concatenate([dq[0], grads.astype(BF16)], 1)
    g_x[0] = rows_back(x[0].astype(F32), gm[0].astype(F32), packed).astype(BF16)

    @pl.when(step == steps - 1)
    def _():
        swap_class().wait()
        class_grads = dkvc[...] + other_c[...]
        stack = cells * classes
        packed = jnp.concatenate([dqc[...], class_grads], 2).reshape(stack, 3 * width)
        values = xc[...].astype(F32).reshape(stack, width)
        result = rows_back(values, gmc[...].reshape(stack, width), packed.astype(BF16))
        g_xc[...] = result.reshape(cells, classes, width).astype(BF16)
        for index in range(last + 1, stages):
            stage(index)
        slab_out[...] = summed[...]


def finish(orders, slab, vec, x, xc, gm, gmc, dq, dqc, dkv, dkvc, gain, bias, w):
    cells, genes, width = x.shape
    classes = xc.shape[1]
    rows = genes // 2
    per_cell = genes // rows
    bits = len(orders[0])
    part = slab.shape[0] // STREAMS
    whole = lambda array: pl.BlockSpec(array.shape, lambda i: (0,) * array.ndim)
    piece = lambda lanes: pl.BlockSpec((1, rows, lanes), lambda i: (i // per_cell, i % per_cell, 0))
    out = lambda shape, kind=BF16: jax.ShapeDtypeStruct(shape, kind)
    dma = lambda *shape: pltpu.SemaphoreType.DMA(shape)
    outs = [
        out((cells, genes, width)),
        out((cells, classes, width)),
        out(slab.shape),
        out(vec.shape, F32),
    ]
    return pl.pallas_call(
        functools.partial(finish_kernel, orders),
        grid=(cells * per_cell,),
        in_specs=[
            whole(slab),
            whole(vec),
            piece(width),
            piece(width),
            piece(width),
            piece(2 * width),
            pl.BlockSpec(memory_space=pl.ANY),
            whole(xc),
            whole(gmc),
            whole(dqc),
            whole(dkvc),
            whole(gain),
            whole(bias),
            whole(w),
        ],
        out_specs=[piece(width)] + [whole(o) for o in outs[1:]],
        out_shape=outs,
        scratch_shapes=[
            pltpu.VMEM((3 * width, width), BF16),
            pltpu.VMEM((STREAMS, part // 2, 128), BF16),
            pltpu.VMEM(slab.shape, BF16),
            pltpu.VMEM((STREAMS, part, 128), BF16),
            pltpu.VMEM((bits + 1,) + vec.shape, F32),
            pltpu.VMEM((cells, genes, 2 * width), BF16),
            pltpu.VMEM(dkvc.shape, F32),
            dma(STREAMS, 2 * bits + 2),
            dma(STREAMS, 2 * bits + 2),
            dma(bits + 1),
            dma(bits + 1),
            dma(cells),
            dma(cells),
            dma(),
            dma(),
        ],
        compiler_params=pltpu.CompilerParams(
            vmem_limit_bytes=VMEM, collective_id=1, has_side_effects=True
        ),
        name="finish",
    )(slab, vec, x, gm, dq, dkv, dkv, xc, gmc, dqc, dkvc, gain, bias, w)


def unpack_kernel(slab, vec, gain, bias, w, g_up, g_down, g_out, g_qkv, *vectors):
    width, ff = g_up.shape
    first = 0

    def take(target):
        nonlocal first
        rows = target.shape[0]
        for start in range(0, target.shape[1], 128):
            target[:, start : start + 128] = slab[first : first + rows, :].astype(F32)
            first += rows

    take(g_up)
    take(g_down)
    take(g_out)
    take(g_qkv)
    line = 0

    def lines(count):
        nonlocal line
        line += count
        return jnp.concatenate([vec[i : i + 1, :] for i in range(line - count, line)], 1)

    up_bias, ln2_gain, ln2_bias, down_bias, ln1_gain, ln1_bias = vectors
    up_bias[...] = lines(ff // 128)
    ln2_gain[...] = lines(width // 128)
    ln2_bias[...] = lines(width // 128)
    down_bias[...] = lines(width // 128)
    packed_sum = lines(3 * width // 128)
    weights = w[...].astype(F32)
    sums = g_qkv[...]
    ln1_gain[...] = jnp.sum((weights * sums).T, 0, keepdims=True)
    ln1_bias[...] = jnp.sum((weights * packed_sum).T, 0, keepdims=True)
    g_qkv[...] = (
        widen(spread_column(gain[...]), 3 * width) * sums
        + widen(spread_column(bias[...]), 3 * width) * packed_sum
    )


def unpack(slab, vec, gain, bias, w, ff):
    width = w.shape[0]
    out = lambda *shape: jax.ShapeDtypeStruct(shape, F32)
    row = out(1, width)
    return pl.pallas_call(
        unpack_kernel,
        out_shape=[
            out(width, ff),
            out(ff, width),
            out(width, width),
            out(width, 3 * width),
            out(1, ff),
            row,
            row,
            row,
            row,
            row,
        ],
        compiler_params=pltpu.CompilerParams(vmem_limit_bytes=VMEM),
        name="unpack",
    )(slab, vec, gain, bias, w)


def shards(
    gene_in,
    class_in,
    expressed,
    ln1_gain,
    ln1_bias,
    w_qkv,
    w_out,
    ln2_gain,
    ln2_bias,
    w_up,
    b_up,
    w_down,
    b_down,
    gene_cot,
    class_cot,
):
    row = lambda vector: vector.reshape(1, -1)
    place = lax.axis_index("gene").reshape(1)
    bits = (lax.axis_size("cell") - 1).bit_length()
    near = list(range(bits - 1))
    orders = [near[i % len(near) :] + near[: i % len(near)] + [bits - 1] for i in range(STREAMS)]
    gain1, bias1 = row(ln1_gain), row(ln1_bias)
    tables = project(expressed, gene_in, class_in, gain1, bias1, w_qkv)
    gene_out, class_out, dq, dqc, dkv, dkvc, gm, gmc, slab, vec = layer(
        expressed,
        place,
        tables,
        gene_in,
        class_in,
        gene_cot,
        class_cot,
        w_out,
        row(ln2_gain),
        row(ln2_bias),
        w_up,
        row(b_up),
        w_down,
        row(b_down),
    )
    gene_grad, class_grad, slab, vec = finish(
        orders, slab, vec, gene_in, class_in, gm, gmc, dq, dqc, dkv, dkvc, gain1, bias1, w_qkv
    )
    g_up, g_down, g_out, g_qkv, g_b_up, g_gain2, g_bias2, g_b_down, g_gain1, g_bias1 = unpack(
        slab, vec, gain1, bias1, w_qkv, w_up.shape[1]
    )
    return (
        gene_out,
        class_out,
        gene_grad,
        class_grad,
        g_gain1[0],
        g_bias1[0],
        g_qkv,
        g_out,
        g_gain2[0],
        g_bias2[0],
        g_up,
        g_b_up[0],
        g_down,
        g_b_down[0],
    )


def solution(mesh):
    genes, cells, whole = P("cell", "gene", None), P("cell", None, None), P()
    return jax.shard_map(
        shards,
        mesh=mesh,
        in_specs=(genes, cells, P("cell")) + (whole,) * 10 + (genes, cells),
        out_specs=(genes, cells, genes, cells) + (whole,) * 10,
        check_vma=False,
    )
```

```python
import functools

import jax
import jax.numpy as jnp
from jax import lax
from jax.experimental import pallas as pl
from jax.experimental.pallas import tpu as pltpu
from jax.sharding import PartitionSpec as P

HEADS = 4
EPS = 1e-05
LOG2E = 1.4426950408889634
SAFE = 40.0
KB = 256
STREAMS = 3
MARKS = 3
VECTOR_ROWS = 32
VMEM = 63 * 2**20
F32 = jnp.float32
BF16 = jnp.bfloat16
MESH = pl.DeviceIdType.MESH


def dot(left, right):
    return jnp.dot(left, right, preferred_element_type=F32)


def dot_nt(left, right):
    return lax.dot_general(left, right, (((1,), (1,)), ((), ())), preferred_element_type=F32)


def dot_tn(left, right):
    return lax.dot_general(left, right, (((0,), (0,)), ((), ())), preferred_element_type=F32)


def spread_column(row):
    return jnp.broadcast_to(row, (128, row.shape[1])).T


def widen(column, lanes):
    return jnp.concatenate([column] * (lanes // 128), axis=1)


def fold_lanes(values):
    total = values[:, :128]
    for start in range(128, values.shape[1], 128):
        total = total + values[:, start : start + 128]
    return total


def norm_rows(values):
    centered = values - jnp.mean(values, -1, keepdims=True)
    inverse = lax.rsqrt(jnp.mean(centered * centered, -1, keepdims=True) + EPS)
    return centered * inverse, inverse


def norm_columns(values):
    scale = 1.0 / values.shape[0]
    centered = values - jnp.sum(values, 0, keepdims=True) * scale
    inverse = lax.rsqrt(jnp.sum(centered * centered, 0, keepdims=True) * scale + EPS)
    return centered * inverse, inverse


def flip(index, stride):
    return index + stride * (1 - 2 * ((index // stride) % 2))


def greet(partners):
    barrier = pltpu.get_barrier_semaphore()
    for partner in partners:
        pl.semaphore_signal(barrier, inc=1, device_id=partner, device_id_type=MESH)
    pl.semaphore_wait(barrier, len(partners))


def project_kernel(
    counts,
    x,
    x_hbm,
    xc,
    gain,
    bias,
    w,
    qt,
    kr,
    va,
    ut,
    stat,
    pc,
    w_t,
    gain_c,
    bias_c,
    other,
    sent,
    received,
):
    cell, half = pl.program_id(0), pl.program_id(1)
    cells = x_hbm.shape[0]
    genes, width = x.shape[1:]
    head = width // HEADS
    place = lax.axis_index("gene")
    partner = {"cell": lax.axis_index("cell"), "gene": 1 - place}

    def swap(index):
        return pltpu.make_async_remote_copy(
            src_ref=x_hbm.at[index],
            dst_ref=other.at[index],
            send_sem=sent.at[index],
            recv_sem=received.at[index],
            device_id=partner,
            device_id_type=MESH,
        )

    @pl.when((cell == 0) & (half == 0))
    def _():
        greet([partner])
        for index in range(cells):
            swap(index).start()
        w_t[...] = w[...].T
        gain_c[...] = spread_column(gain[...])
        bias_c[...] = spread_column(bias[...])

    def norms(columns, first):
        for h in range(HEADS):
            part = columns[h * head : (h + 1) * head]
            size = jnp.sum(part * part, 0, keepdims=True)
            best = size[:, :128]
            for start in range(128, genes, 128):
                best = jnp.maximum(best, size[:, start : start + 128])
            stat[0, 0, first + h : first + h + 1, :] = best

    def tables(values, origin):
        unit, _ = norm_columns(values.T.astype(F32))
        ut[0] = unit.astype(BF16)
        low = unit * widen(gain_c[...], genes) + widen(bias_c[...], genes)
        spot = origin + lax.broadcasted_iota(jnp.int32, (1, genes), 1)
        valid = spot < counts[cell]
        kept = jnp.where(valid, low, 0.0).astype(BF16)
        packed_t = dot(w_t[width:, :], kept)
        mark = jnp.where(
            (lax.broadcasted_iota(jnp.int32, (16, genes), 0) < MARKS) & valid, 1.0, 0.0
        ).astype(BF16)
        for h in range(HEADS):
            va[0, h, :head, :] = packed_t[width + h * head : width + (h + 1) * head].astype(BF16)
            va[0, h, head:, :] = mark
        kr[0] = packed_t[:width].astype(BF16).T
        stat[...] = jnp.zeros_like(stat)
        norms(packed_t[:width], 0)
        return low

    @pl.when(half == 0)
    def _():
        low = tables(x[0], place * genes)
        query_t = dot(w_t[:width, :], low.astype(BF16)).astype(BF16) * (head**-0.5)
        qt[0] = query_t
        norms(query_t.astype(F32), HEADS)
        unit, _ = norm_rows(xc[0].astype(F32))
        class_low = (unit * gain[...] + bias[...]).astype(BF16)
        pc[0] = dot(class_low, w[...]).astype(BF16).astype(F32)

    @pl.when(half == 1)
    def _():
        swap(cell).wait_recv()
        tables(other[cell], (1 - place) * genes)

    @pl.when((cell == cells - 1) & (half == 1))
    def _():
        for index in range(cells):
            swap(index).wait_send()


def project(counts, x, xc, gain, bias, w):
    cells, genes, width = x.shape
    total = 2 * genes
    classes = xc.shape[1]
    head = width // HEADS
    whole = lambda shape: pl.BlockSpec(shape, lambda c, h: (0,) * len(shape))
    rows = pl.BlockSpec((1, genes, width), lambda c, h: (c, h, 0))
    columns = pl.BlockSpec((1, width, genes), lambda c, h: (c, 0, h))
    per_cell = lambda *shape: pl.BlockSpec((1,) + shape, lambda c, h: (c,) + (0,) * len(shape))
    out = lambda shape, kind=BF16: jax.ShapeDtypeStruct(shape, kind)
    return pl.pallas_call(
        project_kernel,
        grid=(cells, 2),
        in_specs=[
            pl.BlockSpec(memory_space=pltpu.SMEM),
            per_cell(genes, width),
            pl.BlockSpec(memory_space=pl.ANY),
            per_cell(classes, width),
            whole((1, width)),
            whole((1, width)),
            whole((width, 3 * width)),
        ],
        out_specs=[
            per_cell(width, genes),
            rows,
            pl.BlockSpec((1, HEADS, head + 16, genes), lambda c, h: (c, 0, 0, h)),
            columns,
            pl.BlockSpec((1, 1, 8, 128), lambda c, h: (c, h, 0, 0)),
            per_cell(classes, 3 * width),
        ],
        out_shape=[
            out((cells, width, genes)),
            out((cells, total, width)),
            out((cells, HEADS, head + 16, total)),
            out((cells, width, total)),
            out((cells, 2, 8, 128), F32),
            out((cells, classes, 3 * width), F32),
        ],
        scratch_shapes=[
            pltpu.VMEM((3 * width, width), BF16),
            pltpu.VMEM((width, 128), F32),
            pltpu.VMEM((width, 128), F32),
            pltpu.VMEM((cells, genes, width), BF16),
            pltpu.SemaphoreType.DMA((cells,)),
            pltpu.SemaphoreType.DMA((cells,)),
        ],
        compiler_params=pltpu.CompilerParams(
            vmem_limit_bytes=VMEM, collective_id=0, has_side_effects=True
        ),
        name="project",
    )(counts, x, x, xc, gain, bias, w)


def gelu_parts(u):
    phi = 0.5 + 0.5 * lax.erf(u * 0.7071067811865476)
    bell = jnp.exp2((u * u) * (-0.5 * LOG2E))
    return u * phi, phi + (u * 0.3989422804014327) * bell


def layer_kernel(
    counts,
    place,
    qt,
    kr,
    va,
    ut,
    stat,
    pc,
    x,
    xc,
    cot,
    cotc,
    w_out,
    gain,
    bias,
    w_up,
    b_up,
    w_down,
    b_down,
    y,
    yc,
    dq,
    dqc,
    dkv,
    dkvc,
    gm,
    gmc,
    slab,
    g_vec,
    w_out_t,
    w_up_t,
    w_down_t,
    gain_c,
    bias_c,
    b_up_c,
    b_down_c,
    probs,
    probs_ck,
    probs_cq,
    mix,
    shift,
    shift_q,
    inv_sum,
    qz,
    da,
    delta,
    att,
    datt,
    x_t,
    dq_acc,
    up_acc,
    g_down,
    g_out,
    qkv_acc,
    up_bias_acc,
    gain_acc,
    bias_acc,
    down_bias_acc,
    packed_sum,
    packed_cols,
):
    cell = pl.program_id(0)
    cells = pl.num_programs(0)
    genes, width = x.shape[1:]
    classes = xc.shape[1]
    head = width // HEADS
    ff = w_up.shape[1]
    stack = HEADS * classes
    factor = head**-0.5
    count = counts[cell]
    own_count = jnp.clip(count - place[0] * genes, 0, genes)
    other_count = jnp.clip(count - (1 - place[0]) * genes, 0, genes)
    own_blocks = (own_count + (KB - 1)) // KB
    other_blocks = (other_count + (KB - 1)) // KB
    half_blocks = genes // KB
    blocks = own_blocks + other_blocks

    def nth_block(index):
        block = jnp.where(index < own_blocks, index, index - own_blocks + half_blocks)
        return pl.multiple_of(block * KB, KB)

    @pl.when(cell == 0)
    def _():
        w_out_t[...] = w_out[...].T
        w_up_t[...] = w_up[...].T
        w_down_t[...] = w_down[...].T
        gain_c[...] = spread_column(gain[...])
        bias_c[...] = spread_column(bias[...])
        b_up_c[...] = spread_column(b_up[...])
        b_down_c[...] = spread_column(b_down[...])
        up_acc[...] = jnp.zeros_like(up_acc)
        up_bias_acc[...] = jnp.zeros_like(up_bias_acc)
        gain_acc[...] = jnp.zeros_like(gain_acc)
        bias_acc[...] = jnp.zeros_like(bias_acc)
        down_bias_acc[...] = jnp.zeros_like(down_bias_acc)
        g_down[...] = jnp.zeros_like(g_down)
        g_out[...] = jnp.zeros_like(g_out)
        qkv_acc[...] = jnp.zeros_like(qkv_acc)
        packed_sum[...] = jnp.zeros_like(packed_sum)
        packed_cols[...] = jnp.zeros_like(packed_cols)

    head_mask = lax.broadcasted_iota(jnp.int32, (stack, width), 1) // head == (
        lax.broadcasted_iota(jnp.int32, (stack, width), 0) // classes
    )
    pair_mask = lax.broadcasted_iota(jnp.int32, (stack, stack), 1) // classes == (
        lax.broadcasted_iota(jnp.int32, (stack, stack), 0) // classes
    )

    def by_head(rows):
        return jnp.where(head_mask, jnp.concatenate([rows] * HEADS, 0), 0.0)

    def from_heads(rows):
        kept = jnp.where(head_mask, rows, 0.0)
        total = kept[:classes]
        for h in range(1, HEADS):
            total = total + kept[h * classes : (h + 1) * classes]
        return total

    packed_c = pc[0]
    query_c = by_head(packed_c[:, :width] * factor)
    key_c = by_head(packed_c[:, width : 2 * width])
    value_c = by_head(packed_c[:, 2 * width :])
    key_c_t = key_c.T.astype(BF16)
    value_c_t = value_c.T.astype(BF16)
    query_cb, key_cb, value_cb = query_c.astype(BF16), key_c.astype(BF16), value_c.astype(BF16)

    half_rows = lax.broadcasted_iota(jnp.int32, (2 * head, genes), 0) // head
    for h in range(HEADS):
        pair = slice((h // 2) * 2 * head, (h // 2 + 1) * 2 * head)
        qz[h] = jnp.where(half_rows == h % 2, qt[0, pair, :].astype(F32), 0.0).astype(BF16)

    size_k = jnp.max(jnp.maximum(stat[0, 0, :HEADS], stat[0, 1, :HEADS]))
    size_q = jnp.max(jnp.maximum(stat[0, 0, HEADS:], stat[0, 1, HEADS:]))
    size_k = jnp.maximum(size_k, jnp.max(jnp.sum(key_c * key_c, -1, keepdims=True)))
    size_q = jnp.maximum(size_q, jnp.max(jnp.sum(query_c * query_c, -1, keepdims=True)))
    safe = size_k * size_q < SAFE * SAFE

    def key_mask(start, shape, axis):
        limit = jnp.where(start < genes, own_count, genes + other_count)
        return start + lax.broadcasted_iota(jnp.int32, shape, axis) < limit

    shift[...] = jnp.zeros_like(shift)
    shift_q[...] = jnp.zeros_like(shift_q)

    @pl.when(jnp.logical_not(safe))
    def _():
        class_scores = dot(key_cb, qt[0])
        for h in range(HEADS):
            shift[h] = jnp.max(class_scores[h * classes : (h + 1) * classes], 0, keepdims=True)
        own_scores = jnp.where(pair_mask, dot(query_cb, key_c_t), -1e30)
        shift_q[...] = jnp.broadcast_to(jnp.max(own_scores, -1, keepdims=True), shift_q.shape)

        @pl.loop(0, blocks)
        def _(block):
            start = nth_block(block)
            for h in range(HEADS):
                scores = dot(
                    kr[0, pl.ds(start, KB), (h // 2) * 2 * head : (h // 2 + 1) * 2 * head], qz[h]
                )
                scores = jnp.where(key_mask(start, scores.shape, 0), scores, -1e30)
                shift[h] = jnp.maximum(shift[h], jnp.max(scores, 0, keepdims=True))
            scores = dot_nt(query_cb, kr[0, pl.ds(start, KB), :])
            scores = jnp.where(key_mask(start, scores.shape, 1), scores, -1e30)
            shift_q[...] = jnp.maximum(shift_q[...], jnp.max(scores, -1, keepdims=True))

        shift[...] = shift[...] * LOG2E
        shift_q[...] = shift_q[...] * LOG2E

    class_scores = dot(key_cb, qt[0])
    shift_rows = jnp.concatenate(
        [jnp.broadcast_to(shift[h], (classes, genes)) for h in range(HEADS)], 0
    )
    class_exp = jnp.exp2(class_scores * LOG2E - shift_rows).astype(BF16)
    probs_ck[...] = class_exp
    class_mix = dot(value_c_t, class_exp)
    for h in range(HEADS):
        mix[h, :head, :] = class_mix[h * head : (h + 1) * head]
        sums = jnp.sum(
            class_exp[h * classes : (h + 1) * classes].astype(F32), 0, keepdims=True
        )
        mix[h, head:, :] = jnp.where(
            lax.broadcasted_iota(jnp.int32, (16, genes), 0) == 0, sums, 0.0
        )
    shift_qc = shift_q[:, :1]
    own_exp = jnp.where(
        pair_mask, jnp.exp2(dot(query_cb, key_c_t) * LOG2E - shift_qc), 0.0
    ).astype(BF16)
    deep = head + 16

    def spread_heads(rows, extra):
        pieces = []
        for h in range(HEADS):
            pieces += [rows[:, h * head : (h + 1) * head], extra]
        return jnp.concatenate(pieces, 1)

    own_mix = spread_heads(
        dot(own_exp, value_cb),
        jnp.broadcast_to(jnp.sum(own_exp.astype(F32), -1, keepdims=True), (stack, 16)),
    )

    def forward_block(block, class_total, shifted):
        start = nth_block(block)
        keys = pl.ds(start, KB)
        scores = [
            dot(kr[0, keys, (h // 2) * 2 * head : (h // 2 + 1) * 2 * head], qz[h])
            for h in range(1)
        ]
        class_scores = dot_nt(query_cb, kr[0, keys, :]) * LOG2E - shift_qc
        for h in range(HEADS):
            if h + 1 < HEADS:
                g = h + 1
                scores.append(
                    dot(kr[0, keys, (g // 2) * 2 * head : (g // 2 + 1) * 2 * head], qz[g])
                )
            scaled = scores[h] * LOG2E
            if shifted:
                scaled = jnp.minimum(scaled - shift[h], 60.0)
            exps = jnp.exp2(scaled).astype(BF16)
            mix[h] += dot(va[0, h, :, keys], exps)
            probs[h, :, keys] = exps.T
        class_exp = jnp.where(
            key_mask(start, class_scores.shape, 1), jnp.exp2(class_scores), 0.0
        ).astype(BF16)
        probs_cq[:, keys] = class_exp
        return class_total + dot_nt(class_exp, va[0, :, :, keys].reshape(HEADS * deep, KB))

    class_total = lax.cond(
        safe,
        lambda: lax.fori_loop(0, blocks, functools.partial(forward_block, shifted=False), own_mix),
        lambda: lax.fori_loop(0, blocks, functools.partial(forward_block, shifted=True), own_mix),
    )
    class_sum = jnp.concatenate(
        [
            class_total[h * classes : (h + 1) * classes, h * deep + head : h * deep + head + 1]
            for h in range(HEADS)
        ],
        0,
    )
    class_total = jnp.concatenate(
        [class_total[:, h * deep : h * deep + head] for h in range(HEADS)], 1
    )
    class_inv = 1.0 / class_sum
    class_att = from_heads(class_total * class_inv)
    for h in range(HEADS):
        inverse = 1.0 / mix[h, head : head + 1, :]
        inv_sum[h] = inverse
        att[h * head : (h + 1) * head, :genes] = (mix[h, :head, :] * inverse).astype(BF16)

    def pad_rows(rows):
        return jnp.concatenate([rows, jnp.zeros((128 - rows.shape[0], width), F32)], 0)

    x_t[:, :genes] = x[0].T
    x_t[:, genes:] = pad_rows(xc[0].astype(F32)).T.astype(BF16)
    att[:, genes:] = pad_rows(class_att).T.astype(BF16)

    def feed(start, columns, with_class):
        lanes = columns + (128 if with_class else 0)
        span = pl.ds(start, lanes)
        wide_gain, wide_bias = widen(gain_c[...], lanes), widen(bias_c[...], lanes)
        cot_r = cot[0, pl.ds(start, columns), :]
        cot_t = cot_r.T
        if with_class:
            padded = pad_rows(cotc[0].astype(F32))
            cot_t = jnp.concatenate([cot_t, padded.T.astype(BF16)], 1)
            cot_r = jnp.concatenate([cot_r, (padded * 0.5).astype(BF16)], 0)
            share = jnp.where(
                lax.broadcasted_iota(jnp.int32, (1, lanes), 1) < columns, 1.0, 0.5
            )
            weigh = lambda values: values * share
            row_share = jnp.where(
                lax.broadcasted_iota(jnp.int32, (lanes, 1), 0) < columns, 1.0, 0.5
            )
            weigh_rows = lambda rows: (rows.astype(F32) * row_share).astype(BF16)
        else:
            weigh = lambda values: values
            weigh_rows = lambda rows: rows
        att_low = att[:, span]
        middle = x_t[:, span].astype(F32) + dot(w_out_t[...], att_low)
        grad_act = dot(w_down[...], cot_t)
        unit, inverse = norm_columns(middle)
        low = (unit * wide_gain + wide_bias).astype(BF16)
        up = dot(w_up_t[...], low) + widen(b_up_c[...], lanes)
        active, slope = gelu_parts(up)
        active = active.astype(BF16)
        grad_up = slope * grad_act
        up_bias_acc[...] += fold_lanes(weigh(grad_up))
        grad_up = grad_up.astype(BF16)
        result = middle + dot(w_down_t[...], active) + widen(b_down_c[...], lanes)
        back = dot(w_up[...], grad_up)
        scaled = back * wide_gain
        scale = 1.0 / width
        grad_middle = cot_t.astype(F32) + inverse * (
            scaled
            - jnp.sum(scaled, 0, keepdims=True) * scale
            - unit * (jnp.sum(scaled * unit, 0, keepdims=True) * scale)
        )
        grad_middle = grad_middle.astype(BF16)
        datt[:, span] = dot(w_out[...], grad_middle).astype(BF16)
        gain_acc[...] += fold_lanes(weigh(back * unit))
        bias_acc[...] += fold_lanes(weigh(back))
        middle_r = grad_middle.T
        g_down[...] += dot(active, cot_r)
        up_acc[...] += dot(grad_up, weigh_rows(low.T))
        g_out[...] += dot(att_low, weigh_rows(middle_r))
        cot_sum = jnp.sum(cot_r.astype(F32), 0, keepdims=True)
        down_bias_acc[...] += cot_sum
        result_r = result.T
        y[0, pl.ds(start, columns), :] = result_r[:columns].astype(BF16)
        gm[0, pl.ds(start, columns), :] = middle_r[:columns]
        if with_class:
            yc[0] = result_r[columns : columns + classes].astype(BF16)
            gmc[0] = middle_r[columns:].astype(F32)[:classes]

    feed_step = 512
    pieces = genes // feed_step

    @pl.loop(0, pieces - 1)
    def _(piece):
        feed(pl.multiple_of(piece * feed_step, feed_step), feed_step, False)

    feed((pieces - 1) * feed_step, feed_step, True)

    for h in range(HEADS):
        own = slice(h * head, (h + 1) * head)
        inverse = inv_sum[h]
        grad = (datt[own, :genes].astype(F32) * inverse).astype(BF16)
        row_delta = jnp.sum(grad.astype(F32) * (mix[h, :head, :] * inverse), 0, keepdims=True)
        delta[h] = row_delta
        datt[own, :genes] = grad
        parts = jnp.zeros((16, genes), F32)
        rest = row_delta
        for i in range(MARKS):
            piece = rest.astype(BF16).astype(F32)
            rest = rest - piece
            parts = jnp.where(
                lax.broadcasted_iota(jnp.int32, (16, genes), 0) == i, -piece, parts
            )
        blank = jnp.zeros((2 * head - deep, genes), BF16)
        da[h] = jnp.concatenate([grad, parts.astype(BF16), blank], 0).T

    class_grad = datt[:, genes:].astype(F32).T[:classes]
    class_grad = by_head(class_grad) * class_inv
    class_grad_b = class_grad.astype(BF16)
    class_grad_h = (class_grad * 0.5).astype(BF16)
    query_ch = (query_c * 0.5).astype(BF16)
    class_delta = jnp.sum(
        class_grad_b.astype(F32) * (class_total * class_inv), -1, keepdims=True
    )

    class_dprob = dot(value_cb, datt[:, :genes])
    delta_rows = jnp.concatenate(
        [jnp.broadcast_to(delta[h], (classes, genes)) for h in range(HEADS)], 0
    )
    class_probs = probs_ck[...]
    class_dscore = (class_probs.astype(F32) * (class_dprob - delta_rows)).astype(BF16)
    dq_acc[...] = dot_tn(class_dscore, key_cb)
    class_dkey = dot_nt(class_dscore, qt[0])
    class_dvalue = dot_nt(class_probs, datt[:, :genes])
    own_dprob = dot(class_grad_b, value_c_t)
    own_dscore = (own_exp.astype(F32) * (own_dprob - class_delta)).astype(BF16)
    class_dquery = dot(own_dscore, key_cb)
    class_dkey = class_dkey + dot(own_dscore.astype(F32).T.astype(BF16), query_ch)
    class_dvalue = class_dvalue + dot(own_exp.astype(F32).T.astype(BF16), class_grad_h)

    class_grad_s = spread_heads(class_grad_b, jnp.zeros((stack, 16), BF16))
    class_grad_ht = class_grad_h.T
    query_ct = query_ch.T
    pair_lanes = lax.broadcasted_iota(jnp.int32, (KB, 2 * head), 1) // head

    def backward_block(block, class_dquery):
        start = nth_block(block)
        keys = pl.ds(start, KB)
        dprobs = [dot(da[0, :, :deep], va[0, 0, :, keys])]
        class_weights = probs_cq[:, keys]
        class_dprob = dot(class_grad_s, va[0, :, :, keys].reshape(HEADS * deep, KB))
        class_dscore = (class_weights.astype(F32) * (class_dprob - class_delta)).astype(BF16)
        dkeys, dvalues, dscores, zeroed = [], [], [], []
        for h in range(HEADS):
            if h + 1 < HEADS:
                dprobs.append(dot(da[h + 1, :, :deep], va[0, h + 1, :, keys]))
            weights = probs[h, :, keys]
            dscore = weights * dprobs[h].astype(BF16)
            own = slice(h * head, (h + 1) * head)
            dvalues.append(dot(datt[own, :genes], weights))
            dkeys.append(dot(qt[0, own, :], dscore))
            pair = slice((h // 2) * 2 * head, (h // 2 + 1) * 2 * head)
            dscores.append(dscore)
            zeroed.append(
                jnp.where(pair_lanes == h % 2, kr[0, keys, pair].astype(F32), 0.0).astype(BF16)
            )
            if h % 2 == 1:
                dq_acc[:, pair] += dot(
                    jnp.concatenate(dscores[h - 1 :], 1), jnp.concatenate(zeroed[h - 1 :], 0)
                )
        dkey = jnp.concatenate(dkeys, 0) + dot(query_ct, class_dscore)
        dvalue = jnp.concatenate(dvalues, 0) + dot(class_grad_ht, class_weights)
        valid = key_mask(start, (1, KB), 1)
        grads = jnp.where(valid, jnp.concatenate([dkey, dvalue], 0), 0.0)
        packed_cols[...] += fold_lanes(grads)
        grads = grads.astype(BF16).T
        dkv[0, keys, :] = grads
        qkv_acc[:, width:] += dot(ut[0, :, keys], grads)
        return class_dquery + dot(class_dscore, kr[0, keys, :])

    class_dquery = lax.fori_loop(0, blocks, backward_block, class_dquery)

    def blank_rows(block):
        dkv[0, pl.ds(pl.multiple_of(block * KB, KB), KB), :] = jnp.zeros((KB, 2 * width), BF16)

    pl.loop(own_blocks, half_blocks)(blank_rows)
    pl.loop(half_blocks + other_blocks, 2 * half_blocks)(blank_rows)

    dquery_r = (dq_acc[...] * factor).astype(BF16)
    dq[0] = dquery_r
    qkv_acc[:, :width] += dot(ut[0, :, :genes], dquery_r)
    class_dquery = from_heads(class_dquery) * factor
    class_dkv = jnp.concatenate([from_heads(class_dkey), from_heads(class_dvalue)], 1)
    dqc[0] = class_dquery
    dkvc[0] = class_dkv
    class_packed = jnp.concatenate([class_dquery * 0.5, class_dkv], 1)
    class_unit, _ = norm_rows(xc[0].astype(F32))
    pad = jnp.zeros((128 - classes, width), F32)
    class_unit_t = jnp.concatenate([class_unit, pad], 0).T.astype(BF16)
    class_packed_p = jnp.concatenate([class_packed] + [jnp.zeros((128 - classes, 3 * width), F32)], 0)
    qkv_acc[...] += dot(class_unit_t, class_packed_p.astype(BF16))
    packed_sum[:, :width] += jnp.sum(dquery_r.astype(F32), 0, keepdims=True)
    packed_sum[...] += jnp.sum(class_packed, 0, keepdims=True)

    @pl.when(cell == cells - 1)
    def _():
        first = 0

        def put(values):
            nonlocal first
            rows = values.shape[0]
            for start in range(0, values.shape[1], 128):
                slab[first : first + rows, :] = values[:, start : start + 128].astype(BF16)
                first += rows

        put(up_acc[...].T)
        put(g_down[...])
        put(g_out[...])
        put(qkv_acc[...])
        g_vec[...] = jnp.zeros_like(g_vec)
        line = 0
        for vector in (
            jnp.sum(up_bias_acc[...].T, 0, keepdims=True),
            jnp.sum(gain_acc[...].T, 0, keepdims=True),
            jnp.sum(bias_acc[...].T, 0, keepdims=True),
            down_bias_acc[...],
            packed_sum[...]
            + jnp.concatenate(
                [jnp.zeros((1, width), F32), jnp.sum(packed_cols[...].T, 0, keepdims=True)], 1
            ),
        ):
            for start in range(0, vector.shape[1], 128):
                g_vec[line : line + 1, :] = vector[:, start : start + 128]
                line += 1


def layer(
    counts, place, tables, x, xc, cot, cotc, w_out, gain, bias, w_up, b_up, w_down, b_down
):
    cells, genes, width = x.shape
    classes = xc.shape[1]
    total = tables[1].shape[1]
    head = width // HEADS
    ff = w_up.shape[1]
    stack = HEADS * classes
    slab_rows = (2 * ff + 4 * width) * width // 128
    whole = lambda shape: pl.BlockSpec(
        shape, lambda c, *_: (0,) * len(shape), pipeline_mode=pl.Buffered(1)
    )
    per_cell = lambda *shape: pl.BlockSpec((1,) + shape, lambda c, *_: (c,) + (0,) * len(shape))
    kept = lambda *shape: whole(shape)
    out = lambda shape, kind=BF16: jax.ShapeDtypeStruct(shape, kind)
    vmem = lambda *shape, kind=BF16: pltpu.VMEM(shape, kind)
    f32 = functools.partial(vmem, kind=F32)
    return pl.pallas_call(
        layer_kernel,
        grid_spec=pltpu.PrefetchScalarGridSpec(
            num_scalar_prefetch=2,
            grid=(cells,),
            in_specs=[
                per_cell(width, genes),
                per_cell(total, width),
                per_cell(HEADS, head + 16, total),
                per_cell(width, total),
                per_cell(2, 8, 128),
                per_cell(classes, 3 * width),
                per_cell(genes, width),
                per_cell(classes, width),
                per_cell(genes, width),
                per_cell(classes, width),
                whole((width, width)),
                whole((1, width)),
                whole((1, width)),
                whole((width, ff)),
                whole((1, ff)),
                whole((ff, width)),
                whole((1, width)),
            ],
            out_specs=[
                per_cell(genes, width),
                per_cell(classes, width),
                per_cell(genes, width),
                per_cell(classes, width),
                per_cell(total, 2 * width),
                per_cell(classes, 2 * width),
                per_cell(genes, width),
                per_cell(classes, width),
                kept(slab_rows, 128),
                kept(VECTOR_ROWS, 128),
            ],
            scratch_shapes=[
                vmem(width, width),
                vmem(ff, width),
                vmem(width, ff),
                f32(width, 128),
                f32(width, 128),
                f32(ff, 128),
                f32(width, 128),
                vmem(HEADS, genes, total),
                vmem(stack, genes),
                vmem(stack, total),
                f32(HEADS, head + 16, genes),
                f32(HEADS, 1, genes),
                f32(stack, 128),
                f32(HEADS, 1, genes),
                vmem(HEADS, 2 * head, genes),
                vmem(HEADS, genes, 2 * head),
                f32(HEADS, 1, genes),
                vmem(width, genes + 128),
                vmem(width, genes + 128),
                vmem(width, genes + 128),
                f32(genes, width),
                f32(ff, width),
                f32(ff, width),
                f32(width, width),
                f32(width, 3 * width),
                f32(ff, 128),
                f32(width, 128),
                f32(width, 128),
                f32(1, width),
                f32(1, 3 * width),
                f32(2 * width, 128),
            ],
        ),
        out_shape=[
            out((cells, genes, width)),
            out((cells, classes, width)),
            out((cells, genes, width)),
            out((cells, classes, width), F32),
            out((cells, total, 2 * width)),
            out((cells, classes, 2 * width), F32),
            out((cells, genes, width)),
            out((cells, classes, width), F32),
            out((slab_rows, 128)),
            out((VECTOR_ROWS, 128), F32),
        ],
        compiler_params=pltpu.CompilerParams(vmem_limit_bytes=VMEM),
        name="layer",
    )(counts, place, *tables, x, xc, cot, cotc, w_out, gain, bias, w_up, b_up, w_down, b_down)


def finish_kernel(
    orders,
    slab,
    vec,
    x,
    gm,
    dq,
    dkv,
    dkv_hbm,
    xc,
    gmc,
    dqc,
    dkvc,
    gain,
    bias,
    w,
    g_x,
    g_xc,
    slab_out,
    vec_out,
    w_t,
    work,
    summed,
    inbox,
    vec_in,
    other,
    other_c,
    send_sems,
    recv_sems,
    vec_send,
    vec_recv,
    swap_send,
    swap_recv,
    class_send,
    class_recv,
):
    step, steps = pl.program_id(0), pl.num_programs(0)
    cells = dkv_hbm.shape[0]
    genes = dkv_hbm.shape[1] // 2
    rows, width = x.shape[1:]
    classes = xc.shape[1]
    per_cell = genes // rows
    me, place = lax.axis_index("cell"), lax.axis_index("gene")
    bits = len(orders[0])
    part = slab.shape[0] // STREAMS
    half = part // 2
    mate = {"cell": me, "gene": 1 - place}

    def peer(bit):
        return {"cell": flip(me, 1 << bit), "gene": place}

    def remote(source, target, send, receive, device):
        return pltpu.make_async_remote_copy(
            src_ref=source,
            dst_ref=target,
            send_sem=send,
            recv_sem=receive,
            device_id=device,
            device_id_type=MESH,
        )

    def swap(cell):
        return remote(
            dkv_hbm.at[cell, pl.ds(genes, genes), :],
            other.at[cell],
            swap_send.at[cell],
            swap_recv.at[cell],
            mate,
        )

    def swap_class():
        return remote(dkvc, other_c, class_send, class_recv, mate)

    def low(stream, level):
        start, size = 0, half
        for i in range(level - 1):
            size = size // 2
            start = start + ((me // (1 << orders[stream][i])) % 2) * size
        return pl.multiple_of(start, 16) if level > 1 else start

    def length(level):
        return part >> level

    def box(level):
        return half - (half >> (level - 1)) + half if level else 0

    def gather(stream, level):
        sems = send_sems.at[stream, level], recv_sems.at[stream, level]
        if level == 0:
            source = slab.at[pl.ds(pl.multiple_of(stream * part + (1 - place) * half, 16), half), :]
            return remote(source, inbox.at[stream, pl.ds(0, half), :], *sems, mate)
        size = length(level + 1)
        bit = orders[stream][level - 1]
        away = 1 - (me // (1 << bit)) % 2
        start = pl.multiple_of(low(stream, level) + away * size, 16)
        return remote(
            work.at[stream, pl.ds(start, size), :],
            inbox.at[stream, pl.ds(box(level), size), :],
            *sems,
            peer(bit),
        )

    def add(stream, level):
        size = length(level + 1)
        if level == 0:
            mine = slab[pl.ds(pl.multiple_of(stream * part + place * half, 16), half), :]
            start = 0
        else:
            start = low(stream, level + 1)
            mine = work[stream, pl.ds(start, size), :]
        total = mine.astype(F32) + inbox[stream, pl.ds(box(level), size), :].astype(F32)
        total = total.astype(BF16)
        if level == bits:
            summed[pl.ds(pl.multiple_of(stream * part + place * half + start, 16), size), :] = total
        else:
            work[stream, pl.ds(start, size), :] = total

    def spread(stream, level):
        sems = send_sems.at[stream, 2 * bits + 1 - level], recv_sems.at[stream, 2 * bits + 1 - level]
        size = length(level + 1)
        start = low(stream, level + 1) if level else 0
        span = pl.ds(pl.multiple_of(stream * part + place * half + start, 16), size)
        device = peer(orders[stream][level - 1]) if level else mate
        return remote(summed.at[span, :], summed.at[span, :], *sems, device)

    def vector(level):
        device = peer(orders[0][level - 1]) if level else mate
        return remote(
            vec if level == 0 else vec_out,
            vec_in.at[level],
            vec_send.at[level],
            vec_recv.at[level],
            device,
        )

    def stage(index):
        if index > 0:
            if index - 1 <= bits:
                for stream in range(STREAMS):
                    gather(stream, index - 1).wait()
                    add(stream, index - 1)
                vector(index - 1).wait()
                before = vec[...] if index == 1 else vec_out[...]
                vec_out[...] = before + vec_in[index - 1]
            else:
                for stream in range(STREAMS):
                    spread(stream, 2 * bits + 2 - index).wait()
        if index <= bits:
            for stream in range(STREAMS):
                gather(stream, index).start()
            vector(index).start()
        elif index < 2 * bits + 2:
            for stream in range(STREAMS):
                spread(stream, 2 * bits + 1 - index).start()

    def rows_back(values, grads, packed):
        unit, inverse = norm_rows(values)
        scaled = dot(packed, w_t[...]) * gain[...]
        return grads + inverse * (
            scaled
            - jnp.mean(scaled, -1, keepdims=True)
            - unit * jnp.mean(scaled * unit, -1, keepdims=True)
        )

    stages = 2 * bits + 3
    last = cells * per_cell - 1
    for index in range(min(stages, last + 1)):

        @pl.when(step == index)
        def _(index=index):
            if index == 0:
                greet([mate] + [peer(bit) for bit in range(bits)])
            stage(index)
            if index == 0:
                for cell in range(cells):
                    swap(cell).start()
                swap_class().start()
                w_t[...] = w[...].T

    cell = step // per_cell

    @pl.when(step % per_cell == 0)
    def _():
        swap(cell).wait()

    grads = dkv[0].astype(F32) + other[
        cell, pl.ds(pl.multiple_of((step % per_cell) * rows, 16), rows), :
    ].astype(F32)
    packed = jnp.concatenate([dq[0], grads.astype(BF16)], 1)
    g_x[0] = rows_back(x[0].astype(F32), gm[0].astype(F32), packed).astype(BF16)

    @pl.when(step == steps - 1)
    def _():
        swap_class().wait()
        class_grads = dkvc[...] + other_c[...]
        stack = cells * classes
        packed = jnp.concatenate([dqc[...], class_grads], 2).reshape(stack, 3 * width)
        values = xc[...].astype(F32).reshape(stack, width)
        result = rows_back(values, gmc[...].reshape(stack, width), packed.astype(BF16))
        g_xc[...] = result.reshape(cells, classes, width).astype(BF16)
        for index in range(last + 1, stages):
            stage(index)
        slab_out[...] = summed[...]


def finish(orders, slab, vec, x, xc, gm, gmc, dq, dqc, dkv, dkvc, gain, bias, w):
    cells, genes, width = x.shape
    classes = xc.shape[1]
    rows = genes // 2
    per_cell = genes // rows
    bits = len(orders[0])
    part = slab.shape[0] // STREAMS
    whole = lambda array: pl.BlockSpec(array.shape, lambda i: (0,) * array.ndim)
    piece = lambda lanes: pl.BlockSpec((1, rows, lanes), lambda i: (i // per_cell, i % per_cell, 0))
    out = lambda shape, kind=BF16: jax.ShapeDtypeStruct(shape, kind)
    dma = lambda *shape: pltpu.SemaphoreType.DMA(shape)
    outs = [
        out((cells, genes, width)),
        out((cells, classes, width)),
        out(slab.shape),
        out(vec.shape, F32),
    ]
    return pl.pallas_call(
        functools.partial(finish_kernel, orders),
        grid=(cells * per_cell,),
        in_specs=[
            whole(slab),
            whole(vec),
            piece(width),
            piece(width),
            piece(width),
            piece(2 * width),
            pl.BlockSpec(memory_space=pl.ANY),
            whole(xc),
            whole(gmc),
            whole(dqc),
            whole(dkvc),
            whole(gain),
            whole(bias),
            whole(w),
        ],
        out_specs=[piece(width)] + [whole(o) for o in outs[1:]],
        out_shape=outs,
        scratch_shapes=[
            pltpu.VMEM((3 * width, width), BF16),
            pltpu.VMEM((STREAMS, part // 2, 128), BF16),
            pltpu.VMEM(slab.shape, BF16),
            pltpu.VMEM((STREAMS, part, 128), BF16),
            pltpu.VMEM((bits + 1,) + vec.shape, F32),
            pltpu.VMEM((cells, genes, 2 * width), BF16),
            pltpu.VMEM(dkvc.shape, F32),
            dma(STREAMS, 2 * bits + 2),
            dma(STREAMS, 2 * bits + 2),
            dma(bits + 1),
            dma(bits + 1),
            dma(cells),
            dma(cells),
            dma(),
            dma(),
        ],
        compiler_params=pltpu.CompilerParams(
            vmem_limit_bytes=VMEM, collective_id=1, has_side_effects=True
        ),
        name="finish",
    )(slab, vec, x, gm, dq, dkv, dkv, xc, gmc, dqc, dkvc, gain, bias, w)


def unpack_kernel(slab, vec, gain, bias, w, g_up, g_down, g_out, g_qkv, *vectors):
    width, ff = g_up.shape
    first = 0

    def take(target):
        nonlocal first
        rows = target.shape[0]
        for start in range(0, target.shape[1], 128):
            target[:, start : start + 128] = slab[first : first + rows, :].astype(F32)
            first += rows

    take(g_up)
    take(g_down)
    take(g_out)
    take(g_qkv)
    line = 0

    def lines(count):
        nonlocal line
        line += count
        return jnp.concatenate([vec[i : i + 1, :] for i in range(line - count, line)], 1)

    up_bias, ln2_gain, ln2_bias, down_bias, ln1_gain, ln1_bias = vectors
    up_bias[...] = lines(ff // 128)
    ln2_gain[...] = lines(width // 128)
    ln2_bias[...] = lines(width // 128)
    down_bias[...] = lines(width // 128)
    packed_sum = lines(3 * width // 128)
    weights = w[...].astype(F32)
    sums = g_qkv[...]
    ln1_gain[...] = jnp.sum((weights * sums).T, 0, keepdims=True)
    ln1_bias[...] = jnp.sum((weights * packed_sum).T, 0, keepdims=True)
    g_qkv[...] = (
        widen(spread_column(gain[...]), 3 * width) * sums
        + widen(spread_column(bias[...]), 3 * width) * packed_sum
    )


def unpack(slab, vec, gain, bias, w, ff):
    width = w.shape[0]
    out = lambda *shape: jax.ShapeDtypeStruct(shape, F32)
    row = out(1, width)
    return pl.pallas_call(
        unpack_kernel,
        out_shape=[
            out(width, ff),
            out(ff, width),
            out(width, width),
            out(width, 3 * width),
            out(1, ff),
            row,
            row,
            row,
            row,
            row,
        ],
        compiler_params=pltpu.CompilerParams(vmem_limit_bytes=VMEM),
        name="unpack",
    )(slab, vec, gain, bias, w)


def shards(
    gene_in,
    class_in,
    expressed,
    ln1_gain,
    ln1_bias,
    w_qkv,
    w_out,
    ln2_gain,
    ln2_bias,
    w_up,
    b_up,
    w_down,
    b_down,
    gene_cot,
    class_cot,
):
    row = lambda vector: vector.reshape(1, -1)
    place = lax.axis_index("gene").reshape(1)
    bits = (lax.axis_size("cell") - 1).bit_length()
    near = list(range(bits - 1))
    orders = [near[i % len(near) :] + near[: i % len(near)] + [bits - 1] for i in range(STREAMS)]
    gain1, bias1 = row(ln1_gain), row(ln1_bias)
    tables = project(expressed, gene_in, class_in, gain1, bias1, w_qkv)
    gene_out, class_out, dq, dqc, dkv, dkvc, gm, gmc, slab, vec = layer(
        expressed,
        place,
        tables,
        gene_in,
        class_in,
        gene_cot,
        class_cot,
        w_out,
        row(ln2_gain),
        row(ln2_bias),
        w_up,
        row(b_up),
        w_down,
        row(b_down),
    )
    gene_grad, class_grad, slab, vec = finish(
        orders, slab, vec, gene_in, class_in, gm, gmc, dq, dqc, dkv, dkvc, gain1, bias1, w_qkv
    )
    g_up, g_down, g_out, g_qkv, g_b_up, g_gain2, g_bias2, g_b_down, g_gain1, g_bias1 = unpack(
        slab, vec, gain1, bias1, w_qkv, w_up.shape[1]
    )
    return (
        gene_out,
        class_out,
        gene_grad,
        class_grad,
        g_gain1[0],
        g_bias1[0],
        g_qkv,
        g_out,
        g_gain2[0],
        g_bias2[0],
        g_up,
        g_b_up[0],
        g_down,
        g_b_down[0],
    )


def solution(mesh):
    genes, cells, whole = P("cell", "gene", None), P("cell", None, None), P()
    return jax.shard_map(
        shards,
        mesh=mesh,
        in_specs=(genes, cells, P("cell")) + (whole,) * 10 + (genes, cells),
        out_specs=(genes, cells, genes, cells) + (whole,) * 10,
        check_vma=False,
    )
```

```python
import functools

import jax
import jax.numpy as jnp
from jax import lax
from jax.experimental import pallas as pl
from jax.experimental.pallas import tpu as pltpu
from jax.sharding import PartitionSpec as P

HEADS = 4
EPS = 1e-05
LOG2E = 1.4426950408889634
SAFE = 40.0
KB = 256
FF_STEP = 512
MARKS = 3
VECTOR_ROWS = 32
VMEM = 63 * 2**20
F32 = jnp.float32
BF16 = jnp.bfloat16
MESH = pl.DeviceIdType.MESH


def dot(left, right):
    return jnp.dot(left, right, preferred_element_type=F32)


def dot_nt(left, right):
    return lax.dot_general(left, right, (((1,), (1,)), ((), ())), preferred_element_type=F32)


def dot_tn(left, right):
    return lax.dot_general(left, right, (((0,), (0,)), ((), ())), preferred_element_type=F32)


def spread_column(row):
    return jnp.broadcast_to(row, (128, row.shape[1])).T


def widen(column, lanes):
    return jnp.concatenate([column] * (lanes // 128), axis=1)


def fold_lanes(values):
    total = values[:, :128]
    for start in range(128, values.shape[1], 128):
        total = total + values[:, start : start + 128]
    return total


def norm_rows(values):
    centered = values - jnp.mean(values, -1, keepdims=True)
    inverse = lax.rsqrt(jnp.mean(centered * centered, -1, keepdims=True) + EPS)
    return centered * inverse, inverse


def norm_columns(values):
    scale = 1.0 / values.shape[0]
    centered = values - jnp.sum(values, 0, keepdims=True) * scale
    inverse = lax.rsqrt(jnp.sum(centered * centered, 0, keepdims=True) * scale + EPS)
    return centered * inverse, inverse


def greet(partners):
    barrier = pltpu.get_barrier_semaphore()
    for partner in partners:
        pl.semaphore_signal(barrier, inc=1, device_id=partner, device_id_type=MESH)
    pl.semaphore_wait(barrier, len(partners))


def project_kernel(
    counts,
    x,
    x_hbm,
    xc,
    gain,
    bias,
    w,
    qt,
    kr,
    va,
    ut,
    stat,
    pc,
    w_t,
    gain_c,
    bias_c,
    other,
    sent,
    received,
):
    cell, half = pl.program_id(0), pl.program_id(1)
    cells = x_hbm.shape[0]
    genes, width = x.shape[1:]
    head = width // HEADS
    place = lax.axis_index("gene")
    partner = {"cell": lax.axis_index("cell"), "gene": 1 - place}

    def swap(index):
        return pltpu.make_async_remote_copy(
            src_ref=x_hbm.at[index],
            dst_ref=other.at[index],
            send_sem=sent.at[index],
            recv_sem=received.at[index],
            device_id=partner,
            device_id_type=MESH,
        )

    @pl.when((cell == 0) & (half == 0))
    def _():
        greet([partner])
        for index in range(cells):
            swap(index).start()
        w_t[...] = w[...].T
        gain_c[...] = spread_column(gain[...])
        bias_c[...] = spread_column(bias[...])

    def norms(columns, first):
        for h in range(HEADS):
            part = columns[h * head : (h + 1) * head]
            size = jnp.sum(part * part, 0, keepdims=True)
            best = size[:, :128]
            for start in range(128, genes, 128):
                best = jnp.maximum(best, size[:, start : start + 128])
            stat[0, 0, first + h : first + h + 1, :] = best

    def tables(values, origin):
        unit, _ = norm_columns(values.T.astype(F32))
        ut[0] = unit.astype(BF16)
        low = unit * widen(gain_c[...], genes) + widen(bias_c[...], genes)
        spot = origin + lax.broadcasted_iota(jnp.int32, (1, genes), 1)
        valid = spot < counts[cell]
        kept = jnp.where(valid, low, 0.0).astype(BF16)
        packed_t = dot(w_t[width:, :], kept)
        mark = jnp.where(
            (lax.broadcasted_iota(jnp.int32, (16, genes), 0) < MARKS) & valid, 1.0, 0.0
        ).astype(BF16)
        for h in range(HEADS):
            va[0, h, :head, :] = packed_t[width + h * head : width + (h + 1) * head].astype(BF16)
            va[0, h, head:, :] = mark
        kr[0] = packed_t[:width].astype(BF16).T
        stat[...] = jnp.zeros_like(stat)
        norms(packed_t[:width], 0)
        return low

    @pl.when(half == 0)
    def _():
        low = tables(x[0], place * genes)
        query_t = dot(w_t[:width, :], low.astype(BF16)).astype(BF16) * (head**-0.5)
        qt[0] = query_t
        norms(query_t.astype(F32), HEADS)
        unit, _ = norm_rows(xc[0].astype(F32))
        class_low = (unit * gain[...] + bias[...]).astype(BF16)
        pc[0] = dot(class_low, w[...]).astype(BF16).astype(F32)

    @pl.when(half == 1)
    def _():
        swap(cell).wait_recv()
        tables(other[cell], (1 - place) * genes)

    @pl.when((cell == cells - 1) & (half == 1))
    def _():
        for index in range(cells):
            swap(index).wait_send()


def project(counts, x, xc, gain, bias, w):
    cells, genes, width = x.shape
    total = 2 * genes
    classes = xc.shape[1]
    head = width // HEADS
    whole = lambda shape: pl.BlockSpec(shape, lambda c, h: (0,) * len(shape))
    rows = pl.BlockSpec((1, genes, width), lambda c, h: (c, h, 0))
    columns = pl.BlockSpec((1, width, genes), lambda c, h: (c, 0, h))
    per_cell = lambda *shape: pl.BlockSpec((1,) + shape, lambda c, h: (c,) + (0,) * len(shape))
    out = lambda shape, kind=BF16: jax.ShapeDtypeStruct(shape, kind)
    return pl.pallas_call(
        project_kernel,
        grid=(cells, 2),
        in_specs=[
            pl.BlockSpec(memory_space=pltpu.SMEM),
            per_cell(genes, width),
            pl.BlockSpec(memory_space=pl.ANY),
            per_cell(classes, width),
            whole((1, width)),
            whole((1, width)),
            whole((width, 3 * width)),
        ],
        out_specs=[
            per_cell(width, genes),
            rows,
            pl.BlockSpec((1, HEADS, head + 16, genes), lambda c, h: (c, 0, 0, h)),
            columns,
            pl.BlockSpec((1, 1, 8, 128), lambda c, h: (c, h, 0, 0)),
            per_cell(classes, 3 * width),
        ],
        out_shape=[
            out((cells, width, genes)),
            out((cells, total, width)),
            out((cells, HEADS, head + 16, total)),
            out((cells, width, total)),
            out((cells, 2, 8, 128), F32),
            out((cells, classes, 3 * width), F32),
        ],
        scratch_shapes=[
            pltpu.VMEM((3 * width, width), BF16),
            pltpu.VMEM((width, 128), F32),
            pltpu.VMEM((width, 128), F32),
            pltpu.VMEM((cells, genes, width), BF16),
            pltpu.SemaphoreType.DMA((cells,)),
            pltpu.SemaphoreType.DMA((cells,)),
        ],
        compiler_params=pltpu.CompilerParams(
            vmem_limit_bytes=VMEM, collective_id=0, has_side_effects=True
        ),
        name="project",
    )(counts, x, x, xc, gain, bias, w)


def gelu_parts(u):
    phi = 0.5 + 0.5 * lax.erf(u * 0.7071067811865476)
    bell = jnp.exp2((u * u) * (-0.5 * LOG2E))
    return u * phi, phi + (u * 0.3989422804014327) * bell


def layer_kernel(
    counts,
    place,
    qt,
    kr,
    va,
    ut,
    stat,
    pc,
    x,
    xc,
    cot,
    cotc,
    w_out,
    gain,
    bias,
    w_up,
    b_up,
    w_down,
    b_down,
    y,
    yc,
    dq,
    dqc,
    dkv,
    dkvc,
    gm,
    gmc,
    slab,
    g_vec,
    w_out_t,
    w_up_t,
    w_down_t,
    gain_c,
    bias_c,
    b_up_c,
    b_down_c,
    probs,
    probs_ck,
    probs_cq,
    mix,
    shift,
    shift_q,
    inv_sum,
    qz,
    da,
    delta,
    att,
    datt,
    dq_t,
    up_acc,
    g_down,
    g_out,
    qkv_acc,
    up_bias_acc,
    gain_acc,
    bias_acc,
    down_bias_acc,
    packed_sum,
    packed_cols,
):
    cell = pl.program_id(0)
    cells = pl.num_programs(0)
    genes, width = x.shape[1:]
    classes = xc.shape[1]
    head = width // HEADS
    ff = w_up.shape[1]
    stack = HEADS * classes
    factor = head**-0.5
    count = counts[cell]
    own_count = jnp.clip(count - place[0] * genes, 0, genes)
    other_count = jnp.clip(count - (1 - place[0]) * genes, 0, genes)
    own_blocks = (own_count + (KB - 1)) // KB
    other_blocks = (other_count + (KB - 1)) // KB
    half_blocks = genes // KB
    blocks = own_blocks + other_blocks

    def nth_block(index):
        block = jnp.where(index < own_blocks, index, index - own_blocks + half_blocks)
        return pl.multiple_of(block * KB, KB)

    @pl.when(cell == 0)
    def _():
        w_out_t[...] = w_out[...].T
        w_up_t[...] = w_up[...].T
        w_down_t[...] = w_down[...].T
        gain_c[...] = spread_column(gain[...])
        bias_c[...] = spread_column(bias[...])
        b_up_c[...] = spread_column(b_up[...])
        b_down_c[...] = spread_column(b_down[...])
        up_acc[...] = jnp.zeros_like(up_acc)
        up_bias_acc[...] = jnp.zeros_like(up_bias_acc)
        gain_acc[...] = jnp.zeros_like(gain_acc)
        bias_acc[...] = jnp.zeros_like(bias_acc)
        down_bias_acc[...] = jnp.zeros_like(down_bias_acc)
        g_down[...] = jnp.zeros_like(g_down)
        g_out[...] = jnp.zeros_like(g_out)
        qkv_acc[...] = jnp.zeros_like(qkv_acc)
        packed_sum[...] = jnp.zeros_like(packed_sum)
        packed_cols[...] = jnp.zeros_like(packed_cols)

    head_mask = lax.broadcasted_iota(jnp.int32, (stack, width), 1) // head == (
        lax.broadcasted_iota(jnp.int32, (stack, width), 0) // classes
    )
    pair_mask = lax.broadcasted_iota(jnp.int32, (stack, stack), 1) // classes == (
        lax.broadcasted_iota(jnp.int32, (stack, stack), 0) // classes
    )

    def by_head(rows):
        return jnp.where(head_mask, jnp.concatenate([rows] * HEADS, 0), 0.0)

    def from_heads(rows):
        kept = jnp.where(head_mask, rows, 0.0)
        total = kept[:classes]
        for h in range(1, HEADS):
            total = total + kept[h * classes : (h + 1) * classes]
        return total

    packed_c = pc[0]
    query_c = by_head(packed_c[:, :width] * factor)
    key_c = by_head(packed_c[:, width : 2 * width])
    value_c = by_head(packed_c[:, 2 * width :])
    key_c_t = key_c.T.astype(BF16)
    value_c_t = value_c.T.astype(BF16)
    query_cb, key_cb, value_cb = query_c.astype(BF16), key_c.astype(BF16), value_c.astype(BF16)

    half_rows = lax.broadcasted_iota(jnp.int32, (2 * head, genes), 0) // head
    for h in range(HEADS):
        pair = slice((h // 2) * 2 * head, (h // 2 + 1) * 2 * head)
        qz[h] = jnp.where(half_rows == h % 2, qt[0, pair, :].astype(F32), 0.0).astype(BF16)

    size_k = jnp.max(jnp.maximum(stat[0, 0, :HEADS], stat[0, 1, :HEADS]))
    size_q = jnp.max(jnp.maximum(stat[0, 0, HEADS:], stat[0, 1, HEADS:]))
    size_k = jnp.maximum(size_k, jnp.max(jnp.sum(key_c * key_c, -1, keepdims=True)))
    size_q = jnp.maximum(size_q, jnp.max(jnp.sum(query_c * query_c, -1, keepdims=True)))
    safe = size_k * size_q < SAFE * SAFE

    def key_mask(start, shape, axis):
        limit = jnp.where(start < genes, own_count, genes + other_count)
        return start + lax.broadcasted_iota(jnp.int32, shape, axis) < limit

    shift[...] = jnp.zeros_like(shift)
    shift_q[...] = jnp.zeros_like(shift_q)

    @pl.when(jnp.logical_not(safe))
    def _():
        class_scores = dot(key_cb, qt[0])
        for h in range(HEADS):
            shift[h] = jnp.max(class_scores[h * classes : (h + 1) * classes], 0, keepdims=True)
        own_scores = jnp.where(pair_mask, dot(query_cb, key_c_t), -1e30)
        shift_q[...] = jnp.broadcast_to(jnp.max(own_scores, -1, keepdims=True), shift_q.shape)

        @pl.loop(0, blocks)
        def _(block):
            start = nth_block(block)
            for h in range(HEADS):
                scores = dot(
                    kr[0, pl.ds(start, KB), (h // 2) * 2 * head : (h // 2 + 1) * 2 * head], qz[h]
                )
                scores = jnp.where(key_mask(start, scores.shape, 0), scores, -1e30)
                shift[h] = jnp.maximum(shift[h], jnp.max(scores, 0, keepdims=True))
            scores = dot_nt(query_cb, kr[0, pl.ds(start, KB), :])
            scores = jnp.where(key_mask(start, scores.shape, 1), scores, -1e30)
            shift_q[...] = jnp.maximum(shift_q[...], jnp.max(scores, -1, keepdims=True))

        shift[...] = shift[...] * LOG2E
        shift_q[...] = shift_q[...] * LOG2E

    class_scores = dot(key_cb, qt[0])
    shift_rows = jnp.concatenate(
        [jnp.broadcast_to(shift[h], (classes, genes)) for h in range(HEADS)], 0
    )
    class_exp = jnp.exp2(class_scores * LOG2E - shift_rows).astype(BF16)
    probs_ck[...] = class_exp
    class_mix = dot(value_c_t, class_exp)
    for h in range(HEADS):
        mix[h, :head, :] = class_mix[h * head : (h + 1) * head]
        sums = jnp.sum(
            class_exp[h * classes : (h + 1) * classes].astype(F32), 0, keepdims=True
        )
        mix[h, head:, :] = jnp.where(
            lax.broadcasted_iota(jnp.int32, (16, genes), 0) == 0, sums, 0.0
        )
    shift_qc = shift_q[:, :1]
    own_exp = jnp.where(
        pair_mask, jnp.exp2(dot(query_cb, key_c_t) * LOG2E - shift_qc), 0.0
    ).astype(BF16)
    deep = head + 16

    def spread_heads(rows, extra):
        pieces = []
        for h in range(HEADS):
            pieces += [rows[:, h * head : (h + 1) * head], extra]
        return jnp.concatenate(pieces, 1)

    own_mix = spread_heads(
        dot(own_exp, value_cb),
        jnp.broadcast_to(jnp.sum(own_exp.astype(F32), -1, keepdims=True), (stack, 16)),
    )

    def forward_block(block, class_total, shifted):
        start = nth_block(block)
        keys = pl.ds(start, KB)
        scores = [
            dot(kr[0, keys, (h // 2) * 2 * head : (h // 2 + 1) * 2 * head], qz[h])
            for h in range(1)
        ]
        class_scores = dot_nt(query_cb, kr[0, keys, :]) * LOG2E - shift_qc
        for h in range(HEADS):
            if h + 1 < HEADS:
                g = h + 1
                scores.append(
                    dot(kr[0, keys, (g // 2) * 2 * head : (g // 2 + 1) * 2 * head], qz[g])
                )
            scaled = scores[h] * LOG2E
            if shifted:
                scaled = jnp.minimum(scaled - shift[h], 60.0)
            exps = jnp.exp2(scaled).astype(BF16)
            mix[h] += dot(va[0, h, :, keys], exps)
            probs[h, :, keys] = exps.T
        class_exp = jnp.where(
            key_mask(start, class_scores.shape, 1), jnp.exp2(class_scores), 0.0
        ).astype(BF16)
        probs_cq[:, keys] = class_exp
        return class_total + dot_nt(class_exp, va[0, :, :, keys].reshape(HEADS * deep, KB))

    class_total = lax.cond(
        safe,
        lambda: lax.fori_loop(0, blocks, functools.partial(forward_block, shifted=False), own_mix),
        lambda: lax.fori_loop(0, blocks, functools.partial(forward_block, shifted=True), own_mix),
    )
    class_sum = jnp.concatenate(
        [
            class_total[h * classes : (h + 1) * classes, h * deep + head : h * deep + head + 1]
            for h in range(HEADS)
        ],
        0,
    )
    class_total = jnp.concatenate(
        [class_total[:, h * deep : h * deep + head] for h in range(HEADS)], 1
    )
    class_inv = 1.0 / class_sum
    class_att = from_heads(class_total * class_inv)
    for h in range(HEADS):
        inverse = 1.0 / mix[h, head : head + 1, :]
        inv_sum[h] = inverse
        att[h * head : (h + 1) * head, :genes] = (mix[h, :head, :] * inverse).astype(BF16)

    def pad_rows(rows):
        return jnp.concatenate([rows, jnp.zeros((128 - rows.shape[0], width), F32)], 0)

    att[:, genes:] = pad_rows(class_att).T.astype(BF16)

    def feed(start, columns, with_class):
        lanes = columns + (128 if with_class else 0)
        span = pl.ds(start, lanes)
        wide_gain, wide_bias = widen(gain_c[...], lanes), widen(bias_c[...], lanes)
        cot_r = cot[0, pl.ds(start, columns), :]
        cot_t = cot_r.T
        x_t = x[0, pl.ds(start, columns), :].T
        if with_class:
            x_t = jnp.concatenate([x_t, pad_rows(xc[0].astype(F32)).T.astype(BF16)], 1)
            padded = pad_rows(cotc[0].astype(F32))
            cot_t = jnp.concatenate([cot_t, padded.T.astype(BF16)], 1)
            cot_r = jnp.concatenate([cot_r, (padded * 0.5).astype(BF16)], 0)
            share = jnp.where(
                lax.broadcasted_iota(jnp.int32, (1, lanes), 1) < columns, 1.0, 0.5
            )
            weigh = lambda values: values * share
            row_share = jnp.where(
                lax.broadcasted_iota(jnp.int32, (lanes, 1), 0) < columns, 1.0, 0.5
            )
            weigh_rows = lambda rows: (rows.astype(F32) * row_share).astype(BF16)
        else:
            weigh = lambda values: values
            weigh_rows = lambda rows: rows
        att_low = att[:, span]
        middle = x_t.astype(F32) + dot(w_out_t[...], att_low)
        unit, inverse = norm_columns(middle)
        low = (unit * wide_gain + wide_bias).astype(BF16)
        low_r = weigh_rows(low.T)
        result = middle + widen(b_down_c[...], lanes)
        back = jnp.zeros((width, lanes), F32)
        for first in range(0, ff, FF_STEP):
            part = slice(first, first + FF_STEP)
            up = dot(w_up_t[part, :], low) + widen(b_up_c[part, :], lanes)
            grad_act = dot(w_down[part, :], cot_t)
            active, slope = gelu_parts(up)
            active = active.astype(BF16)
            grad_up = slope * grad_act
            up_bias_acc[part, :] += fold_lanes(weigh(grad_up))
            grad_up = grad_up.astype(BF16)
            result += dot(w_down_t[:, part], active)
            back += dot(w_up[:, part], grad_up)
            g_down[part, :] += dot(active, cot_r)
            up_acc[part, :] += dot(grad_up, low_r)
        scaled = back * wide_gain
        scale = 1.0 / width
        grad_middle = cot_t.astype(F32) + inverse * (
            scaled
            - jnp.sum(scaled, 0, keepdims=True) * scale
            - unit * (jnp.sum(scaled * unit, 0, keepdims=True) * scale)
        )
        grad_middle = grad_middle.astype(BF16)
        datt[:, span] = dot(w_out[...], grad_middle).astype(BF16)
        gain_acc[...] += fold_lanes(weigh(back * unit))
        bias_acc[...] += fold_lanes(weigh(back))
        middle_r = grad_middle.T
        g_out[...] += dot(att_low, weigh_rows(middle_r))
        cot_sum = jnp.sum(cot_r.astype(F32), 0, keepdims=True)
        down_bias_acc[...] += cot_sum
        result_r = result.T
        y[0, pl.ds(start, columns), :] = result_r[:columns].astype(BF16)
        gm[0, pl.ds(start, columns), :] = middle_r[:columns]
        if with_class:
            yc[0] = result_r[columns : columns + classes].astype(BF16)
            gmc[0] = middle_r[columns:].astype(F32)[:classes]

    feed_step = 512
    pieces = genes // feed_step

    @pl.loop(0, pieces - 1)
    def _(piece):
        feed(pl.multiple_of(piece * feed_step, feed_step), feed_step, False)

    feed((pieces - 1) * feed_step, feed_step, True)

    for h in range(HEADS):
        own = slice(h * head, (h + 1) * head)
        inverse = inv_sum[h]
        grad = (datt[own, :genes].astype(F32) * inverse).astype(BF16)
        row_delta = jnp.sum(grad.astype(F32) * (mix[h, :head, :] * inverse), 0, keepdims=True)
        delta[h] = row_delta
        datt[own, :genes] = grad
        parts = jnp.zeros((16, genes), F32)
        rest = row_delta
        for i in range(MARKS):
            piece = rest.astype(BF16).astype(F32)
            rest = rest - piece
            parts = jnp.where(
                lax.broadcasted_iota(jnp.int32, (16, genes), 0) == i, -piece, parts
            )
        blank = jnp.zeros((2 * head - deep, genes), BF16)
        da[h] = jnp.concatenate([grad, parts.astype(BF16), blank], 0).T

    class_grad = datt[:, genes:].astype(F32).T[:classes]
    class_grad = by_head(class_grad) * class_inv
    class_grad_b = class_grad.astype(BF16)
    class_grad_h = (class_grad * 0.5).astype(BF16)
    query_ch = (query_c * 0.5).astype(BF16)
    class_delta = jnp.sum(
        class_grad_b.astype(F32) * (class_total * class_inv), -1, keepdims=True
    )

    class_dprob = dot(value_cb, datt[:, :genes])
    delta_rows = jnp.concatenate(
        [jnp.broadcast_to(delta[h], (classes, genes)) for h in range(HEADS)], 0
    )
    class_probs = probs_ck[...]
    class_dscore = (class_probs.astype(F32) * (class_dprob - delta_rows)).astype(BF16)
    dq_t[...] = dot(key_c_t, class_dscore)
    class_dkey = dot_nt(class_dscore, qt[0])
    class_dvalue = dot_nt(class_probs, datt[:, :genes])
    own_dprob = dot(class_grad_b, value_c_t)
    own_dscore = (own_exp.astype(F32) * (own_dprob - class_delta)).astype(BF16)
    class_dquery = dot(own_dscore, key_cb)
    class_dkey = class_dkey + dot(own_dscore.astype(F32).T.astype(BF16), query_ch)
    class_dvalue = class_dvalue + dot(own_exp.astype(F32).T.astype(BF16), class_grad_h)

    class_grad_s = spread_heads(class_grad_b, jnp.zeros((stack, 16), BF16))
    class_grad_ht = class_grad_h.T
    query_ct = query_ch.T

    def backward_block(block, class_dquery):
        start = nth_block(block)
        keys = pl.ds(start, KB)
        dprobs = [dot(da[0, :, :deep], va[0, 0, :, keys])]
        class_weights = probs_cq[:, keys]
        class_dprob = dot(class_grad_s, va[0, :, :, keys].reshape(HEADS * deep, KB))
        class_dscore = (class_weights.astype(F32) * (class_dprob - class_delta)).astype(BF16)
        dkeys, dvalues = [], []
        key_t = kr[0, keys, :].T
        for h in range(HEADS):
            if h + 1 < HEADS:
                dprobs.append(dot(da[h + 1, :, :deep], va[0, h + 1, :, keys]))
            weights = probs[h, :, keys]
            dscore = weights * dprobs[h].astype(BF16)
            own = slice(h * head, (h + 1) * head)
            dvalues.append(dot(datt[own, :genes], weights))
            dkeys.append(dot(qt[0, own, :], dscore))
            spot = slice(h % 2 * 2, h % 2 * 2 + 2)
            qz[spot] = dscore.T.reshape(2, KB // 2, genes)
            dq_t[own, :] += dot(key_t[own, :], qz[spot].reshape(KB, genes))
        dkey = jnp.concatenate(dkeys, 0) + dot(query_ct, class_dscore)
        dvalue = jnp.concatenate(dvalues, 0) + dot(class_grad_ht, class_weights)
        valid = key_mask(start, (1, KB), 1)
        grads = jnp.where(valid, jnp.concatenate([dkey, dvalue], 0), 0.0)
        packed_cols[...] += fold_lanes(grads)
        grads = grads.astype(BF16).T
        dkv[0, keys, :] = grads
        qkv_acc[:, width:] += dot(ut[0, :, keys], grads)
        return class_dquery + dot(class_dscore, kr[0, keys, :])

    class_dquery = lax.fori_loop(0, blocks, backward_block, class_dquery)

    def blank_rows(block):
        dkv[0, pl.ds(pl.multiple_of(block * KB, KB), KB), :] = jnp.zeros((KB, 2 * width), BF16)

    pl.loop(own_blocks, half_blocks)(blank_rows)
    pl.loop(half_blocks + other_blocks, 2 * half_blocks)(blank_rows)

    dquery_r = (dq_t[...] * factor).astype(BF16).T
    dq[0] = dquery_r
    qkv_acc[:, :width] += dot(ut[0, :, :genes], dquery_r)
    class_dquery = from_heads(class_dquery) * factor
    class_dkv = jnp.concatenate([from_heads(class_dkey), from_heads(class_dvalue)], 1)
    dqc[0] = class_dquery
    dkvc[0] = class_dkv
    class_packed = jnp.concatenate([class_dquery * 0.5, class_dkv], 1)
    class_unit, _ = norm_rows(xc[0].astype(F32))
    pad = jnp.zeros((128 - classes, width), F32)
    class_unit_t = jnp.concatenate([class_unit, pad], 0).T.astype(BF16)
    class_packed_p = jnp.concatenate([class_packed] + [jnp.zeros((128 - classes, 3 * width), F32)], 0)
    qkv_acc[...] += dot(class_unit_t, class_packed_p.astype(BF16))
    packed_sum[:, :width] += jnp.sum(dquery_r.astype(F32), 0, keepdims=True)
    packed_sum[...] += jnp.sum(class_packed, 0, keepdims=True)

    @pl.when(cell == cells - 1)
    def _():
        first = 0

        def put(values):
            nonlocal first
            rows = values.shape[0]
            for start in range(0, values.shape[1], 128):
                slab[first : first + rows, :] = values[:, start : start + 128].astype(BF16)
                first += rows

        put(up_acc[...].T)
        put(g_down[...])
        put(g_out[...])
        put(qkv_acc[...])
        if first < slab.shape[0]:
            slab[first:, :] = jnp.zeros((slab.shape[0] - first, 128), BF16)
        g_vec[...] = jnp.zeros_like(g_vec)
        line = 0
        for vector in (
            jnp.sum(up_bias_acc[...].T, 0, keepdims=True),
            jnp.sum(gain_acc[...].T, 0, keepdims=True),
            jnp.sum(bias_acc[...].T, 0, keepdims=True),
            down_bias_acc[...],
            packed_sum[...]
            + jnp.concatenate(
                [jnp.zeros((1, width), F32), jnp.sum(packed_cols[...].T, 0, keepdims=True)], 1
            ),
        ):
            for start in range(0, vector.shape[1], 128):
                g_vec[line : line + 1, :] = vector[:, start : start + 128]
                line += 1


def layer(
    counts, place, tables, x, xc, cot, cotc, w_out, gain, bias, w_up, b_up, w_down, b_down
):
    cells, genes, width = x.shape
    classes = xc.shape[1]
    total = tables[1].shape[1]
    head = width // HEADS
    ff = w_up.shape[1]
    stack = HEADS * classes
    slab_rows = Reduction.padded((2 * ff + 4 * width) * width // 128, lax.axis_size("cell"))
    whole = lambda shape: pl.BlockSpec(
        shape, lambda c, *_: (0,) * len(shape), pipeline_mode=pl.Buffered(1)
    )
    per_cell = lambda *shape: pl.BlockSpec((1,) + shape, lambda c, *_: (c,) + (0,) * len(shape))
    kept = lambda *shape: whole(shape)
    out = lambda shape, kind=BF16: jax.ShapeDtypeStruct(shape, kind)
    vmem = lambda *shape, kind=BF16: pltpu.VMEM(shape, kind)
    f32 = functools.partial(vmem, kind=F32)
    return pl.pallas_call(
        layer_kernel,
        grid_spec=pltpu.PrefetchScalarGridSpec(
            num_scalar_prefetch=2,
            grid=(cells,),
            in_specs=[
                per_cell(width, genes),
                per_cell(total, width),
                per_cell(HEADS, head + 16, total),
                per_cell(width, total),
                per_cell(2, 8, 128),
                per_cell(classes, 3 * width),
                per_cell(genes, width),
                per_cell(classes, width),
                per_cell(genes, width),
                per_cell(classes, width),
                whole((width, width)),
                whole((1, width)),
                whole((1, width)),
                whole((width, ff)),
                whole((1, ff)),
                whole((ff, width)),
                whole((1, width)),
            ],
            out_specs=[
                per_cell(genes, width),
                per_cell(classes, width),
                per_cell(genes, width),
                per_cell(classes, width),
                per_cell(total, 2 * width),
                per_cell(classes, 2 * width),
                per_cell(genes, width),
                per_cell(classes, width),
                kept(slab_rows, 128),
                kept(VECTOR_ROWS, 128),
            ],
            scratch_shapes=[
                vmem(width, width),
                vmem(ff, width),
                vmem(width, ff),
                f32(width, 128),
                f32(width, 128),
                f32(ff, 128),
                f32(width, 128),
                vmem(HEADS, genes, total),
                vmem(stack, genes),
                vmem(stack, total),
                f32(HEADS, head + 16, genes),
                f32(HEADS, 1, genes),
                f32(stack, 128),
                f32(HEADS, 1, genes),
                vmem(HEADS, 2 * head, genes),
                vmem(HEADS, genes, 2 * head),
                f32(HEADS, 1, genes),
                vmem(width, genes + 128),
                vmem(width, genes + 128),
                f32(width, genes),
                f32(ff, width),
                f32(ff, width),
                f32(width, width),
                f32(width, 3 * width),
                f32(ff, 128),
                f32(width, 128),
                f32(width, 128),
                f32(1, width),
                f32(1, 3 * width),
                f32(2 * width, 128),
            ],
        ),
        out_shape=[
            out((cells, genes, width)),
            out((cells, classes, width)),
            out((cells, genes, width)),
            out((cells, classes, width), F32),
            out((cells, total, 2 * width)),
            out((cells, classes, 2 * width), F32),
            out((cells, genes, width)),
            out((cells, classes, width), F32),
            out((slab_rows, 128)),
            out((VECTOR_ROWS, 128), F32),
        ],
        compiler_params=pltpu.CompilerParams(vmem_limit_bytes=VMEM),
        name="layer",
    )(counts, place, *tables, x, xc, cot, cotc, w_out, gain, bias, w_up, b_up, w_down, b_down)


class Reduction:
    @staticmethod
    def groups(cells):
        bits = (cells - 1).bit_length()
        return [(shift, min(2, bits - shift)) for shift in range(0, bits, 2)]

    @staticmethod
    def streams(rows, cells):
        groups = Reduction.groups(cells)
        unit = 2 * 16 * cells
        units = -(-rows // unit)
        count = min(len(groups), units)
        shares = [units // count] * count
        if count == 2:
            shares[1] = max(1, units // 3)
        shares[0] = units - sum(shares[1:])
        result, first = [], 0
        for i, share in enumerate(shares):
            result.append((first, share * unit, groups[i:] + groups[:i]))
            first += share * unit
        return result

    @staticmethod
    def padded(rows, cells):
        first, size, _ = Reduction.streams(rows, cells)[-1]
        return first + size

    @staticmethod
    def scratch(rows, cells):
        rows = Reduction.padded(rows, cells)
        hops = 2 + 2 * sum((1 << bits) - 1 for _, bits in Reduction.groups(cells))
        sems = (len(Reduction.streams(rows, cells)), hops)
        return [
            pltpu.VMEM((rows // 2, 128), BF16),
            pltpu.VMEM((rows, 128), BF16),
            pltpu.VMEM((rows, 128), BF16),
            pltpu.SemaphoreType.DMA(sems),
            pltpu.SemaphoreType.DMA(sems),
        ]

    def __init__(self, source, cells, work, inbox, total, sent, received):
        self.source, self.work, self.inbox, self.total = source, work, inbox, total
        self.sent, self.received = sent, received
        self.plan = self.streams(source.shape[0], cells)
        self.depth = len(self.groups(cells))
        self.stages = 2 * self.depth + 3
        self.me, self.place = lax.axis_index("cell"), lax.axis_index("gene")

    def peer(self, group, ahead):
        shift, bits = group
        radix = 1 << bits
        digit = (self.me // (1 << shift)) % radix
        there = (digit + ahead) % radix
        return {"cell": self.me + (there - digit) * (1 << shift), "gene": self.place}, there

    def digit(self, group):
        return (self.me // (1 << group[0])) % (1 << group[1])

    def held(self, stream, level):
        _, rows, order = self.plan[stream]
        first, size = 0, rows // 2
        for group in order[:level]:
            size = size >> group[1]
            first = first + self.digit(group) * size
        return first, size

    def slot(self, stream, level):
        first, rows, order = self.plan[stream]
        size = rows // 2
        spot = first
        for i in range(level):
            spot += size if i == 0 else ((1 << order[i - 1][1]) - 1) * size
            size = size >> order[i][1] if i < len(order) else size
        return spot

    def copy(self, source, target, stream, hop, ahead, device):
        return pltpu.make_async_remote_copy(
            src_ref=source,
            dst_ref=target,
            send_sem=self.sent.at[stream, hop + ahead - 1],
            recv_sem=self.received.at[stream, hop + ahead - 1],
            device_id=device,
            device_id_type=MESH,
        )

    def hop(self, stream, index):
        peers = [1] + [(1 << bits) - 1 for _, bits in self.plan[stream][2]]
        return sum((peers + peers[::-1])[:index])

    def rows(self, first, size):
        return pl.ds(pl.multiple_of(first, 16), size)

    def scatter(self, stream, level):
        first, rows, order = self.plan[stream]
        half = rows // 2
        if level == 0:
            mate = {"cell": self.me, "gene": 1 - self.place}
            source = self.source.at[self.rows(first + (1 - self.place) * half, half), :]
            target = self.inbox.at[pl.ds(first, half), :]
            return [self.copy(source, target, stream, 0, 1, mate)]
        group = order[level - 1]
        start, size = self.held(stream, level - 1)
        size = size >> group[1]
        copies = []
        for ahead in range(1, 1 << group[1]):
            device, there = self.peer(group, ahead)
            source = self.work.at[self.rows(first // 2 + start + there * size, size), :]
            target = self.inbox.at[pl.ds(self.slot(stream, level) + (ahead - 1) * size, size), :]
            copies.append(self.copy(source, target, stream, self.hop(stream, level), ahead, device))
        return copies

    def add(self, stream, level):
        first, rows, order = self.plan[stream]
        half = rows // 2
        start, size = self.held(stream, level)
        if level == 0:
            value = self.source[self.rows(first + self.place * half, half), :].astype(F32)
            count = 1
        else:
            value = self.work[self.rows(first // 2 + start, size), :].astype(F32)
            count = (1 << order[level - 1][1]) - 1
        for i in range(count):
            value += self.inbox[pl.ds(self.slot(stream, level) + i * size, size), :].astype(F32)
        if level == self.depth:
            self.total[self.rows(first + self.place * half + start, size), :] = value.astype(BF16)
        else:
            self.work[self.rows(first // 2 + start, size), :] = value.astype(BF16)

    def gather(self, stream, level):
        first, rows, order = self.plan[stream]
        half = rows // 2
        start, size = self.held(stream, level)
        span = self.total.at[self.rows(first + self.place * half + start, size), :]
        hop = self.hop(stream, 2 * self.depth + 1 - level)
        if level == 0:
            mate = {"cell": self.me, "gene": 1 - self.place}
            return [self.copy(span, span, stream, hop, 1, mate)]
        group = order[level - 1]
        return [
            self.copy(span, span, stream, hop, ahead, self.peer(group, ahead)[0])
            for ahead in range(1, 1 << group[1])
        ]

    def copies(self, stream, index):
        if index <= self.depth:
            return self.scatter(stream, index)
        return self.gather(stream, 2 * self.depth + 1 - index)

    def stage(self, index):
        if index > 0:
            for stream in range(len(self.plan)):
                for copy in self.copies(stream, index - 1):
                    copy.wait()
                if index - 1 <= self.depth:
                    self.add(stream, index - 1)
        if index < self.stages - 1:
            for stream in range(len(self.plan)):
                for copy in self.copies(stream, index):
                    copy.start()


class VectorSum:
    @staticmethod
    def scratch(shape, cells):
        groups = Reduction.groups(cells)
        return [
            pltpu.VMEM((2 + sum(1 << bits for _, bits in groups),) + shape, F32),
            pltpu.SemaphoreType.DMA((len(groups) + 1, 3)),
            pltpu.SemaphoreType.DMA((len(groups) + 1, 3)),
        ]

    def __init__(self, cells, reduction, slots, sent, received):
        self.reduction, self.slots, self.sent, self.received = reduction, slots, sent, received
        self.groups = reduction.groups(cells)

    def first(self, level):
        return 0 if level == 0 else 2 + sum(1 << bits for _, bits in self.groups[: level - 1])

    def size(self, level):
        return 2 if level == 0 else 1 << self.groups[level - 1][1]

    def copies(self, level):
        r = self.reduction
        if level == 0:
            mine = r.place
            devices = [{"cell": r.me, "gene": 1 - r.place}]
        else:
            group = self.groups[level - 1]
            mine = r.digit(group)
            devices = [r.peer(group, ahead)[0] for ahead in range(1, self.size(level))]
        spot = self.slots.at[self.first(level) + mine]
        return mine, [
            pltpu.make_async_remote_copy(
                src_ref=spot,
                dst_ref=spot,
                send_sem=self.sent.at[level, i],
                recv_sem=self.received.at[level, i],
                device_id=device,
                device_id_type=MESH,
            )
            for i, device in enumerate(devices)
        ]

    def start(self, level, value):
        mine, copies = self.copies(level)
        self.slots[self.first(level) + mine] = value
        for copy in copies:
            copy.start()

    def finish(self, level):
        for copy in self.copies(level)[1]:
            copy.wait()
        first = self.first(level)
        total = self.slots[first]
        for i in range(1, self.size(level)):
            total = total + self.slots[first + i]
        return total

    def stage(self, index, value):
        levels = len(self.groups)
        if 0 < index <= levels + 1:
            value = self.finish(index - 1)
        if index <= levels:
            self.start(index, value)
        return value if index == levels + 1 else None


def finish_kernel(
    slab,
    vec,
    x,
    gm,
    dq,
    dkv,
    dkv_hbm,
    xc,
    gmc,
    dqc,
    dkvc,
    gain,
    bias,
    w,
    g_x,
    g_xc,
    slab_out,
    vec_out,
    w_t,
    other,
    other_c,
    swap_send,
    swap_recv,
    class_send,
    class_recv,
    *reduction_scratch,
):
    step, steps = pl.program_id(0), pl.num_programs(0)
    cells = dkv_hbm.shape[0]
    genes = dkv_hbm.shape[1] // 2
    rows, width = x.shape[1:]
    classes = xc.shape[1]
    per_cell = genes // rows
    all_cells = lax.axis_size("cell")
    sums = Reduction(slab, all_cells, *reduction_scratch[:5])
    vectors = VectorSum(all_cells, sums, *reduction_scratch[5:])
    mate = {"cell": sums.me, "gene": 1 - sums.place}

    def swap(cell):
        return pltpu.make_async_remote_copy(
            src_ref=dkv_hbm.at[cell, pl.ds(genes, genes), :],
            dst_ref=other.at[cell],
            send_sem=swap_send.at[cell],
            recv_sem=swap_recv.at[cell],
            device_id=mate,
            device_id_type=MESH,
        )

    def swap_class():
        return pltpu.make_async_remote_copy(
            src_ref=dkvc,
            dst_ref=other_c,
            send_sem=class_send,
            recv_sem=class_recv,
            device_id=mate,
            device_id_type=MESH,
        )

    def stage(index):
        sums.stage(index)
        done = vectors.stage(index, vec[...] if index == 0 else None)
        if done is not None:
            vec_out[...] = done

    def rows_back(values, grads, packed):
        unit, inverse = norm_rows(values)
        scaled = dot(packed, w_t[...]) * gain[...]
        return grads + inverse * (
            scaled
            - jnp.mean(scaled, -1, keepdims=True)
            - unit * jnp.mean(scaled * unit, -1, keepdims=True)
        )

    last = cells * per_cell - 1
    for index in range(min(sums.stages, last + 1)):

        @pl.when(step == index)
        def _(index=index):
            if index == 0:
                partners = [mate]
                for group in sums.groups(all_cells):
                    for ahead in range(1, 1 << group[1]):
                        partners.append(sums.peer(group, ahead)[0])
                greet(partners)
            stage(index)
            if index == 0:
                for cell in range(cells):
                    swap(cell).start()
                swap_class().start()
                w_t[...] = w[...].T

    cell = step // per_cell

    @pl.when(step % per_cell == 0)
    def _():
        swap(cell).wait()

    grads = dkv[0].astype(F32) + other[
        cell, pl.ds(pl.multiple_of((step % per_cell) * rows, 16), rows), :
    ].astype(F32)
    packed = jnp.concatenate([dq[0], grads.astype(BF16)], 1)
    g_x[0] = rows_back(x[0].astype(F32), gm[0].astype(F32), packed).astype(BF16)

    @pl.when(step == steps - 1)
    def _():
        swap_class().wait()
        class_grads = dkvc[...] + other_c[...]
        stack = cells * classes
        packed = jnp.concatenate([dqc[...], class_grads], 2).reshape(stack, 3 * width)
        values = xc[...].astype(F32).reshape(stack, width)
        result = rows_back(values, gmc[...].reshape(stack, width), packed.astype(BF16))
        g_xc[...] = result.reshape(cells, classes, width)
        for index in range(last + 1, sums.stages):
            stage(index)
        slab_out[...] = sums.total[...]


def finish(slab, vec, x, xc, gm, gmc, dq, dqc, dkv, dkvc, gain, bias, w):
    cells, genes, width = x.shape
    classes = xc.shape[1]
    rows = genes // 2
    per_cell = genes // rows
    all_cells = lax.axis_size("cell")
    whole = lambda array: pl.BlockSpec(array.shape, lambda i: (0,) * array.ndim)
    piece = lambda lanes: pl.BlockSpec((1, rows, lanes), lambda i: (i // per_cell, i % per_cell, 0))
    out = lambda shape, kind=BF16: jax.ShapeDtypeStruct(shape, kind)
    dma = lambda *shape: pltpu.SemaphoreType.DMA(shape)
    outs = [
        out((cells, genes, width)),
        out((cells, classes, width), F32),
        out(slab.shape),
        out(vec.shape, F32),
    ]
    return pl.pallas_call(
        finish_kernel,
        grid=(cells * per_cell,),
        in_specs=[
            whole(slab),
            whole(vec),
            piece(width),
            piece(width),
            piece(width),
            piece(2 * width),
            pl.BlockSpec(memory_space=pl.ANY),
            whole(xc),
            whole(gmc),
            whole(dqc),
            whole(dkvc),
            whole(gain),
            whole(bias),
            whole(w),
        ],
        out_specs=[piece(width)] + [whole(o) for o in outs[1:]],
        out_shape=outs,
        scratch_shapes=[
            pltpu.VMEM((3 * width, width), BF16),
            pltpu.VMEM((cells, genes, 2 * width), BF16),
            pltpu.VMEM(dkvc.shape, F32),
            dma(cells),
            dma(cells),
            dma(),
            dma(),
        ]
        + Reduction.scratch(slab.shape[0], all_cells)
        + VectorSum.scratch(vec.shape, all_cells),
        compiler_params=pltpu.CompilerParams(
            vmem_limit_bytes=VMEM, collective_id=1, has_side_effects=True
        ),
        name="finish",
    )(slab, vec, x, gm, dq, dkv, dkv, xc, gmc, dqc, dkvc, gain, bias, w)


def unpack_kernel(
    slab, vec, gain, bias, w, x, xc, g_up, g_down, g_out, g_qkv, g_x, g_xc, *vectors
):
    step = pl.program_id(0)
    width, ff = g_up.shape
    g_x[...] = x[...]
    first = 0

    def take(target, at):
        nonlocal first
        rows = target.shape[0]
        begin = first
        first += rows * target.shape[1] // 128

        @pl.when(step == at)
        def _():
            for i in range(target.shape[1] // 128):
                spot = begin + i * rows
                target[:, i * 128 : (i + 1) * 128] = slab[spot : spot + rows, :].astype(F32)

    take(g_up, 0)
    take(g_down, 1)
    take(g_out, 1)
    line = 0

    def lines(count):
        nonlocal line
        line += count
        return jnp.concatenate([vec[i : i + 1, :] for i in range(line - count, line)], 1)

    up_bias, ln2_gain, ln2_bias, down_bias, ln1_gain, ln1_bias = vectors

    @pl.when(step == 2)
    def _():
        g_xc[...] = xc[...].astype(BF16)
        up_bias[...] = lines(ff // 128)
        ln2_gain[...] = lines(width // 128)
        ln2_bias[...] = lines(width // 128)
        down_bias[...] = lines(width // 128)
        packed_sum = lines(3 * width // 128)
        weights = w[...].astype(F32)
        sums = jnp.concatenate(
            [
                slab[first + i * width : first + (i + 1) * width, :].astype(F32)
                for i in range(3 * width // 128)
            ],
            1,
        )
        ln1_gain[...] = jnp.sum((weights * sums).T, 0, keepdims=True)
        ln1_bias[...] = jnp.sum((weights * packed_sum).T, 0, keepdims=True)
        g_qkv[...] = (
            widen(spread_column(gain[...]), 3 * width) * sums
            + widen(spread_column(bias[...]), 3 * width) * packed_sum
        )


def unpack(slab, vec, gain, bias, w, x, xc, ff):
    width = w.shape[0]
    cells, genes, _ = x.shape
    out = lambda *shape: jax.ShapeDtypeStruct(shape, F32)
    whole = lambda array: pl.BlockSpec(array.shape, lambda i: (0,) * len(array.shape))
    piece = pl.BlockSpec((1, genes, width), lambda i: (i, 0, 0))
    row = out(1, width)
    outs = [
        out(width, ff),
        out(ff, width),
        out(width, width),
        out(width, 3 * width),
        jax.ShapeDtypeStruct(x.shape, BF16),
        jax.ShapeDtypeStruct(xc.shape, BF16),
        out(1, ff),
        row,
        row,
        row,
        row,
        row,
    ]
    specs = [whole(o) for o in outs]
    specs[4] = piece
    return pl.pallas_call(
        unpack_kernel,
        grid=(cells,),
        in_specs=[whole(slab), whole(vec), whole(gain), whole(bias), whole(w), piece, whole(xc)],
        out_specs=specs,
        out_shape=outs,
        compiler_params=pltpu.CompilerParams(vmem_limit_bytes=VMEM),
        name="unpack",
    )(slab, vec, gain, bias, w, x, xc)


def shards(
    gene_in,
    class_in,
    expressed,
    ln1_gain,
    ln1_bias,
    w_qkv,
    w_out,
    ln2_gain,
    ln2_bias,
    w_up,
    b_up,
    w_down,
    b_down,
    gene_cot,
    class_cot,
):
    row = lambda vector: vector.reshape(1, -1)
    place = lax.axis_index("gene").reshape(1)
    gain1, bias1 = row(ln1_gain), row(ln1_bias)
    tables = project(expressed, gene_in, class_in, gain1, bias1, w_qkv)
    gene_out, class_out, dq, dqc, dkv, dkvc, gm, gmc, slab, vec = layer(
        expressed,
        place,
        tables,
        gene_in,
        class_in,
        gene_cot,
        class_cot,
        w_out,
        row(ln2_gain),
        row(ln2_bias),
        w_up,
        row(b_up),
        w_down,
        row(b_down),
    )
    gene_grad, class_grad, slab, vec = finish(
        slab, vec, gene_in, class_in, gm, gmc, dq, dqc, dkv, dkvc, gain1, bias1, w_qkv
    )
    (
        g_up,
        g_down,
        g_out,
        g_qkv,
        gene_grad,
        class_grad,
        g_b_up,
        g_gain2,
        g_bias2,
        g_b_down,
        g_gain1,
        g_bias1,
    ) = unpack(slab, vec, gain1, bias1, w_qkv, gene_grad, class_grad, w_up.shape[1])
    return (
        gene_out,
        class_out,
        gene_grad,
        class_grad,
        g_gain1[0],
        g_bias1[0],
        g_qkv,
        g_out,
        g_gain2[0],
        g_bias2[0],
        g_up,
        g_b_up[0],
        g_down,
        g_b_down[0],
    )


def solution(mesh):
    genes, cells, whole = P("cell", "gene", None), P("cell", None, None), P()
    return jax.shard_map(
        shards,
        mesh=mesh,
        in_specs=(genes, cells, P("cell")) + (whole,) * 10 + (genes, cells),
        out_specs=(genes, cells, genes, cells) + (whole,) * 10,
        check_vma=False,
    )
```

```python
import functools

import jax
import jax.numpy as jnp
from jax import lax
from jax.experimental import pallas as pl
from jax.experimental.pallas import tpu as pltpu
from jax.sharding import PartitionSpec as P

HEADS = 4
EPS = 1e-05
LOG2E = 1.4426950408889634
SAFE = 40.0
KB = 256
PIECE = 512
FF_STEP = 512
FEED_AHEAD = 2
AHEAD = 2
MARKS = 3
VECTOR_ROWS = 32
CUTS = 2
STAGES = (0, 1, 4, 7)
VMEM = 63 * 2**20
F32 = jnp.float32
BF16 = jnp.bfloat16
MESH = pl.DeviceIdType.MESH


def dot(left, right):
    return jnp.dot(left, right, preferred_element_type=F32)


def dot_nt(left, right):
    return lax.dot_general(left, right, (((1,), (1,)), ((), ())), preferred_element_type=F32)


def dot_tn(left, right):
    return lax.dot_general(left, right, (((0,), (0,)), ((), ())), preferred_element_type=F32)


def spread_column(row):
    return jnp.broadcast_to(row, (128, row.shape[1])).T


def widen(column, lanes):
    return jnp.concatenate([column] * (lanes // 128), axis=1)


def fold_lanes(values):
    total = values[:, :128]
    for start in range(128, values.shape[1], 128):
        total = total + values[:, start : start + 128]
    return total


def paired_loop(count, body, carried):
    carried = lax.fori_loop(
        0, count // 2, lambda i, value: body(2 * i + 1, body(2 * i, value)), carried
    )
    return lax.fori_loop(count // 2 * 2, count, body, carried)


def norm_rows(values):
    centered = values - jnp.mean(values, -1, keepdims=True)
    inverse = lax.rsqrt(jnp.mean(centered * centered, -1, keepdims=True) + EPS)
    return centered * inverse, inverse


def norm_columns(values):
    scale = 1.0 / values.shape[0]
    centered = values - jnp.sum(values, 0, keepdims=True) * scale
    inverse = lax.rsqrt(jnp.sum(centered * centered, 0, keepdims=True) * scale + EPS)
    return centered * inverse, inverse


def greet(partners):
    barrier = pltpu.get_barrier_semaphore()
    for partner in partners:
        pl.semaphore_signal(barrier, inc=1, device_id=partner, device_id_type=MESH)
    pl.semaphore_wait(barrier, len(partners))


def project_kernel(
    counts,
    x,
    x_hbm,
    xc,
    gain,
    bias,
    w,
    qt,
    kr,
    va,
    ut,
    stat,
    pc,
    w_t,
    gain_c,
    bias_c,
    other,
    sent,
    received,
):
    cell = pl.program_id(0)
    cells = x_hbm.shape[0]
    genes, width = x.shape[1:]
    head = width // HEADS
    place = lax.axis_index("gene")
    partner = {"cell": lax.axis_index("cell"), "gene": 1 - place}

    def swap(index):
        return pltpu.make_async_remote_copy(
            src_ref=x_hbm.at[index],
            dst_ref=other.at[index],
            send_sem=sent.at[index],
            recv_sem=received.at[index],
            device_id=partner,
            device_id_type=MESH,
        )

    @pl.when(cell == 0)
    def _():
        greet([partner])
        for index in range(cells):
            swap(index).start()
        w_t[...] = w[...].T
        gain_c[...] = spread_column(gain[...])
        bias_c[...] = spread_column(bias[...])

    def norms(columns, row, line):
        for h in range(HEADS):
            part = columns[h * head : (h + 1) * head]
            size = jnp.sum(part * part, 0, keepdims=True)
            best = size[:, :128]
            for start in range(128, columns.shape[1], 128):
                best = jnp.maximum(best, size[:, start : start + 128])
            stat[0, row, line + h : line + h + 1, :] = best

    def tables(values, half, origin):
        lows = []
        for first in range(0, genes, PIECE):
            span = slice(half * genes + first, half * genes + first + PIECE)
            unit, _ = norm_columns(values[first : first + PIECE].T.astype(F32))
            ut[0, :, span] = unit.astype(BF16)
            low = unit * widen(gain_c[...], PIECE) + widen(bias_c[...], PIECE)
            spot = origin + first + lax.broadcasted_iota(jnp.int32, (1, PIECE), 1)
            valid = spot < counts[cell]
            kept = jnp.where(valid, low, 0.0).astype(BF16)
            lows.append(low.astype(BF16))
            packed_t = dot(w_t[width:, :], kept)
            mark = jnp.where(
                (lax.broadcasted_iota(jnp.int32, (16, PIECE), 0) < MARKS) & valid, 1.0, 0.0
            ).astype(BF16)
            for h in range(HEADS):
                rows = slice(width + h * head, width + (h + 1) * head)
                va[0, h, :head, span] = packed_t[rows].astype(BF16)
                va[0, h, head:, span] = mark
            kr[0, span, :] = packed_t[:width].astype(BF16).T
            norms(packed_t[:width], half * (genes // PIECE) + first // PIECE, 0)
        return lows

    stat[...] = jnp.zeros_like(stat)
    for i, low in enumerate(tables(x[0], 0, place * genes)):
        query_t = dot(w_t[:width, :], low).astype(BF16) * (head**-0.5)
        qt[0, :, i * PIECE : (i + 1) * PIECE] = query_t
        norms(query_t.astype(F32), i, HEADS)
    unit, _ = norm_rows(xc[0].astype(F32))
    class_low = (unit * gain[...] + bias[...]).astype(BF16)
    pc[0] = dot(class_low, w[...]).astype(BF16).astype(F32)
    swap(cell).wait_recv()
    tables(other[cell], 1, (1 - place) * genes)

    @pl.when(cell == cells - 1)
    def _():
        for index in range(cells):
            swap(index).wait_send()


def project(counts, x, xc, gain, bias, w):
    cells, genes, width = x.shape
    total = 2 * genes
    classes = xc.shape[1]
    head = width // HEADS
    pieces = total // PIECE
    whole = lambda shape: pl.BlockSpec(shape, lambda c: (0,) * len(shape))
    per_cell = lambda *shape: pl.BlockSpec((1,) + shape, lambda c: (c,) + (0,) * len(shape))
    out = lambda shape, kind=BF16: jax.ShapeDtypeStruct(shape, kind)
    return pl.pallas_call(
        project_kernel,
        grid=(cells,),
        in_specs=[
            pl.BlockSpec(memory_space=pltpu.SMEM),
            per_cell(genes, width),
            pl.BlockSpec(memory_space=pl.ANY),
            per_cell(classes, width),
            whole((1, width)),
            whole((1, width)),
            whole((width, 3 * width)),
        ],
        out_specs=[
            per_cell(width, genes),
            per_cell(total, width),
            per_cell(HEADS, head + 16, total),
            per_cell(width, total),
            per_cell(pieces, 8, 128),
            per_cell(classes, 3 * width),
        ],
        out_shape=[
            out((cells, width, genes)),
            out((cells, total, width)),
            out((cells, HEADS, head + 16, total)),
            out((cells, width, total)),
            out((cells, pieces, 8, 128), F32),
            out((cells, classes, 3 * width), F32),
        ],
        scratch_shapes=[
            pltpu.VMEM((3 * width, width), BF16),
            pltpu.VMEM((width, 128), F32),
            pltpu.VMEM((width, 128), F32),
            pltpu.VMEM((cells, genes, width), BF16),
            pltpu.SemaphoreType.DMA((cells,)),
            pltpu.SemaphoreType.DMA((cells,)),
        ],
        compiler_params=pltpu.CompilerParams(
            vmem_limit_bytes=VMEM, collective_id=0, has_side_effects=True
        ),
        name="project",
    )(counts, x, x, xc, gain, bias, w)


def gelu_parts(u):
    phi = 0.5 + 0.5 * lax.erf(u * 0.7071067811865476)
    bell = jnp.exp2((u * u) * (-0.5 * LOG2E))
    return u * phi, phi + (u * 0.3989422804014327) * bell


def layer_kernel(
    counts,
    place,
    qt,
    kr,
    va,
    ut,
    stat,
    pc,
    x,
    xc,
    cot,
    cotc,
    w_out,
    gain,
    bias,
    w_up,
    b_up,
    w_down,
    b_down,
    y,
    yc,
    dq,
    dqc,
    dkv,
    dkvc,
    gm,
    gmc,
    slab,
    g_vec,
    w_out_t,
    w_up_t,
    w_down_t,
    gain_c,
    bias_c,
    b_up_c,
    b_down_c,
    probs,
    probs_ck,
    probs_cq,
    mix,
    shift,
    shift_q,
    inv_sum,
    qz,
    da,
    delta,
    att,
    datt,
    dq_t,
    grads_t,
    up_acc,
    g_down,
    g_out,
    qkv_acc,
    up_bias_acc,
    gain_acc,
    bias_acc,
    down_bias_acc,
    packed_sum,
    packed_cols,
):
    cell = pl.program_id(0)
    cells = pl.num_programs(0)
    genes, width = x.shape[1:]
    classes = xc.shape[1]
    head = width // HEADS
    ff = w_up.shape[1]
    stack = HEADS * classes
    factor = head**-0.5
    count = counts[cell]
    own_count = jnp.clip(count - place[0] * genes, 0, genes)
    other_count = jnp.clip(count - (1 - place[0]) * genes, 0, genes)
    own_blocks = (own_count + (KB - 1)) // KB
    other_blocks = (other_count + (KB - 1)) // KB
    half_blocks = genes // KB
    blocks = own_blocks + other_blocks

    def nth_block(index):
        block = jnp.where(index < own_blocks, index, index - own_blocks + half_blocks)
        return pl.multiple_of(block * KB, KB)

    @pl.when(cell == 0)
    def _():
        w_out_t[...] = w_out[...].T
        w_up_t[...] = w_up[...].T
        w_down_t[...] = w_down[...].T
        gain_c[...] = spread_column(gain[...])
        bias_c[...] = spread_column(bias[...])
        b_up_c[...] = spread_column(b_up[...])
        b_down_c[...] = spread_column(b_down[...])
        up_acc[...] = jnp.zeros_like(up_acc)
        up_bias_acc[...] = jnp.zeros_like(up_bias_acc)
        gain_acc[...] = jnp.zeros_like(gain_acc)
        bias_acc[...] = jnp.zeros_like(bias_acc)
        down_bias_acc[...] = jnp.zeros_like(down_bias_acc)
        g_down[...] = jnp.zeros_like(g_down)
        g_out[...] = jnp.zeros_like(g_out)
        qkv_acc[...] = jnp.zeros_like(qkv_acc)
        packed_sum[...] = jnp.zeros_like(packed_sum)
        packed_cols[...] = jnp.zeros_like(packed_cols)

    head_mask = lax.broadcasted_iota(jnp.int32, (stack, width), 1) // head == (
        lax.broadcasted_iota(jnp.int32, (stack, width), 0) // classes
    )
    pair_mask = lax.broadcasted_iota(jnp.int32, (stack, stack), 1) // classes == (
        lax.broadcasted_iota(jnp.int32, (stack, stack), 0) // classes
    )

    def by_head(rows):
        return jnp.where(head_mask, jnp.concatenate([rows] * HEADS, 0), 0.0)

    def from_heads(rows):
        kept = jnp.where(head_mask, rows, 0.0)
        total = kept[:classes]
        for h in range(1, HEADS):
            total = total + kept[h * classes : (h + 1) * classes]
        return total

    packed_c = pc[0]
    query_c = by_head(packed_c[:, :width] * factor)
    key_c = by_head(packed_c[:, width : 2 * width])
    value_c = by_head(packed_c[:, 2 * width :])
    key_c_t = key_c.T.astype(BF16)
    value_c_t = value_c.T.astype(BF16)
    query_cb, key_cb, value_cb = query_c.astype(BF16), key_c.astype(BF16), value_c.astype(BF16)

    half_rows = lax.broadcasted_iota(jnp.int32, (2 * head, genes), 0) // head
    for h in range(HEADS):
        pair = slice((h // 2) * 2 * head, (h // 2 + 1) * 2 * head)
        qz[h] = jnp.where(half_rows == h % 2, qt[0, pair, :].astype(F32), 0.0).astype(BF16)

    sizes = jnp.max(stat[0], 0)
    size_k, size_q = jnp.max(sizes[:HEADS]), jnp.max(sizes[HEADS:])
    size_k = jnp.maximum(size_k, jnp.max(jnp.sum(key_c * key_c, -1, keepdims=True)))
    size_q = jnp.maximum(size_q, jnp.max(jnp.sum(query_c * query_c, -1, keepdims=True)))
    safe = size_k * size_q < SAFE * SAFE

    def key_mask(start, shape, axis):
        limit = jnp.where(start < genes, own_count, genes + other_count)
        return start + lax.broadcasted_iota(jnp.int32, shape, axis) < limit

    shift[...] = jnp.zeros_like(shift)
    shift_q[...] = jnp.zeros_like(shift_q)

    @pl.when(jnp.logical_not(safe))
    def _():
        class_scores = dot(key_cb, qt[0])
        for h in range(HEADS):
            shift[h] = jnp.max(class_scores[h * classes : (h + 1) * classes], 0, keepdims=True)
        own_scores = jnp.where(pair_mask, dot(query_cb, key_c_t), -1e30)
        shift_q[...] = jnp.broadcast_to(jnp.max(own_scores, -1, keepdims=True), shift_q.shape)

        @pl.loop(0, blocks)
        def _(block):
            start = nth_block(block)
            for h in range(HEADS):
                scores = dot(
                    kr[0, pl.ds(start, KB), (h // 2) * 2 * head : (h // 2 + 1) * 2 * head], qz[h]
                )
                scores = jnp.where(key_mask(start, scores.shape, 0), scores, -1e30)
                shift[h] = jnp.maximum(shift[h], jnp.max(scores, 0, keepdims=True))
            scores = dot_nt(query_cb, kr[0, pl.ds(start, KB), :])
            scores = jnp.where(key_mask(start, scores.shape, 1), scores, -1e30)
            shift_q[...] = jnp.maximum(shift_q[...], jnp.max(scores, -1, keepdims=True))

        shift[...] = shift[...] * LOG2E
        shift_q[...] = shift_q[...] * LOG2E

    class_scores = dot(key_cb, qt[0])
    shift_rows = jnp.concatenate(
        [jnp.broadcast_to(shift[h], (classes, genes)) for h in range(HEADS)], 0
    )
    class_exp = jnp.exp2(class_scores * LOG2E - shift_rows).astype(BF16)
    probs_ck[...] = class_exp
    class_mix = dot(value_c_t, class_exp)
    for h in range(HEADS):
        mix[h, :head, :] = class_mix[h * head : (h + 1) * head]
        sums = jnp.sum(
            class_exp[h * classes : (h + 1) * classes].astype(F32), 0, keepdims=True
        )
        mix[h, head:, :] = jnp.where(
            lax.broadcasted_iota(jnp.int32, (16, genes), 0) == 0, sums, 0.0
        )
    shift_qc = shift_q[:, :1]
    own_exp = jnp.where(
        pair_mask, jnp.exp2(dot(query_cb, key_c_t) * LOG2E - shift_qc), 0.0
    ).astype(BF16)
    deep = head + 16

    def spread_heads(rows, extra):
        pieces = []
        for h in range(HEADS):
            pieces += [rows[:, h * head : (h + 1) * head], extra]
        return jnp.concatenate(pieces, 1)

    own_mix = spread_heads(
        dot(own_exp, value_cb),
        jnp.broadcast_to(jnp.sum(own_exp.astype(F32), -1, keepdims=True), (stack, 16)),
    )

    def forward_block(block, class_total, shifted):
        start = nth_block(block)
        keys = pl.ds(start, KB)
        scores = [
            dot(kr[0, keys, (h // 2) * 2 * head : (h // 2 + 1) * 2 * head], qz[h])
            for h in range(1)
        ]
        class_scores = dot_nt(query_cb, kr[0, keys, :]) * LOG2E - shift_qc
        for h in range(HEADS):
            if h + 1 < HEADS:
                g = h + 1
                scores.append(
                    dot(kr[0, keys, (g // 2) * 2 * head : (g // 2 + 1) * 2 * head], qz[g])
                )
            scaled = scores[h] * LOG2E
            if shifted:
                scaled = jnp.minimum(scaled - shift[h], 60.0)
            exps = jnp.exp2(scaled).astype(BF16)
            mix[h] += dot(va[0, h, :, keys], exps)
            probs[h, :, keys] = exps.T
        class_exp = jnp.where(
            key_mask(start, class_scores.shape, 1), jnp.exp2(class_scores), 0.0
        ).astype(BF16)
        probs_cq[:, keys] = class_exp
        return class_total + dot_nt(class_exp, va[0, :, :, keys].reshape(HEADS * deep, KB))

    class_total = lax.cond(
        safe,
        lambda: paired_loop(blocks, functools.partial(forward_block, shifted=False), own_mix),
        lambda: lax.fori_loop(0, blocks, functools.partial(forward_block, shifted=True), own_mix),
    )
    class_sum = jnp.concatenate(
        [
            class_total[h * classes : (h + 1) * classes, h * deep + head : h * deep + head + 1]
            for h in range(HEADS)
        ],
        0,
    )
    class_total = jnp.concatenate(
        [class_total[:, h * deep : h * deep + head] for h in range(HEADS)], 1
    )
    class_inv = 1.0 / class_sum
    class_att = from_heads(class_total * class_inv)
    for h in range(HEADS):
        inverse = 1.0 / mix[h, head : head + 1, :]
        inv_sum[h] = inverse
        att[h * head : (h + 1) * head, :genes] = (mix[h, :head, :] * inverse).astype(BF16)

    def pad_rows(rows):
        return jnp.concatenate([rows, jnp.zeros((128 - rows.shape[0], width), F32)], 0)

    att[:, genes:] = pad_rows(class_att).T.astype(BF16)

    def feed(start, columns, with_class):
        lanes = columns + (128 if with_class else 0)
        span = pl.ds(start, lanes)
        wide_gain = widen(gain_c[...], lanes)
        cot_r = cot[0, pl.ds(start, columns), :]
        cot_t = cot_r.T
        x_t = x[0, pl.ds(start, columns), :].T
        if with_class:
            x_t = jnp.concatenate([x_t, pad_rows(xc[0].astype(F32)).T.astype(BF16)], 1)
            padded = pad_rows(cotc[0].astype(F32))
            cot_t = jnp.concatenate([cot_t, padded.T.astype(BF16)], 1)
            cot_r = jnp.concatenate([cot_r, (padded * 0.5).astype(BF16)], 0)
            share = jnp.where(
                lax.broadcasted_iota(jnp.int32, (1, lanes), 1) < columns, 1.0, 0.5
            )
            weigh = lambda values: values * share
            row_share = jnp.where(
                lax.broadcasted_iota(jnp.int32, (lanes, 1), 0) < columns, 1.0, 0.5
            )
            weigh_rows = lambda rows: (rows.astype(F32) * row_share).astype(BF16)
        else:
            weigh = lambda values: values
            weigh_rows = lambda rows: rows
        parts = [slice(first, first + FF_STEP) for first in range(0, ff, FF_STEP)]
        held = {}

        def begin():
            held["att"] = att[:, span]
            middle = x_t.astype(F32) + dot(w_out_t[...], held["att"])
            held["unit"], held["inverse"] = norm_columns(middle)
            held["low"] = (held["unit"] * wide_gain + widen(bias_c[...], lanes)).astype(BF16)
            held["low_r"] = weigh_rows(held["low"].T)
            held["result"] = middle + widen(b_down_c[...], lanes)
            held["back"] = jnp.zeros((width, lanes), F32)

        def rise(part):
            up = dot(w_up_t[part, :], held["low"]) + widen(b_up_c[part, :], lanes)
            held[part.start] = up, dot(w_down[part, :], cot_t)

        def fall(part):
            up, grad_act = held.pop(part.start)
            active, slope = gelu_parts(up)
            active = active.astype(BF16)
            grad_up = slope * grad_act
            up_bias_acc[part, :] += fold_lanes(weigh(grad_up))
            grad_up = grad_up.astype(BF16)
            held["result"] += dot(w_down_t[:, part], active)
            held["back"] += dot(w_up[:, part], grad_up)
            g_down[part, :] += dot(active, cot_r)
            up_acc[part, :] += dot(grad_up, held["low_r"])

        def end():
            back, unit = held["back"], held["unit"]
            scaled = back * wide_gain
            scale = 1.0 / width
            grad_middle = cot_t.astype(F32) + held["inverse"] * (
                scaled
                - jnp.sum(scaled, 0, keepdims=True) * scale
                - unit * (jnp.sum(scaled * unit, 0, keepdims=True) * scale)
            )
            grad_middle = grad_middle.astype(BF16)
            datt[:, span] = dot(w_out[...], grad_middle).astype(BF16)
            gain_acc[...] += fold_lanes(weigh(back * unit))
            bias_acc[...] += fold_lanes(weigh(back))
            middle_r = grad_middle.T
            g_out[...] += dot(held["att"], weigh_rows(middle_r))
            down_bias_acc[...] += jnp.sum(cot_r.astype(F32), 0, keepdims=True)
            result_r = held["result"].T
            y[0, pl.ds(start, columns), :] = result_r[:columns].astype(BF16)
            gm[0, pl.ds(start, columns), :] = middle_r[:columns]
            if with_class:
                yc[0] = result_r[columns : columns + classes].astype(BF16)
                gmc[0] = middle_r[columns:].astype(F32)[:classes]

        rises = [begin] + [functools.partial(rise, part) for part in parts]
        falls = [functools.partial(fall, part) for part in parts] + [end]
        return rises, falls

    feed_step = 512
    pieces = genes // feed_step
    rises, falls = [], []
    for piece in range(pieces):
        more_rises, more_falls = feed(piece * feed_step, feed_step, piece == pieces - 1)
        rises += more_rises
        falls += more_falls
    for i in range(len(rises) + FEED_AHEAD):
        if i < len(rises):
            rises[i]()
        if i >= FEED_AHEAD:
            falls[i - FEED_AHEAD]()

    for h in range(HEADS):
        own = slice(h * head, (h + 1) * head)
        inverse = inv_sum[h]
        grad = (datt[own, :genes].astype(F32) * inverse).astype(BF16)
        row_delta = jnp.sum(grad.astype(F32) * (mix[h, :head, :] * inverse), 0, keepdims=True)
        delta[h] = row_delta
        datt[own, :genes] = grad
        parts = jnp.zeros((16, genes), F32)
        rest = row_delta
        for i in range(MARKS):
            piece = rest.astype(BF16).astype(F32)
            rest = rest - piece
            parts = jnp.where(
                lax.broadcasted_iota(jnp.int32, (16, genes), 0) == i, -piece, parts
            )
        blank = jnp.zeros((2 * head - deep, genes), BF16)
        da[h] = jnp.concatenate([grad, parts.astype(BF16), blank], 0).T

    class_grad = datt[:, genes:].astype(F32).T[:classes]
    class_grad = by_head(class_grad) * class_inv
    class_grad_b = class_grad.astype(BF16)
    class_grad_h = (class_grad * 0.5).astype(BF16)
    query_ch = (query_c * 0.5).astype(BF16)
    class_delta = jnp.sum(
        class_grad_b.astype(F32) * (class_total * class_inv), -1, keepdims=True
    )

    class_dprob = dot(value_cb, datt[:, :genes])
    delta_rows = jnp.concatenate(
        [jnp.broadcast_to(delta[h], (classes, genes)) for h in range(HEADS)], 0
    )
    class_probs = probs_ck[...]
    class_dscore = (class_probs.astype(F32) * (class_dprob - delta_rows)).astype(BF16)
    dq_t[...] = dot(key_c_t, class_dscore)
    class_dkey = dot_nt(class_dscore, qt[0])
    class_dvalue = dot_nt(class_probs, datt[:, :genes])
    own_dprob = dot(class_grad_b, value_c_t)
    own_dscore = (own_exp.astype(F32) * (own_dprob - class_delta)).astype(BF16)
    class_dquery = dot(own_dscore, key_cb)
    class_dkey = class_dkey + dot(own_dscore.astype(F32).T.astype(BF16), query_ch)
    class_dvalue = class_dvalue + dot(own_exp.astype(F32).T.astype(BF16), class_grad_h)

    class_grad_s = spread_heads(class_grad_b, jnp.zeros((stack, 16), BF16))
    class_grad_ht = class_grad_h.T
    query_ct = query_ch.T

    def settle(start):
        keys = pl.ds(pl.multiple_of(start, KB), KB)
        grads = grads_t[...].T
        dkv[0, keys, :] = grads
        qkv_acc[:, width:] += dot(ut[0, :, keys], grads)

    def backward_block(block, carried):
        class_dquery, previous = carried
        start = nth_block(block)
        keys = pl.ds(start, KB)
        dprobs = [dot(da[h, :, :deep], va[0, h, :, keys]) for h in range(AHEAD)]
        settle(previous)
        class_weights = probs_cq[:, keys]
        class_dprob = dot(class_grad_s, va[0, :, :, keys].reshape(HEADS * deep, KB))
        class_dscore = (class_weights.astype(F32) * (class_dprob - class_delta)).astype(BF16)
        dkeys, dvalues, dscores = [], [], []
        key_t = kr[0, keys, :].T
        for h in range(HEADS + 1):
            if h + AHEAD < HEADS:
                dprobs.append(dot(da[h + AHEAD, :, :deep], va[0, h + AHEAD, :, keys]))
            if h < HEADS:
                weights = probs[h, :, keys]
                dscore = weights * dprobs[h].astype(BF16)
                dscores.append(dscore)
                spot = slice(h % 2 * 2, h % 2 * 2 + 2)
                qz[spot] = dscore.T.reshape(2, KB // 2, genes)
                own = slice(h * head, (h + 1) * head)
                dvalues.append(dot(datt[own, :genes], weights))
                dkeys.append(dot(qt[0, own, :], dscore))
            if h > 0:
                own = slice((h - 1) * head, h * head)
                spot = slice((h - 1) % 2 * 2, (h - 1) % 2 * 2 + 2)
                dq_t[own, :] += dot(key_t[own, :], qz[spot].reshape(KB, genes))
        class_dquery = class_dquery + dot(class_dscore, kr[0, keys, :])
        dkey = jnp.concatenate(dkeys, 0) + dot(query_ct, class_dscore)
        dvalue = jnp.concatenate(dvalues, 0) + dot(class_grad_ht, class_weights)
        valid = key_mask(start, (1, KB), 1)
        grads = jnp.where(valid, jnp.concatenate([dkey, dvalue], 0), 0.0)
        packed_cols[...] += fold_lanes(grads)
        grads_t[...] = grads.astype(BF16)
        return class_dquery, start

    grads_t[...] = jnp.zeros_like(grads_t)
    class_dquery, previous = paired_loop(
        blocks, backward_block, (class_dquery, nth_block(0))
    )
    settle(previous)

    def blank_rows(block):
        dkv[0, pl.ds(pl.multiple_of(block * KB, KB), KB), :] = jnp.zeros((KB, 2 * width), BF16)

    pl.loop(own_blocks, half_blocks)(blank_rows)
    pl.loop(half_blocks + other_blocks, 2 * half_blocks)(blank_rows)

    dquery_r = (dq_t[...] * factor).astype(BF16).T
    dq[0] = dquery_r
    qkv_acc[:, :width] += dot(ut[0, :, :genes], dquery_r)
    class_dquery = from_heads(class_dquery) * factor
    class_dkv = jnp.concatenate([from_heads(class_dkey), from_heads(class_dvalue)], 1)
    dqc[0] = class_dquery
    dkvc[0] = class_dkv
    class_packed = jnp.concatenate([class_dquery * 0.5, class_dkv], 1)
    class_unit, _ = norm_rows(xc[0].astype(F32))
    pad = jnp.zeros((128 - classes, width), F32)
    class_unit_t = jnp.concatenate([class_unit, pad], 0).T.astype(BF16)
    class_packed_p = jnp.concatenate([class_packed] + [jnp.zeros((128 - classes, 3 * width), F32)], 0)
    qkv_acc[...] += dot(class_unit_t, class_packed_p.astype(BF16))
    packed_sum[:, :width] += jnp.sum(dquery_r.astype(F32), 0, keepdims=True)
    packed_sum[...] += jnp.sum(class_packed, 0, keepdims=True)

    @pl.when(cell == cells - 1)
    def _():
        first = 0

        def put(values):
            nonlocal first
            rows = values.shape[0]
            for start in range(0, values.shape[1], 128):
                slab[first : first + rows, :] = values[:, start : start + 128].astype(BF16)
                first += rows

        put(up_acc[...].T)
        put(g_down[...])
        put(g_out[...])
        put(qkv_acc[...])
        if first < slab.shape[0]:
            slab[first:, :] = jnp.zeros((slab.shape[0] - first, 128), BF16)
        g_vec[...] = jnp.zeros_like(g_vec)
        line = 0
        for vector in (
            jnp.sum(up_bias_acc[...].T, 0, keepdims=True),
            jnp.sum(gain_acc[...].T, 0, keepdims=True),
            jnp.sum(bias_acc[...].T, 0, keepdims=True),
            down_bias_acc[...],
            packed_sum[...]
            + jnp.concatenate(
                [jnp.zeros((1, width), F32), jnp.sum(packed_cols[...].T, 0, keepdims=True)], 1
            ),
        ):
            for start in range(0, vector.shape[1], 128):
                g_vec[line : line + 1, :] = vector[:, start : start + 128]
                line += 1


def layer(
    counts, place, tables, x, xc, cot, cotc, w_out, gain, bias, w_up, b_up, w_down, b_down
):
    cells, genes, width = x.shape
    classes = xc.shape[1]
    total = tables[1].shape[1]
    head = width // HEADS
    ff = w_up.shape[1]
    stack = HEADS * classes
    slab_rows = Reduction.padded((2 * ff + 4 * width) * width // 128, lax.axis_size("cell"))
    whole = lambda shape: pl.BlockSpec(
        shape, lambda c, *_: (0,) * len(shape), pipeline_mode=pl.Buffered(1)
    )
    per_cell = lambda *shape: pl.BlockSpec((1,) + shape, lambda c, *_: (c,) + (0,) * len(shape))
    kept = lambda *shape: whole(shape)
    out = lambda shape, kind=BF16: jax.ShapeDtypeStruct(shape, kind)
    vmem = lambda *shape, kind=BF16: pltpu.VMEM(shape, kind)
    f32 = functools.partial(vmem, kind=F32)
    return pl.pallas_call(
        layer_kernel,
        grid_spec=pltpu.PrefetchScalarGridSpec(
            num_scalar_prefetch=2,
            grid=(cells,),
            in_specs=[
                per_cell(width, genes),
                per_cell(total, width),
                per_cell(HEADS, head + 16, total),
                per_cell(width, total),
                per_cell(total // PIECE, 8, 128),
                per_cell(classes, 3 * width),
                per_cell(genes, width),
                per_cell(classes, width),
                per_cell(genes, width),
                per_cell(classes, width),
                whole((width, width)),
                whole((1, width)),
                whole((1, width)),
                whole((width, ff)),
                whole((1, ff)),
                whole((ff, width)),
                whole((1, width)),
            ],
            out_specs=[
                per_cell(genes, width),
                per_cell(classes, width),
                per_cell(genes, width),
                per_cell(classes, width),
                per_cell(total, 2 * width),
                per_cell(classes, 2 * width),
                per_cell(genes, width),
                per_cell(classes, width),
                kept(slab_rows, 128),
                kept(VECTOR_ROWS, 128),
            ],
            scratch_shapes=[
                vmem(width, width),
                vmem(ff, width),
                vmem(width, ff),
                f32(width, 128),
                f32(width, 128),
                f32(ff, 128),
                f32(width, 128),
                vmem(HEADS, genes, total),
                vmem(stack, genes),
                vmem(stack, total),
                f32(HEADS, head + 16, genes),
                f32(HEADS, 1, genes),
                f32(stack, 128),
                f32(HEADS, 1, genes),
                vmem(HEADS, 2 * head, genes),
                vmem(HEADS, genes, 2 * head),
                f32(HEADS, 1, genes),
                vmem(width, genes + 128),
                vmem(width, genes + 128),
                f32(width, genes),
                vmem(2 * width, KB),
                f32(ff, width),
                f32(ff, width),
                f32(width, width),
                f32(width, 3 * width),
                f32(ff, 128),
                f32(width, 128),
                f32(width, 128),
                f32(1, width),
                f32(1, 3 * width),
                f32(2 * width, 128),
            ],
        ),
        out_shape=[
            out((cells, genes, width)),
            out((cells, classes, width)),
            out((cells, genes, width)),
            out((cells, classes, width), F32),
            out((cells, total, 2 * width)),
            out((cells, classes, 2 * width), F32),
            out((cells, genes, width)),
            out((cells, classes, width), F32),
            out((slab_rows, 128)),
            out((VECTOR_ROWS, 128), F32),
        ],
        compiler_params=pltpu.CompilerParams(vmem_limit_bytes=VMEM),
        name="layer",
    )(counts, place, *tables, x, xc, cot, cotc, w_out, gain, bias, w_up, b_up, w_down, b_down)


class Reduction:
    @staticmethod
    def groups(cells):
        bits = (cells - 1).bit_length()
        return [(shift, min(2, bits - shift)) for shift in range(0, bits, 2)]

    @staticmethod
    def streams(rows, cells):
        groups = Reduction.groups(cells)
        unit = 2 * 16 * cells
        units = -(-rows // unit)
        kinds = min(len(groups), units)
        shares = [units // kinds] * kinds
        if kinds == 2:
            shares[1] = max(1, units // 3)
        shares[0] = units - sum(shares[1:])
        result, first = [], 0
        for turn in range(CUTS):
            for i, share in enumerate(shares):
                share = share * (turn + 1) // CUTS - share * turn // CUTS
                if share:
                    result.append((first, share * unit, groups[i:] + groups[:i]))
                    first += share * unit
        return result

    @staticmethod
    def padded(rows, cells):
        first, size, _ = Reduction.streams(rows, cells)[-1]
        return first + size

    @staticmethod
    def scratch(rows, cells):
        rows = Reduction.padded(rows, cells)
        hops = 2 + 2 * sum((1 << bits) - 1 for _, bits in Reduction.groups(cells))
        sems = (len(Reduction.streams(rows, cells)), hops)
        return [
            pltpu.VMEM((rows // 2, 128), BF16),
            pltpu.VMEM((rows, 128), BF16),
            pltpu.VMEM((rows, 128), BF16),
            pltpu.SemaphoreType.DMA(sems),
            pltpu.SemaphoreType.DMA(sems),
        ]

    def __init__(self, source, cells, work, inbox, total, sent, received):
        self.source, self.work, self.inbox, self.total = source, work, inbox, total
        self.sent, self.received = sent, received
        self.plan = self.streams(source.shape[0], cells)
        self.depth = len(self.groups(cells))
        self.stages = 2 * self.depth + 3
        self.me, self.place = lax.axis_index("cell"), lax.axis_index("gene")

    def peer(self, group, ahead):
        shift, bits = group
        radix = 1 << bits
        digit = (self.me // (1 << shift)) % radix
        there = (digit + ahead) % radix
        return {"cell": self.me + (there - digit) * (1 << shift), "gene": self.place}, there

    def digit(self, group):
        return (self.me // (1 << group[0])) % (1 << group[1])

    def held(self, stream, level):
        _, rows, order = self.plan[stream]
        first, size = 0, rows // 2
        for group in order[:level]:
            size = size >> group[1]
            first = first + self.digit(group) * size
        return first, size

    def slot(self, stream, level):
        first, rows, order = self.plan[stream]
        size = rows // 2
        spot = first
        for i in range(level):
            spot += size if i == 0 else ((1 << order[i - 1][1]) - 1) * size
            size = size >> order[i][1] if i < len(order) else size
        return spot

    def copy(self, source, target, stream, hop, ahead, device):
        return pltpu.make_async_remote_copy(
            src_ref=source,
            dst_ref=target,
            send_sem=self.sent.at[stream, hop + ahead - 1],
            recv_sem=self.received.at[stream, hop + ahead - 1],
            device_id=device,
            device_id_type=MESH,
        )

    def hop(self, stream, index):
        peers = [1] + [(1 << bits) - 1 for _, bits in self.plan[stream][2]]
        return sum((peers + peers[::-1])[:index])

    def rows(self, first, size):
        return pl.ds(pl.multiple_of(first, 16), size)

    def scatter(self, stream, level):
        first, rows, order = self.plan[stream]
        half = rows // 2
        if level == 0:
            mate = {"cell": self.me, "gene": 1 - self.place}
            source = self.source.at[self.rows(first + (1 - self.place) * half, half), :]
            target = self.inbox.at[pl.ds(first, half), :]
            return [self.copy(source, target, stream, 0, 1, mate)]
        group = order[level - 1]
        start, size = self.held(stream, level - 1)
        size = size >> group[1]
        copies = []
        for ahead in range(1, 1 << group[1]):
            device, there = self.peer(group, ahead)
            source = self.work.at[self.rows(first // 2 + start + there * size, size), :]
            target = self.inbox.at[pl.ds(self.slot(stream, level) + (ahead - 1) * size, size), :]
            copies.append(self.copy(source, target, stream, self.hop(stream, level), ahead, device))
        return copies

    def add(self, stream, level):
        first, rows, order = self.plan[stream]
        half = rows // 2
        start, size = self.held(stream, level)
        if level == 0:
            value = self.source[self.rows(first + self.place * half, half), :].astype(F32)
            count = 1
        else:
            value = self.work[self.rows(first // 2 + start, size), :].astype(F32)
            count = (1 << order[level - 1][1]) - 1
        for i in range(count):
            value += self.inbox[pl.ds(self.slot(stream, level) + i * size, size), :].astype(F32)
        if level == self.depth:
            self.total[self.rows(first + self.place * half + start, size), :] = value.astype(BF16)
        else:
            self.work[self.rows(first // 2 + start, size), :] = value.astype(BF16)

    def gather(self, stream, level):
        first, rows, order = self.plan[stream]
        half = rows // 2
        start, size = self.held(stream, level)
        span = self.total.at[self.rows(first + self.place * half + start, size), :]
        hop = self.hop(stream, 2 * self.depth + 1 - level)
        if level == 0:
            mate = {"cell": self.me, "gene": 1 - self.place}
            return [self.copy(span, span, stream, hop, 1, mate)]
        group = order[level - 1]
        return [
            self.copy(span, span, stream, hop, ahead, self.peer(group, ahead)[0])
            for ahead in range(1, 1 << group[1])
        ]

    def copies(self, stream, index):
        if index <= self.depth:
            return self.scatter(stream, index)
        return self.gather(stream, 2 * self.depth + 1 - index)

    def stage(self, index):
        for stream in range(len(self.plan)):
            if index > 0:
                for copy in self.copies(stream, index - 1):
                    copy.wait()
                if index - 1 <= self.depth:
                    self.add(stream, index - 1)
            if index < self.stages - 1:
                for copy in self.copies(stream, index):
                    copy.start()


class VectorSum:
    @staticmethod
    def scratch(shape, cells):
        groups = Reduction.groups(cells)
        return [
            pltpu.VMEM((2 + sum(1 << bits for _, bits in groups),) + shape, F32),
            pltpu.SemaphoreType.DMA((len(groups) + 1, 3)),
            pltpu.SemaphoreType.DMA((len(groups) + 1, 3)),
        ]

    def __init__(self, cells, reduction, slots, sent, received):
        self.reduction, self.slots, self.sent, self.received = reduction, slots, sent, received
        self.groups = reduction.groups(cells)

    def first(self, level):
        return 0 if level == 0 else 2 + sum(1 << bits for _, bits in self.groups[: level - 1])

    def size(self, level):
        return 2 if level == 0 else 1 << self.groups[level - 1][1]

    def copies(self, level):
        r = self.reduction
        if level == 0:
            mine = r.place
            devices = [{"cell": r.me, "gene": 1 - r.place}]
        else:
            group = self.groups[level - 1]
            mine = r.digit(group)
            devices = [r.peer(group, ahead)[0] for ahead in range(1, self.size(level))]
        spot = self.slots.at[self.first(level) + mine]
        return mine, [
            pltpu.make_async_remote_copy(
                src_ref=spot,
                dst_ref=spot,
                send_sem=self.sent.at[level, i],
                recv_sem=self.received.at[level, i],
                device_id=device,
                device_id_type=MESH,
            )
            for i, device in enumerate(devices)
        ]

    def start(self, level, value):
        mine, copies = self.copies(level)
        self.slots[self.first(level) + mine] = value
        for copy in copies:
            copy.start()

    def finish(self, level):
        for copy in self.copies(level)[1]:
            copy.wait()
        first = self.first(level)
        total = self.slots[first]
        for i in range(1, self.size(level)):
            total = total + self.slots[first + i]
        return total

    def stage(self, index, value):
        levels = len(self.groups)
        if 0 < index <= levels + 1:
            value = self.finish(index - 1)
        if index <= levels:
            self.start(index, value)
        return value if index == levels + 1 else None


def finish_kernel(
    slab,
    vec,
    x,
    gm,
    dq,
    dkv,
    dkv_hbm,
    xc,
    gmc,
    dqc,
    dkvc,
    gain,
    bias,
    w,
    g_x,
    g_xc,
    slab_out,
    vec_out,
    w_t,
    other,
    other_c,
    swap_send,
    swap_recv,
    class_send,
    class_recv,
    *reduction_scratch,
):
    step, steps = pl.program_id(0), pl.num_programs(0)
    cells = dkv_hbm.shape[0]
    genes = dkv_hbm.shape[1] // 2
    rows, width = x.shape[1:]
    classes = xc.shape[1]
    per_cell = genes // rows
    all_cells = lax.axis_size("cell")
    sums = Reduction(slab, all_cells, *reduction_scratch[:5])
    vectors = VectorSum(all_cells, sums, *reduction_scratch[5:])
    mate = {"cell": sums.me, "gene": 1 - sums.place}

    def swap(cell):
        return pltpu.make_async_remote_copy(
            src_ref=dkv_hbm.at[cell, pl.ds(genes, genes), :],
            dst_ref=other.at[cell],
            send_sem=swap_send.at[cell],
            recv_sem=swap_recv.at[cell],
            device_id=mate,
            device_id_type=MESH,
        )

    def swap_class():
        return pltpu.make_async_remote_copy(
            src_ref=dkvc,
            dst_ref=other_c,
            send_sem=class_send,
            recv_sem=class_recv,
            device_id=mate,
            device_id_type=MESH,
        )

    def stage(index):
        sums.stage(index)
        done = vectors.stage(index, vec[...] if index == 0 else None)
        if done is not None:
            vec_out[...] = done

    def rows_back(values, grads, packed):
        unit, inverse = norm_rows(values)
        scaled = dot(packed, w_t[...]) * gain[...]
        return grads + inverse * (
            scaled
            - jnp.mean(scaled, -1, keepdims=True)
            - unit * jnp.mean(scaled * unit, -1, keepdims=True)
        )

    for index, at in enumerate(STAGES):

        @pl.when(step == at)
        def _(index=index):
            if index == 0:
                partners = [mate]
                for group in sums.groups(all_cells):
                    for ahead in range(1, 1 << group[1]):
                        partners.append(sums.peer(group, ahead)[0])
                greet(partners)
            stage(index)
            if index == 0:
                for cell in range(cells):
                    swap(cell).start()
                swap_class().start()
                w_t[...] = w[...].T

    cell = step // per_cell

    @pl.when(step % per_cell == 0)
    def _():
        swap(cell).wait()

    grads = dkv[0].astype(F32) + other[
        cell, pl.ds(pl.multiple_of((step % per_cell) * rows, 16), rows), :
    ].astype(F32)
    packed = jnp.concatenate([dq[0], grads.astype(BF16)], 1)
    g_x[0] = rows_back(x[0].astype(F32), gm[0].astype(F32), packed).astype(BF16)

    @pl.when(step == steps - 1)
    def _():
        swap_class().wait()
        class_grads = dkvc[...] + other_c[...]
        stack = cells * classes
        packed = jnp.concatenate([dqc[...], class_grads], 2).reshape(stack, 3 * width)
        values = xc[...].astype(F32).reshape(stack, width)
        result = rows_back(values, gmc[...].reshape(stack, width), packed.astype(BF16))
        g_xc[...] = result.reshape(cells, classes, width)
        for index in range(len(STAGES), sums.stages):
            stage(index)
        slab_out[...] = sums.total[...]


def finish(slab, vec, x, xc, gm, gmc, dq, dqc, dkv, dkvc, gain, bias, w):
    cells, genes, width = x.shape
    classes = xc.shape[1]
    rows = genes // 2
    per_cell = genes // rows
    all_cells = lax.axis_size("cell")
    whole = lambda array: pl.BlockSpec(array.shape, lambda i: (0,) * array.ndim)
    piece = lambda lanes: pl.BlockSpec((1, rows, lanes), lambda i: (i // per_cell, i % per_cell, 0))
    out = lambda shape, kind=BF16: jax.ShapeDtypeStruct(shape, kind)
    dma = lambda *shape: pltpu.SemaphoreType.DMA(shape)
    outs = [
        out((cells, genes, width)),
        out((cells, classes, width), F32),
        out(slab.shape),
        out(vec.shape, F32),
    ]
    return pl.pallas_call(
        finish_kernel,
        grid=(cells * per_cell,),
        in_specs=[
            whole(slab),
            whole(vec),
            piece(width),
            piece(width),
            piece(width),
            piece(2 * width),
            pl.BlockSpec(memory_space=pl.ANY),
            whole(xc),
            whole(gmc),
            whole(dqc),
            whole(dkvc),
            whole(gain),
            whole(bias),
            whole(w),
        ],
        out_specs=[piece(width)] + [whole(o) for o in outs[1:]],
        out_shape=outs,
        scratch_shapes=[
            pltpu.VMEM((3 * width, width), BF16),
            pltpu.VMEM((cells, genes, 2 * width), BF16),
            pltpu.VMEM(dkvc.shape, F32),
            dma(cells),
            dma(cells),
            dma(),
            dma(),
        ]
        + Reduction.scratch(slab.shape[0], all_cells)
        + VectorSum.scratch(vec.shape, all_cells),
        compiler_params=pltpu.CompilerParams(
            vmem_limit_bytes=VMEM, collective_id=1, has_side_effects=True
        ),
        name="finish",
    )(slab, vec, x, gm, dq, dkv, dkv, xc, gmc, dqc, dkvc, gain, bias, w)


def unpack_kernel(slab, vec, gain, bias, w, x, xc, g_x, g_up, g_down, g_out, g_qkv, g_xc, *rest):
    *vectors, up, down, out, qkv, passing, sems = rest
    width, ff = up.shape
    copies = [
        pltpu.make_async_copy(source, target, sems.at[i])
        for i, (source, target) in enumerate(
            [(x, passing), (up, g_up), (down, g_down), (out, g_out), (qkv, g_qkv), (passing, g_x)]
        )
    ]
    copies[0].start()
    first = 0

    def take(target):
        nonlocal first
        rows = target.shape[0]
        for start in range(0, target.shape[1], 128):
            target[:, start : start + 128] = slab[first : first + rows, :].astype(F32)
            first += rows

    for copy, target in zip(copies[1:4], (up, down, out)):
        take(target)
        copy.start()
    copies[0].wait()
    copies[5].start()
    take(qkv)
    line = 0

    def lines(count):
        nonlocal line
        line += count
        return jnp.concatenate([vec[i : i + 1, :] for i in range(line - count, line)], 1)

    up_bias, ln2_gain, ln2_bias, down_bias, ln1_gain, ln1_bias = vectors
    up_bias[...] = lines(ff // 128)
    ln2_gain[...] = lines(width // 128)
    ln2_bias[...] = lines(width // 128)
    down_bias[...] = lines(width // 128)
    packed_sum = lines(3 * width // 128)
    weights = w[...].astype(F32)
    sums = qkv[...]
    qkv[...] = (
        widen(spread_column(gain[...]), 3 * width) * sums
        + widen(spread_column(bias[...]), 3 * width) * packed_sum
    )
    copies[4].start()
    ln1_gain[...] = jnp.sum((weights * sums).T, 0, keepdims=True)
    ln1_bias[...] = jnp.sum((weights * packed_sum).T, 0, keepdims=True)
    g_xc[...] = xc[...].astype(BF16)
    for copy in copies[1:]:
        copy.wait()


def unpack(slab, vec, gain, bias, w, x, xc, ff):
    width = w.shape[0]
    out = lambda *shape: jax.ShapeDtypeStruct(shape, F32)
    row = out(1, width)
    sums = [(width, ff), (ff, width), (width, width), (width, 3 * width)]
    anywhere = pl.BlockSpec(memory_space=pl.ANY)
    local = pl.BlockSpec(memory_space=pltpu.VMEM)
    return pl.pallas_call(
        unpack_kernel,
        in_specs=[local] * 5 + [anywhere, local],
        out_specs=[anywhere] * 5 + [local] * 7,
        out_shape=[jax.ShapeDtypeStruct(x.shape, BF16)]
        + [out(*shape) for shape in sums]
        + [jax.ShapeDtypeStruct(xc.shape, BF16), out(1, ff), row, row, row, row, row],
        scratch_shapes=[pltpu.VMEM(shape, F32) for shape in sums]
        + [pltpu.VMEM(x.shape, BF16), pltpu.SemaphoreType.DMA((6,))],
        compiler_params=pltpu.CompilerParams(vmem_limit_bytes=VMEM),
        name="unpack",
    )(slab, vec, gain, bias, w, x, xc)


def shards(
    gene_in,
    class_in,
    expressed,
    ln1_gain,
    ln1_bias,
    w_qkv,
    w_out,
    ln2_gain,
    ln2_bias,
    w_up,
    b_up,
    w_down,
    b_down,
    gene_cot,
    class_cot,
):
    row = lambda vector: vector.reshape(1, -1)
    place = lax.axis_index("gene").reshape(1)
    gain1, bias1 = row(ln1_gain), row(ln1_bias)
    tables = project(expressed, gene_in, class_in, gain1, bias1, w_qkv)
    gene_out, class_out, dq, dqc, dkv, dkvc, gm, gmc, slab, vec = layer(
        expressed,
        place,
        tables,
        gene_in,
        class_in,
        gene_cot,
        class_cot,
        w_out,
        row(ln2_gain),
        row(ln2_bias),
        w_up,
        row(b_up),
        w_down,
        row(b_down),
    )
    gene_grad, class_grad, slab, vec = finish(
        slab, vec, gene_in, class_in, gm, gmc, dq, dqc, dkv, dkvc, gain1, bias1, w_qkv
    )
    (
        gene_grad,
        g_up,
        g_down,
        g_out,
        g_qkv,
        class_grad,
        g_b_up,
        g_gain2,
        g_bias2,
        g_b_down,
        g_gain1,
        g_bias1,
    ) = unpack(slab, vec, gain1, bias1, w_qkv, gene_grad, class_grad, w_up.shape[1])
    return (
        gene_out,
        class_out,
        gene_grad,
        class_grad,
        g_gain1[0],
        g_bias1[0],
        g_qkv,
        g_out,
        g_gain2[0],
        g_bias2[0],
        g_up,
        g_b_up[0],
        g_down,
        g_b_down[0],
    )


def solution(mesh):
    genes, cells, whole = P("cell", "gene", None), P("cell", None, None), P()
    return jax.shard_map(
        shards,
        mesh=mesh,
        in_specs=(genes, cells, P("cell")) + (whole,) * 10 + (genes, cells),
        out_specs=(genes, cells, genes, cells) + (whole,) * 10,
        check_vma=False,
    )
```

```python
import functools

import jax
import jax.numpy as jnp
from jax import lax
from jax.experimental import pallas as pl
from jax.experimental.pallas import tpu as pltpu
from jax.sharding import PartitionSpec as P

HEADS = 4
EPS = 1e-05
LOG2E = 1.4426950408889634
SAFE = 40.0
KB = 256
PIECE = 512
FF_STEP = 512
FEED_AHEAD = 2
AHEAD = 2
MARKS = 3
VECTOR_ROWS = 32
CUTS = 2
STAGES = (0, 1, 4, 7)
VMEM = 63 * 2**20
F32 = jnp.float32
BF16 = jnp.bfloat16
MESH = pl.DeviceIdType.MESH


def dot(left, right):
    return jnp.dot(left, right, preferred_element_type=F32)


def dot_nt(left, right):
    return lax.dot_general(left, right, (((1,), (1,)), ((), ())), preferred_element_type=F32)


def dot_tn(left, right):
    return lax.dot_general(left, right, (((0,), (0,)), ((), ())), preferred_element_type=F32)


def spread_column(row):
    return jnp.broadcast_to(row, (128, row.shape[1])).T


def widen(column, lanes):
    return jnp.concatenate([column] * (lanes // 128), axis=1)


def fold_lanes(values):
    total = values[:, :128]
    for start in range(128, values.shape[1], 128):
        total = total + values[:, start : start + 128]
    return total


def paired_loop(count, body, carried):
    carried = lax.fori_loop(
        0, count // 2, lambda i, value: body(2 * i + 1, body(2 * i, value)), carried
    )
    return lax.fori_loop(count // 2 * 2, count, body, carried)


def norm_rows(values):
    centered = values - jnp.mean(values, -1, keepdims=True)
    inverse = lax.rsqrt(jnp.mean(centered * centered, -1, keepdims=True) + EPS)
    return centered * inverse, inverse


def norm_columns(values):
    scale = 1.0 / values.shape[0]
    centered = values - jnp.sum(values, 0, keepdims=True) * scale
    inverse = lax.rsqrt(jnp.sum(centered * centered, 0, keepdims=True) * scale + EPS)
    return centered * inverse, inverse


def greet(partners):
    barrier = pltpu.get_barrier_semaphore()
    for partner in partners:
        pl.semaphore_signal(barrier, inc=1, device_id=partner, device_id_type=MESH)
    pl.semaphore_wait(barrier, len(partners))


def project_kernel(
    counts,
    x,
    x_hbm,
    xc,
    gain,
    bias,
    w,
    qt,
    kr,
    va,
    ut,
    stat,
    pc,
    w_t,
    gain_c,
    bias_c,
    other,
    sent,
    received,
):
    cell = pl.program_id(0)
    cells = x_hbm.shape[0]
    genes, width = x.shape[1:]
    head = width // HEADS
    place = lax.axis_index("gene")
    partner = {"cell": lax.axis_index("cell"), "gene": 1 - place}

    def swap(index):
        return pltpu.make_async_remote_copy(
            src_ref=x_hbm.at[index],
            dst_ref=other.at[index],
            send_sem=sent.at[index],
            recv_sem=received.at[index],
            device_id=partner,
            device_id_type=MESH,
        )

    @pl.when(cell == 0)
    def _():
        greet([partner])
        for index in range(cells):
            swap(index).start()
        w_t[...] = w[...].T
        gain_c[...] = spread_column(gain[...])
        bias_c[...] = spread_column(bias[...])

    def norms(columns, row, line):
        for h in range(HEADS):
            part = columns[h * head : (h + 1) * head]
            size = jnp.sum(part * part, 0, keepdims=True)
            best = size[:, :128]
            for start in range(128, columns.shape[1], 128):
                best = jnp.maximum(best, size[:, start : start + 128])
            stat[0, row, line + h : line + h + 1, :] = best

    def tables(values, half, origin):
        lows = []
        for first in range(0, genes, PIECE):
            span = slice(half * genes + first, half * genes + first + PIECE)
            unit, _ = norm_columns(values[first : first + PIECE].T.astype(F32))
            ut[0, :, span] = unit.astype(BF16)
            low = unit * widen(gain_c[...], PIECE) + widen(bias_c[...], PIECE)
            spot = origin + first + lax.broadcasted_iota(jnp.int32, (1, PIECE), 1)
            valid = spot < counts[cell]
            kept = jnp.where(valid, low, 0.0).astype(BF16)
            lows.append(low.astype(BF16))
            packed_t = dot(w_t[width:, :], kept)
            mark = jnp.where(
                (lax.broadcasted_iota(jnp.int32, (16, PIECE), 0) < MARKS) & valid, 1.0, 0.0
            ).astype(BF16)
            for h in range(HEADS):
                rows = slice(width + h * head, width + (h + 1) * head)
                va[0, h, :head, span] = packed_t[rows].astype(BF16)
                va[0, h, head:, span] = mark
            kr[0, span, :] = packed_t[:width].astype(BF16).T
            norms(packed_t[:width], half * (genes // PIECE) + first // PIECE, 0)
        return lows

    stat[...] = jnp.zeros_like(stat)
    for i, low in enumerate(tables(x[0], 0, place * genes)):
        query_t = dot(w_t[:width, :], low).astype(BF16) * (head**-0.5)
        qt[0, :, i * PIECE : (i + 1) * PIECE] = query_t
        norms(query_t.astype(F32), i, HEADS)
    unit, _ = norm_rows(xc[0].astype(F32))
    class_low = (unit * gain[...] + bias[...]).astype(BF16)
    pc[0] = dot(class_low, w[...]).astype(BF16).astype(F32)
    swap(cell).wait_recv()
    tables(other[cell], 1, (1 - place) * genes)

    @pl.when(cell == cells - 1)
    def _():
        for index in range(cells):
            swap(index).wait_send()


def project(counts, x, xc, gain, bias, w):
    cells, genes, width = x.shape
    total = 2 * genes
    classes = xc.shape[1]
    head = width // HEADS
    pieces = total // PIECE
    whole = lambda shape: pl.BlockSpec(shape, lambda c: (0,) * len(shape))
    per_cell = lambda *shape: pl.BlockSpec((1,) + shape, lambda c: (c,) + (0,) * len(shape))
    out = lambda shape, kind=BF16: jax.ShapeDtypeStruct(shape, kind)
    return pl.pallas_call(
        project_kernel,
        grid=(cells,),
        in_specs=[
            pl.BlockSpec(memory_space=pltpu.SMEM),
            per_cell(genes, width),
            pl.BlockSpec(memory_space=pl.ANY),
            per_cell(classes, width),
            whole((1, width)),
            whole((1, width)),
            whole((width, 3 * width)),
        ],
        out_specs=[
            per_cell(width, genes),
            per_cell(total, width),
            per_cell(HEADS, head + 16, total),
            per_cell(width, total),
            per_cell(pieces, 8, 128),
            per_cell(classes, 3 * width),
        ],
        out_shape=[
            out((cells, width, genes)),
            out((cells, total, width)),
            out((cells, HEADS, head + 16, total)),
            out((cells, width, total)),
            out((cells, pieces, 8, 128), F32),
            out((cells, classes, 3 * width), F32),
        ],
        scratch_shapes=[
            pltpu.VMEM((3 * width, width), BF16),
            pltpu.VMEM((width, 128), F32),
            pltpu.VMEM((width, 128), F32),
            pltpu.VMEM((cells, genes, width), BF16),
            pltpu.SemaphoreType.DMA((cells,)),
            pltpu.SemaphoreType.DMA((cells,)),
        ],
        compiler_params=pltpu.CompilerParams(
            vmem_limit_bytes=VMEM, collective_id=0, has_side_effects=True
        ),
        name="project",
    )(counts, x, x, xc, gain, bias, w)


def gelu_parts(u):
    phi = 0.5 + 0.5 * lax.erf(u * 0.7071067811865476)
    bell = jnp.exp2((u * u) * (-0.5 * LOG2E))
    return u * phi, phi + (u * 0.3989422804014327) * bell


def layer_kernel(
    counts,
    place,
    qt,
    kr,
    va,
    ut,
    stat,
    pc,
    x,
    xc,
    cot,
    cotc,
    w_out,
    gain,
    bias,
    w_up,
    b_up,
    w_down,
    b_down,
    y,
    yc,
    dq,
    dqc,
    dkv,
    dkvc,
    gm,
    gmc,
    slab,
    g_vec,
    w_out_t,
    w_up_t,
    w_down_t,
    gain_c,
    bias_c,
    b_up_c,
    b_down_c,
    probs,
    probs_ck,
    probs_cq,
    mix,
    shift,
    shift_q,
    inv_sum,
    qz,
    da,
    delta,
    att,
    datt,
    dq_t,
    grads_t,
    up_acc,
    g_down,
    g_out,
    qkv_acc,
    up_bias_acc,
    gain_acc,
    bias_acc,
    down_bias_acc,
    packed_sum,
    packed_cols,
    class_units,
    class_packs,
):
    cell = pl.program_id(0)
    cells = pl.num_programs(0)
    genes, width = x.shape[1:]
    classes = xc.shape[1]
    head = width // HEADS
    ff = w_up.shape[1]
    stack = HEADS * classes
    factor = head**-0.5
    count = counts[cell]
    own_count = jnp.clip(count - place[0] * genes, 0, genes)
    other_count = jnp.clip(count - (1 - place[0]) * genes, 0, genes)
    own_blocks = (own_count + (KB - 1)) // KB
    other_blocks = (other_count + (KB - 1)) // KB
    half_blocks = genes // KB
    blocks = own_blocks + other_blocks

    def nth_block(index):
        block = jnp.where(index < own_blocks, index, index - own_blocks + half_blocks)
        return pl.multiple_of(block * KB, KB)

    @pl.when(cell == 0)
    def _():
        w_out_t[...] = w_out[...].T
        w_up_t[...] = w_up[...].T
        w_down_t[...] = w_down[...].T
        gain_c[...] = spread_column(gain[...])
        bias_c[...] = spread_column(bias[...])
        b_up_c[...] = spread_column(b_up[...])
        b_down_c[...] = spread_column(b_down[...])
        up_acc[...] = jnp.zeros_like(up_acc)
        up_bias_acc[...] = jnp.zeros_like(up_bias_acc)
        gain_acc[...] = jnp.zeros_like(gain_acc)
        bias_acc[...] = jnp.zeros_like(bias_acc)
        down_bias_acc[...] = jnp.zeros_like(down_bias_acc)
        g_down[...] = jnp.zeros_like(g_down)
        g_out[...] = jnp.zeros_like(g_out)
        qkv_acc[...] = jnp.zeros_like(qkv_acc)
        packed_sum[...] = jnp.zeros_like(packed_sum)
        packed_cols[...] = jnp.zeros_like(packed_cols)

    head_mask = lax.broadcasted_iota(jnp.int32, (stack, width), 1) // head == (
        lax.broadcasted_iota(jnp.int32, (stack, width), 0) // classes
    )
    pair_mask = lax.broadcasted_iota(jnp.int32, (stack, stack), 1) // classes == (
        lax.broadcasted_iota(jnp.int32, (stack, stack), 0) // classes
    )

    def by_head(rows):
        return jnp.where(head_mask, jnp.concatenate([rows] * HEADS, 0), 0.0)

    def from_heads(rows):
        kept = jnp.where(head_mask, rows, 0.0)
        total = kept[:classes]
        for h in range(1, HEADS):
            total = total + kept[h * classes : (h + 1) * classes]
        return total

    packed_c = pc[0]
    query_c = by_head(packed_c[:, :width] * factor)
    key_c = by_head(packed_c[:, width : 2 * width])
    value_c = by_head(packed_c[:, 2 * width :])
    key_c_t = key_c.T.astype(BF16)
    value_c_t = value_c.T.astype(BF16)
    query_cb, key_cb, value_cb = query_c.astype(BF16), key_c.astype(BF16), value_c.astype(BF16)

    blank = jnp.zeros((head, genes), BF16)
    for h in range(HEADS):
        own = slice(h % 2 * head, (h % 2 + 1) * head)
        rest = slice((1 - h % 2) * head, (2 - h % 2) * head)
        qz[h, own, :] = qt[0, h * head : (h + 1) * head, :]
        qz[h, rest, :] = blank

    sizes = jnp.max(stat[0], 0)
    size_k, size_q = jnp.max(sizes[:HEADS]), jnp.max(sizes[HEADS:])
    size_k = jnp.maximum(size_k, jnp.max(jnp.sum(key_c * key_c, -1, keepdims=True)))
    size_q = jnp.maximum(size_q, jnp.max(jnp.sum(query_c * query_c, -1, keepdims=True)))
    safe = size_k * size_q < SAFE * SAFE

    def key_mask(start, shape, axis):
        limit = jnp.where(start < genes, own_count, genes + other_count)
        return start + lax.broadcasted_iota(jnp.int32, shape, axis) < limit

    shift[...] = jnp.zeros_like(shift)
    shift_q[...] = jnp.zeros_like(shift_q)

    @pl.when(jnp.logical_not(safe))
    def _():
        class_scores = dot(key_cb, qt[0])
        for h in range(HEADS):
            shift[h] = jnp.max(class_scores[h * classes : (h + 1) * classes], 0, keepdims=True)
        own_scores = jnp.where(pair_mask, dot(query_cb, key_c_t), -1e30)
        shift_q[...] = jnp.broadcast_to(jnp.max(own_scores, -1, keepdims=True), shift_q.shape)

        @pl.loop(0, blocks)
        def _(block):
            start = nth_block(block)
            for h in range(HEADS):
                scores = dot(
                    kr[0, pl.ds(start, KB), (h // 2) * 2 * head : (h // 2 + 1) * 2 * head], qz[h]
                )
                scores = jnp.where(key_mask(start, scores.shape, 0), scores, -1e30)
                shift[h] = jnp.maximum(shift[h], jnp.max(scores, 0, keepdims=True))
            scores = dot_nt(query_cb, kr[0, pl.ds(start, KB), :])
            scores = jnp.where(key_mask(start, scores.shape, 1), scores, -1e30)
            shift_q[...] = jnp.maximum(shift_q[...], jnp.max(scores, -1, keepdims=True))

        shift[...] = shift[...] * LOG2E
        shift_q[...] = shift_q[...] * LOG2E

    class_scores = dot(key_cb, qt[0])
    shift_rows = jnp.concatenate(
        [jnp.broadcast_to(shift[h], (classes, genes)) for h in range(HEADS)], 0
    )
    class_exp = jnp.exp2(class_scores * LOG2E - shift_rows).astype(BF16)
    probs_ck[...] = class_exp
    class_mix = dot(value_c_t, class_exp)
    for h in range(HEADS):
        mix[h, :head, :] = class_mix[h * head : (h + 1) * head]
        sums = jnp.sum(
            class_exp[h * classes : (h + 1) * classes].astype(F32), 0, keepdims=True
        )
        mix[h, head:, :] = jnp.where(
            lax.broadcasted_iota(jnp.int32, (16, genes), 0) == 0, sums, 0.0
        )
    shift_qc = shift_q[:, :1]
    own_exp = jnp.where(
        pair_mask, jnp.exp2(dot(query_cb, key_c_t) * LOG2E - shift_qc), 0.0
    ).astype(BF16)
    deep = head + 16

    def spread_heads(rows, extra):
        pieces = []
        for h in range(HEADS):
            pieces += [rows[:, h * head : (h + 1) * head], extra]
        return jnp.concatenate(pieces, 1)

    own_mix = spread_heads(
        dot(own_exp, value_cb),
        jnp.broadcast_to(jnp.sum(own_exp.astype(F32), -1, keepdims=True), (stack, 16)),
    )

    def forward_block(block, class_total, shifted):
        start = nth_block(block)
        keys = pl.ds(start, KB)
        scores = [
            dot(kr[0, keys, (h // 2) * 2 * head : (h // 2 + 1) * 2 * head], qz[h])
            for h in range(1)
        ]
        class_scores = dot_nt(query_cb, kr[0, keys, :]) * LOG2E - shift_qc
        all_values = va[0, :, :, keys].reshape(HEADS * deep, KB)
        for h in range(HEADS):
            if h + 1 < HEADS:
                g = h + 1
                scores.append(
                    dot(kr[0, keys, (g // 2) * 2 * head : (g // 2 + 1) * 2 * head], qz[g])
                )
            scaled = scores[h] * LOG2E
            if shifted:
                scaled = jnp.minimum(scaled - shift[h], 60.0)
            exps = jnp.exp2(scaled).astype(BF16)
            first = min(h * deep, HEADS * deep - 112)
            kept = slice(h * deep - first, (h + 1) * deep - first)
            mix[h] += dot(all_values[first : first + 112], exps)[kept]
            probs[h, :, keys] = exps.T
        class_exp = jnp.where(
            key_mask(start, class_scores.shape, 1), jnp.exp2(class_scores), 0.0
        ).astype(BF16)
        probs_cq[:, keys] = class_exp
        return class_total + dot_nt(class_exp, va[0, :, :, keys].reshape(HEADS * deep, KB))

    class_total = lax.cond(
        safe,
        lambda: paired_loop(blocks, functools.partial(forward_block, shifted=False), own_mix),
        lambda: lax.fori_loop(0, blocks, functools.partial(forward_block, shifted=True), own_mix),
    )
    class_sum = jnp.concatenate(
        [
            class_total[h * classes : (h + 1) * classes, h * deep + head : h * deep + head + 1]
            for h in range(HEADS)
        ],
        0,
    )
    class_total = jnp.concatenate(
        [class_total[:, h * deep : h * deep + head] for h in range(HEADS)], 1
    )
    class_inv = 1.0 / class_sum
    class_att = from_heads(class_total * class_inv)
    for h in range(HEADS):
        inverse = 1.0 / mix[h, head : head + 1, :]
        inv_sum[h] = inverse
        att[h * head : (h + 1) * head, :genes] = (mix[h, :head, :] * inverse).astype(BF16)

    def pad_rows(rows):
        return jnp.concatenate([rows, jnp.zeros((128 - rows.shape[0], width), F32)], 0)

    att[:, genes:] = pad_rows(class_att).T.astype(BF16)

    def feed(start, columns, with_class):
        lanes = columns + (128 if with_class else 0)
        span = pl.ds(start, lanes)
        wide_gain = widen(gain_c[...], lanes)
        cot_r = cot[0, pl.ds(start, columns), :]
        cot_t = cot_r.T
        x_t = x[0, pl.ds(start, columns), :].T
        if with_class:
            x_t = jnp.concatenate([x_t, pad_rows(xc[0].astype(F32)).T.astype(BF16)], 1)
            padded = pad_rows(cotc[0].astype(F32))
            cot_t = jnp.concatenate([cot_t, padded.T.astype(BF16)], 1)
            cot_r = jnp.concatenate([cot_r, (padded * 0.5).astype(BF16)], 0)
            share = jnp.where(
                lax.broadcasted_iota(jnp.int32, (1, lanes), 1) < columns, 1.0, 0.5
            )
            weigh = lambda values: values * share
            row_share = jnp.where(
                lax.broadcasted_iota(jnp.int32, (lanes, 1), 0) < columns, 1.0, 0.5
            )
            weigh_rows = lambda rows: (rows.astype(F32) * row_share).astype(BF16)
        else:
            weigh = lambda values: values
            weigh_rows = lambda rows: rows
        parts = [slice(first, first + FF_STEP) for first in range(0, ff, FF_STEP)]
        held = {}

        def begin():
            held["att"] = att[:, span]
            middle = x_t.astype(F32) + dot(w_out_t[...], held["att"])
            held["unit"], held["inverse"] = norm_columns(middle)
            held["low"] = (held["unit"] * wide_gain + widen(bias_c[...], lanes)).astype(BF16)
            held["low_r"] = weigh_rows(held["low"].T)
            held["result"] = middle + widen(b_down_c[...], lanes)
            held["back"] = jnp.zeros((width, lanes), F32)

        def rise(part):
            up = dot(w_up_t[part, :], held["low"]) + widen(b_up_c[part, :], lanes)
            held[part.start] = up, dot(w_down[part, :], cot_t)

        def fall(part):
            up, grad_act = held.pop(part.start)
            active, slope = gelu_parts(up)
            active = active.astype(BF16)
            grad_up = slope * grad_act
            up_bias_acc[part, :] += fold_lanes(weigh(grad_up))
            grad_up = grad_up.astype(BF16)
            held["result"] += dot(w_down_t[:, part], active)
            held["back"] += dot(w_up[:, part], grad_up)
            g_down[part, :] += dot(active, cot_r)
            up_acc[part, :] += dot(grad_up, held["low_r"])

        def end():
            back, unit = held["back"], held["unit"]
            scaled = back * wide_gain
            scale = 1.0 / width
            grad_middle = cot_t.astype(F32) + held["inverse"] * (
                scaled
                - jnp.sum(scaled, 0, keepdims=True) * scale
                - unit * (jnp.sum(scaled * unit, 0, keepdims=True) * scale)
            )
            grad_middle = grad_middle.astype(BF16)
            datt[:, span] = dot(w_out[...], grad_middle).astype(BF16)
            gain_acc[...] += fold_lanes(weigh(back * unit))
            bias_acc[...] += fold_lanes(weigh(back))
            middle_r = grad_middle.T
            g_out[...] += dot(held["att"], weigh_rows(middle_r))
            down_bias_acc[...] += jnp.sum(cot_r.astype(F32), 0, keepdims=True)
            result_r = held["result"].T
            y[0, pl.ds(start, columns), :] = result_r[:columns].astype(BF16)
            gm[0, pl.ds(start, columns), :] = middle_r[:columns]
            if with_class:
                yc[0] = result_r[columns : columns + classes].astype(BF16)
                gmc[0] = middle_r[columns:].astype(F32)[:classes]

        rises = [begin] + [functools.partial(rise, part) for part in parts]
        falls = [functools.partial(fall, part) for part in parts] + [end]
        return rises, falls

    feed_step = 512
    pieces = genes // feed_step
    rises, falls = [], []
    for piece in range(pieces):
        more_rises, more_falls = feed(piece * feed_step, feed_step, piece == pieces - 1)
        rises += more_rises
        falls += more_falls
    for i in range(len(rises) + FEED_AHEAD):
        if i < len(rises):
            rises[i]()
        if i >= FEED_AHEAD:
            falls[i - FEED_AHEAD]()

    for h in range(HEADS):
        own = slice(h * head, (h + 1) * head)
        inverse = inv_sum[h]
        grad = (datt[own, :genes].astype(F32) * inverse).astype(BF16)
        row_delta = jnp.sum(grad.astype(F32) * (mix[h, :head, :] * inverse), 0, keepdims=True)
        delta[h] = row_delta
        datt[own, :genes] = grad
        parts = jnp.zeros((16, genes), F32)
        rest = row_delta
        for i in range(MARKS):
            piece = rest.astype(BF16).astype(F32)
            rest = rest - piece
            parts = jnp.where(
                lax.broadcasted_iota(jnp.int32, (16, genes), 0) == i, -piece, parts
            )
        blank = jnp.zeros((2 * head - deep, genes), BF16)
        da[h] = jnp.concatenate([grad, parts.astype(BF16), blank], 0).T

    class_grad = datt[:, genes:].astype(F32).T[:classes]
    class_grad = by_head(class_grad) * class_inv
    class_grad_b = class_grad.astype(BF16)
    class_grad_h = (class_grad * 0.5).astype(BF16)
    query_ch = (query_c * 0.5).astype(BF16)
    class_delta = jnp.sum(
        class_grad_b.astype(F32) * (class_total * class_inv), -1, keepdims=True
    )

    class_dprob = dot(value_cb, datt[:, :genes])
    delta_rows = jnp.concatenate(
        [jnp.broadcast_to(delta[h], (classes, genes)) for h in range(HEADS)], 0
    )
    class_probs = probs_ck[...]
    class_dscore = (class_probs.astype(F32) * (class_dprob - delta_rows)).astype(BF16)
    dq_t[...] = dot(key_c_t, class_dscore)
    class_dkey = dot_nt(class_dscore, qt[0])
    class_dvalue = dot_nt(class_probs, datt[:, :genes])
    own_dprob = dot(class_grad_b, value_c_t)
    own_dscore = (own_exp.astype(F32) * (own_dprob - class_delta)).astype(BF16)
    class_dquery = dot(own_dscore, key_cb)
    class_dkey = class_dkey + dot(own_dscore.astype(F32).T.astype(BF16), query_ch)
    class_dvalue = class_dvalue + dot(own_exp.astype(F32).T.astype(BF16), class_grad_h)

    class_grad_s = spread_heads(class_grad_b, jnp.zeros((stack, 16), BF16))
    class_grad_ht = class_grad_h.T
    query_ct = query_ch.T

    def settle(start):
        keys = pl.ds(pl.multiple_of(start, KB), KB)
        grads = grads_t[...].T
        dkv[0, keys, :] = grads
        qkv_acc[:, width:] += dot(ut[0, :, keys], grads)

    def backward_block(block, carried):
        class_dquery, previous = carried
        start = nth_block(block)
        keys = pl.ds(start, KB)
        dprobs = [dot(da[h, :, :deep], va[0, h, :, keys]) for h in range(AHEAD)]
        settle(previous)
        class_weights = probs_cq[:, keys]
        class_dprob = dot(class_grad_s, va[0, :, :, keys].reshape(HEADS * deep, KB))
        class_dscore = (class_weights.astype(F32) * (class_dprob - class_delta)).astype(BF16)
        dkeys, dvalues, dscores = [], [], []
        key_t = kr[0, keys, :].T
        for h in range(HEADS + 1):
            if h + AHEAD < HEADS:
                dprobs.append(dot(da[h + AHEAD, :, :deep], va[0, h + AHEAD, :, keys]))
            if h < HEADS:
                weights = probs[h, :, keys]
                dscore = weights * dprobs[h].astype(BF16)
                dscores.append(dscore)
                spot = slice(h % 2 * 2, h % 2 * 2 + 2)
                qz[spot] = dscore.T.reshape(2, KB // 2, genes)
                own = slice(h * head, (h + 1) * head)
                pair = slice((h // 2) * 2 * head, (h // 2 + 1) * 2 * head)
                kept = slice(h % 2 * head, (h % 2 + 1) * head)
                dvalues.append(dot(datt[pair, :genes], weights)[kept])
                dkeys.append(dot(qt[0, pair, :], dscore)[kept])
            if h > 0:
                own = slice((h - 1) * head, h * head)
                spot = slice((h - 1) % 2 * 2, (h - 1) % 2 * 2 + 2)
                pair = slice(((h - 1) // 2) * 2 * head, ((h - 1) // 2 + 1) * 2 * head)
                kept = slice((h - 1) % 2 * head, ((h - 1) % 2 + 1) * head)
                dq_t[own, :] += dot(key_t[pair, :], qz[spot].reshape(KB, genes))[kept]
        class_dquery = class_dquery + dot(class_dscore, kr[0, keys, :])
        dkey = jnp.concatenate(dkeys, 0) + dot(query_ct, class_dscore)
        dvalue = jnp.concatenate(dvalues, 0) + dot(class_grad_ht, class_weights)
        valid = key_mask(start, (1, KB), 1)
        grads = jnp.where(valid, jnp.concatenate([dkey, dvalue], 0), 0.0)
        packed_cols[...] += fold_lanes(grads)
        grads_t[...] = grads.astype(BF16)
        return class_dquery, start

    grads_t[...] = jnp.zeros_like(grads_t)
    class_dquery, previous = paired_loop(
        blocks, backward_block, (class_dquery, nth_block(0))
    )
    settle(previous)

    def blank_rows(block):
        dkv[0, pl.ds(pl.multiple_of(block * KB, KB), KB), :] = jnp.zeros((KB, 2 * width), BF16)

    pl.loop(own_blocks, half_blocks)(blank_rows)
    pl.loop(half_blocks + other_blocks, 2 * half_blocks)(blank_rows)

    dquery_r = (dq_t[...] * factor).astype(BF16).T
    dq[0] = dquery_r
    qkv_acc[:, :width] += dot(ut[0, :, :genes], dquery_r)
    class_dquery = from_heads(class_dquery) * factor
    class_dkv = jnp.concatenate([from_heads(class_dkey), from_heads(class_dvalue)], 1)
    dqc[0] = class_dquery
    dkvc[0] = class_dkv
    class_packed = jnp.concatenate([class_dquery * 0.5, class_dkv], 1)
    class_unit, _ = norm_rows(xc[0].astype(F32))
    class_lines = pl.ds(pl.multiple_of(cell * classes, classes), classes)
    class_units[class_lines, :] = class_unit
    class_packs[class_lines, :] = class_packed
    packed_sum[:, :width] += jnp.sum(dquery_r.astype(F32), 0, keepdims=True)
    packed_sum[...] += jnp.sum(class_packed, 0, keepdims=True)

    @pl.when(cell == cells - 1)
    def _():
        first = 0

        def put(values):
            nonlocal first
            rows = values.shape[0]
            for start in range(0, values.shape[1], 128):
                slab[first : first + rows, :] = values[:, start : start + 128].astype(BF16)
                first += rows

        qkv_acc[...] += dot(
            class_units[...].T.astype(BF16), class_packs[...].astype(BF16)
        )
        put(up_acc[...].T)
        put(g_down[...])
        put(g_out[...])
        put(qkv_acc[...])
        if first < slab.shape[0]:
            slab[first:, :] = jnp.zeros((slab.shape[0] - first, 128), BF16)
        g_vec[...] = jnp.zeros_like(g_vec)
        line = 0
        for vector in (
            jnp.sum(up_bias_acc[...].T, 0, keepdims=True),
            jnp.sum(gain_acc[...].T, 0, keepdims=True),
            jnp.sum(bias_acc[...].T, 0, keepdims=True),
            down_bias_acc[...],
            packed_sum[...]
            + jnp.concatenate(
                [jnp.zeros((1, width), F32), jnp.sum(packed_cols[...].T, 0, keepdims=True)], 1
            ),
        ):
            for start in range(0, vector.shape[1], 128):
                g_vec[line : line + 1, :] = vector[:, start : start + 128]
                line += 1


def layer(
    counts, place, tables, x, xc, cot, cotc, w_out, gain, bias, w_up, b_up, w_down, b_down
):
    cells, genes, width = x.shape
    classes = xc.shape[1]
    total = tables[1].shape[1]
    head = width // HEADS
    ff = w_up.shape[1]
    stack = HEADS * classes
    slab_rows = Reduction.padded((2 * ff + 4 * width) * width // 128, lax.axis_size("cell"))
    whole = lambda shape: pl.BlockSpec(
        shape, lambda c, *_: (0,) * len(shape), pipeline_mode=pl.Buffered(1)
    )
    per_cell = lambda *shape: pl.BlockSpec((1,) + shape, lambda c, *_: (c,) + (0,) * len(shape))
    kept = lambda *shape: whole(shape)
    out = lambda shape, kind=BF16: jax.ShapeDtypeStruct(shape, kind)
    vmem = lambda *shape, kind=BF16: pltpu.VMEM(shape, kind)
    f32 = functools.partial(vmem, kind=F32)
    return pl.pallas_call(
        layer_kernel,
        grid_spec=pltpu.PrefetchScalarGridSpec(
            num_scalar_prefetch=2,
            grid=(cells,),
            in_specs=[
                per_cell(width, genes),
                per_cell(total, width),
                per_cell(HEADS, head + 16, total),
                per_cell(width, total),
                per_cell(total // PIECE, 8, 128),
                per_cell(classes, 3 * width),
                per_cell(genes, width),
                per_cell(classes, width),
                per_cell(genes, width),
                per_cell(classes, width),
                whole((width, width)),
                whole((1, width)),
                whole((1, width)),
                whole((width, ff)),
                whole((1, ff)),
                whole((ff, width)),
                whole((1, width)),
            ],
            out_specs=[
                per_cell(genes, width),
                per_cell(classes, width),
                per_cell(genes, width),
                per_cell(classes, width),
                per_cell(total, 2 * width),
                per_cell(classes, 2 * width),
                per_cell(genes, width),
                per_cell(classes, width),
                kept(slab_rows, 128),
                kept(VECTOR_ROWS, 128),
            ],
            scratch_shapes=[
                vmem(width, width),
                vmem(ff, width),
                vmem(width, ff),
                f32(width, 128),
                f32(width, 128),
                f32(ff, 128),
                f32(width, 128),
                vmem(HEADS, genes, total),
                vmem(stack, genes),
                vmem(stack, total),
                f32(HEADS, head + 16, genes),
                f32(HEADS, 1, genes),
                f32(stack, 128),
                f32(HEADS, 1, genes),
                vmem(HEADS, 2 * head, genes),
                vmem(HEADS, genes, 2 * head),
                f32(HEADS, 1, genes),
                vmem(width, genes + 128),
                vmem(width, genes + 128),
                f32(width, genes),
                vmem(2 * width, KB),
                f32(ff, width),
                f32(ff, width),
                f32(width, width),
                f32(width, 3 * width),
                f32(ff, 128),
                f32(width, 128),
                f32(width, 128),
                f32(1, width),
                f32(1, 3 * width),
                f32(2 * width, 128),
                f32(cells * classes, width),
                f32(cells * classes, 3 * width),
            ],
        ),
        out_shape=[
            out((cells, genes, width)),
            out((cells, classes, width)),
            out((cells, genes, width)),
            out((cells, classes, width), F32),
            out((cells, total, 2 * width)),
            out((cells, classes, 2 * width), F32),
            out((cells, genes, width)),
            out((cells, classes, width), F32),
            out((slab_rows, 128)),
            out((VECTOR_ROWS, 128), F32),
        ],
        compiler_params=pltpu.CompilerParams(vmem_limit_bytes=VMEM),
        name="layer",
    )(counts, place, *tables, x, xc, cot, cotc, w_out, gain, bias, w_up, b_up, w_down, b_down)


class Reduction:
    @staticmethod
    def groups(cells):
        bits = (cells - 1).bit_length()
        return [(shift, min(2, bits - shift)) for shift in range(0, bits, 2)]

    @staticmethod
    def streams(rows, cells):
        groups = Reduction.groups(cells)
        unit = 2 * 16 * cells
        units = -(-rows // unit)
        kinds = min(len(groups), units)
        shares = [units // kinds] * kinds
        if kinds == 2:
            shares[1] = max(1, units // 3)
        shares[0] = units - sum(shares[1:])
        result, first = [], 0
        for turn in range(CUTS):
            for i, share in enumerate(shares):
                share = share * (turn + 1) // CUTS - share * turn // CUTS
                if share:
                    result.append((first, share * unit, groups[i:] + groups[:i]))
                    first += share * unit
        return result

    @staticmethod
    def padded(rows, cells):
        first, size, _ = Reduction.streams(rows, cells)[-1]
        return first + size

    @staticmethod
    def scratch(rows, cells):
        rows = Reduction.padded(rows, cells)
        hops = 2 + 2 * sum((1 << bits) - 1 for _, bits in Reduction.groups(cells))
        sems = (len(Reduction.streams(rows, cells)), hops)
        return [
            pltpu.VMEM((rows // 2, 128), BF16),
            pltpu.VMEM((rows, 128), BF16),
            pltpu.VMEM((rows, 128), BF16),
            pltpu.SemaphoreType.DMA(sems),
            pltpu.SemaphoreType.DMA(sems),
        ]

    def __init__(self, source, cells, work, inbox, total, sent, received):
        self.source, self.work, self.inbox, self.total = source, work, inbox, total
        self.sent, self.received = sent, received
        self.plan = self.streams(source.shape[0], cells)
        self.depth = len(self.groups(cells))
        self.stages = 2 * self.depth + 3
        self.me, self.place = lax.axis_index("cell"), lax.axis_index("gene")

    def peer(self, group, ahead):
        shift, bits = group
        radix = 1 << bits
        digit = (self.me // (1 << shift)) % radix
        there = (digit + ahead) % radix
        return {"cell": self.me + (there - digit) * (1 << shift), "gene": self.place}, there

    def digit(self, group):
        return (self.me // (1 << group[0])) % (1 << group[1])

    def held(self, stream, level):
        _, rows, order = self.plan[stream]
        first, size = 0, rows // 2
        for group in order[:level]:
            size = size >> group[1]
            first = first + self.digit(group) * size
        return first, size

    def slot(self, stream, level):
        first, rows, order = self.plan[stream]
        size = rows // 2
        spot = first
        for i in range(level):
            spot += size if i == 0 else ((1 << order[i - 1][1]) - 1) * size
            size = size >> order[i][1] if i < len(order) else size
        return spot

    def copy(self, source, target, stream, hop, ahead, device):
        return pltpu.make_async_remote_copy(
            src_ref=source,
            dst_ref=target,
            send_sem=self.sent.at[stream, hop + ahead - 1],
            recv_sem=self.received.at[stream, hop + ahead - 1],
            device_id=device,
            device_id_type=MESH,
        )

    def hop(self, stream, index):
        peers = [1] + [(1 << bits) - 1 for _, bits in self.plan[stream][2]]
        return sum((peers + peers[::-1])[:index])

    def rows(self, first, size):
        return pl.ds(pl.multiple_of(first, 16), size)

    def scatter(self, stream, level):
        first, rows, order = self.plan[stream]
        half = rows // 2
        if level == 0:
            mate = {"cell": self.me, "gene": 1 - self.place}
            source = self.source.at[self.rows(first + (1 - self.place) * half, half), :]
            target = self.inbox.at[pl.ds(first, half), :]
            return [self.copy(source, target, stream, 0, 1, mate)]
        group = order[level - 1]
        start, size = self.held(stream, level - 1)
        size = size >> group[1]
        copies = []
        for ahead in range(1, 1 << group[1]):
            device, there = self.peer(group, ahead)
            source = self.work.at[self.rows(first // 2 + start + there * size, size), :]
            target = self.inbox.at[pl.ds(self.slot(stream, level) + (ahead - 1) * size, size), :]
            copies.append(self.copy(source, target, stream, self.hop(stream, level), ahead, device))
        return copies

    def add(self, stream, level):
        first, rows, order = self.plan[stream]
        half = rows // 2
        start, size = self.held(stream, level)
        if level == 0:
            value = self.source[self.rows(first + self.place * half, half), :].astype(F32)
            count = 1
        else:
            value = self.work[self.rows(first // 2 + start, size), :].astype(F32)
            count = (1 << order[level - 1][1]) - 1
        for i in range(count):
            value += self.inbox[pl.ds(self.slot(stream, level) + i * size, size), :].astype(F32)
        if level == self.depth:
            self.total[self.rows(first + self.place * half + start, size), :] = value.astype(BF16)
        else:
            self.work[self.rows(first // 2 + start, size), :] = value.astype(BF16)

    def gather(self, stream, level):
        first, rows, order = self.plan[stream]
        half = rows // 2
        start, size = self.held(stream, level)
        span = self.total.at[self.rows(first + self.place * half + start, size), :]
        hop = self.hop(stream, 2 * self.depth + 1 - level)
        if level == 0:
            mate = {"cell": self.me, "gene": 1 - self.place}
            return [self.copy(span, span, stream, hop, 1, mate)]
        group = order[level - 1]
        return [
            self.copy(span, span, stream, hop, ahead, self.peer(group, ahead)[0])
            for ahead in range(1, 1 << group[1])
        ]

    def copies(self, stream, index):
        if index <= self.depth:
            return self.scatter(stream, index)
        return self.gather(stream, 2 * self.depth + 1 - index)

    def stage(self, index):
        for stream in range(len(self.plan)):
            if index > 0:
                for copy in self.copies(stream, index - 1):
                    copy.wait()
                if index - 1 <= self.depth:
                    self.add(stream, index - 1)
            if index < self.stages - 1:
                for copy in self.copies(stream, index):
                    copy.start()


class VectorSum:
    @staticmethod
    def scratch(shape, cells):
        groups = Reduction.groups(cells)
        return [
            pltpu.VMEM((2 + sum(1 << bits for _, bits in groups),) + shape, F32),
            pltpu.SemaphoreType.DMA((len(groups) + 1, 3)),
            pltpu.SemaphoreType.DMA((len(groups) + 1, 3)),
        ]

    def __init__(self, cells, reduction, slots, sent, received):
        self.reduction, self.slots, self.sent, self.received = reduction, slots, sent, received
        self.groups = reduction.groups(cells)

    def first(self, level):
        return 0 if level == 0 else 2 + sum(1 << bits for _, bits in self.groups[: level - 1])

    def size(self, level):
        return 2 if level == 0 else 1 << self.groups[level - 1][1]

    def copies(self, level):
        r = self.reduction
        if level == 0:
            mine = r.place
            devices = [{"cell": r.me, "gene": 1 - r.place}]
        else:
            group = self.groups[level - 1]
            mine = r.digit(group)
            devices = [r.peer(group, ahead)[0] for ahead in range(1, self.size(level))]
        spot = self.slots.at[self.first(level) + mine]
        return mine, [
            pltpu.make_async_remote_copy(
                src_ref=spot,
                dst_ref=spot,
                send_sem=self.sent.at[level, i],
                recv_sem=self.received.at[level, i],
                device_id=device,
                device_id_type=MESH,
            )
            for i, device in enumerate(devices)
        ]

    def start(self, level, value):
        mine, copies = self.copies(level)
        self.slots[self.first(level) + mine] = value
        for copy in copies:
            copy.start()

    def finish(self, level):
        for copy in self.copies(level)[1]:
            copy.wait()
        first = self.first(level)
        total = self.slots[first]
        for i in range(1, self.size(level)):
            total = total + self.slots[first + i]
        return total

    def stage(self, index, value):
        levels = len(self.groups)
        if 0 < index <= levels + 1:
            value = self.finish(index - 1)
        if index <= levels:
            self.start(index, value)
        return value if index == levels + 1 else None


def finish_kernel(
    slab,
    vec,
    x,
    gm,
    dq,
    dkv,
    dkv_hbm,
    xc,
    gmc,
    dqc,
    dkvc,
    gain,
    bias,
    w,
    g_x,
    g_xc,
    slab_out,
    vec_out,
    w_t,
    other,
    other_c,
    swap_send,
    swap_recv,
    class_send,
    class_recv,
    *reduction_scratch,
):
    step, steps = pl.program_id(0), pl.num_programs(0)
    cells = dkv_hbm.shape[0]
    genes = dkv_hbm.shape[1] // 2
    rows, width = x.shape[1:]
    classes = xc.shape[1]
    per_cell = genes // rows
    all_cells = lax.axis_size("cell")
    sums = Reduction(slab, all_cells, *reduction_scratch[:5])
    vectors = VectorSum(all_cells, sums, *reduction_scratch[5:])
    mate = {"cell": sums.me, "gene": 1 - sums.place}

    def swap(cell):
        return pltpu.make_async_remote_copy(
            src_ref=dkv_hbm.at[cell, pl.ds(genes, genes), :],
            dst_ref=other.at[cell],
            send_sem=swap_send.at[cell],
            recv_sem=swap_recv.at[cell],
            device_id=mate,
            device_id_type=MESH,
        )

    def swap_class():
        return pltpu.make_async_remote_copy(
            src_ref=dkvc,
            dst_ref=other_c,
            send_sem=class_send,
            recv_sem=class_recv,
            device_id=mate,
            device_id_type=MESH,
        )

    def stage(index):
        sums.stage(index)
        done = vectors.stage(index, vec[...] if index == 0 else None)
        if done is not None:
            vec_out[...] = done

    def rows_back(values, grads, packed):
        unit, inverse = norm_rows(values)
        scaled = dot(packed, w_t[...]) * gain[...]
        return grads + inverse * (
            scaled
            - jnp.mean(scaled, -1, keepdims=True)
            - unit * jnp.mean(scaled * unit, -1, keepdims=True)
        )

    for index, at in enumerate(STAGES):

        @pl.when(step == at)
        def _(index=index):
            if index == 0:
                partners = [mate]
                for group in sums.groups(all_cells):
                    for ahead in range(1, 1 << group[1]):
                        partners.append(sums.peer(group, ahead)[0])
                greet(partners)
            stage(index)
            if index == 0:
                for cell in range(cells):
                    swap(cell).start()
                swap_class().start()
                w_t[...] = w[...].T

    cell = step // per_cell

    @pl.when(step % per_cell == 0)
    def _():
        swap(cell).wait()

    grads = dkv[0].astype(F32) + other[
        cell, pl.ds(pl.multiple_of((step % per_cell) * rows, 16), rows), :
    ].astype(F32)
    packed = jnp.concatenate([dq[0], grads.astype(BF16)], 1)
    g_x[0] = rows_back(x[0].astype(F32), gm[0].astype(F32), packed).astype(BF16)

    @pl.when(step == steps - 1)
    def _():
        swap_class().wait()
        class_grads = dkvc[...] + other_c[...]
        stack = cells * classes
        packed = jnp.concatenate([dqc[...], class_grads], 2).reshape(stack, 3 * width)
        values = xc[...].astype(F32).reshape(stack, width)
        result = rows_back(values, gmc[...].reshape(stack, width), packed.astype(BF16))
        g_xc[...] = result.reshape(cells, classes, width)
        for index in range(len(STAGES), sums.stages):
            stage(index)
        slab_out[...] = sums.total[...]


def finish(slab, vec, x, xc, gm, gmc, dq, dqc, dkv, dkvc, gain, bias, w):
    cells, genes, width = x.shape
    classes = xc.shape[1]
    rows = genes // 2
    per_cell = genes // rows
    all_cells = lax.axis_size("cell")
    whole = lambda array: pl.BlockSpec(array.shape, lambda i: (0,) * array.ndim)
    piece = lambda lanes: pl.BlockSpec((1, rows, lanes), lambda i: (i // per_cell, i % per_cell, 0))
    out = lambda shape, kind=BF16: jax.ShapeDtypeStruct(shape, kind)
    dma = lambda *shape: pltpu.SemaphoreType.DMA(shape)
    outs = [
        out((cells, genes, width)),
        out((cells, classes, width), F32),
        out(slab.shape),
        out(vec.shape, F32),
    ]
    return pl.pallas_call(
        finish_kernel,
        grid=(cells * per_cell,),
        in_specs=[
            whole(slab),
            whole(vec),
            piece(width),
            piece(width),
            piece(width),
            piece(2 * width),
            pl.BlockSpec(memory_space=pl.ANY),
            whole(xc),
            whole(gmc),
            whole(dqc),
            whole(dkvc),
            whole(gain),
            whole(bias),
            whole(w),
        ],
        out_specs=[piece(width)] + [whole(o) for o in outs[1:]],
        out_shape=outs,
        scratch_shapes=[
            pltpu.VMEM((3 * width, width), BF16),
            pltpu.VMEM((cells, genes, 2 * width), BF16),
            pltpu.VMEM(dkvc.shape, F32),
            dma(cells),
            dma(cells),
            dma(),
            dma(),
        ]
        + Reduction.scratch(slab.shape[0], all_cells)
        + VectorSum.scratch(vec.shape, all_cells),
        compiler_params=pltpu.CompilerParams(
            vmem_limit_bytes=VMEM, collective_id=1, has_side_effects=True
        ),
        name="finish",
    )(slab, vec, x, gm, dq, dkv, dkv, xc, gmc, dqc, dkvc, gain, bias, w)


def unpack_kernel(slab, vec, gain, bias, w, x, xc, g_x, g_up, g_down, g_out, g_qkv, g_xc, *rest):
    *vectors, up, down, out, qkv, passing, sems = rest
    width, ff = up.shape
    copies = [
        pltpu.make_async_copy(source, target, sems.at[i])
        for i, (source, target) in enumerate(
            [(x, passing), (up, g_up), (down, g_down), (out, g_out), (qkv, g_qkv), (passing, g_x)]
        )
    ]
    copies[0].start()
    first = 0

    def take(target):
        nonlocal first
        rows = target.shape[0]
        for start in range(0, target.shape[1], 128):
            target[:, start : start + 128] = slab[first : first + rows, :].astype(F32)
            first += rows

    for copy, target in zip(copies[1:4], (up, down, out)):
        take(target)
        copy.start()
    copies[0].wait()
    copies[5].start()
    take(qkv)
    line = 0

    def lines(count):
        nonlocal line
        line += count
        return jnp.concatenate([vec[i : i + 1, :] for i in range(line - count, line)], 1)

    up_bias, ln2_gain, ln2_bias, down_bias, ln1_gain, ln1_bias = vectors
    up_bias[...] = lines(ff // 128)
    ln2_gain[...] = lines(width // 128)
    ln2_bias[...] = lines(width // 128)
    down_bias[...] = lines(width // 128)
    packed_sum = lines(3 * width // 128)
    weights = w[...].astype(F32)
    sums = qkv[...]
    qkv[...] = (
        widen(spread_column(gain[...]), 3 * width) * sums
        + widen(spread_column(bias[...]), 3 * width) * packed_sum
    )
    copies[4].start()
    ln1_gain[...] = jnp.sum((weights * sums).T, 0, keepdims=True)
    ln1_bias[...] = jnp.sum((weights * packed_sum).T, 0, keepdims=True)
    g_xc[...] = xc[...].astype(BF16)
    for copy in copies[1:]:
        copy.wait()


def unpack(slab, vec, gain, bias, w, x, xc, ff):
    width = w.shape[0]
    out = lambda *shape: jax.ShapeDtypeStruct(shape, F32)
    row = out(1, width)
    sums = [(width, ff), (ff, width), (width, width), (width, 3 * width)]
    anywhere = pl.BlockSpec(memory_space=pl.ANY)
    local = pl.BlockSpec(memory_space=pltpu.VMEM)
    return pl.pallas_call(
        unpack_kernel,
        in_specs=[local] * 5 + [anywhere, local],
        out_specs=[anywhere] * 5 + [local] * 7,
        out_shape=[jax.ShapeDtypeStruct(x.shape, BF16)]
        + [out(*shape) for shape in sums]
        + [jax.ShapeDtypeStruct(xc.shape, BF16), out(1, ff), row, row, row, row, row],
        scratch_shapes=[pltpu.VMEM(shape, F32) for shape in sums]
        + [pltpu.VMEM(x.shape, BF16), pltpu.SemaphoreType.DMA((6,))],
        compiler_params=pltpu.CompilerParams(vmem_limit_bytes=VMEM),
        name="unpack",
    )(slab, vec, gain, bias, w, x, xc)


def shards(
    gene_in,
    class_in,
    expressed,
    ln1_gain,
    ln1_bias,
    w_qkv,
    w_out,
    ln2_gain,
    ln2_bias,
    w_up,
    b_up,
    w_down,
    b_down,
    gene_cot,
    class_cot,
):
    row = lambda vector: vector.reshape(1, -1)
    place = lax.axis_index("gene").reshape(1)
    gain1, bias1 = row(ln1_gain), row(ln1_bias)
    tables = project(expressed, gene_in, class_in, gain1, bias1, w_qkv)
    gene_out, class_out, dq, dqc, dkv, dkvc, gm, gmc, slab, vec = layer(
        expressed,
        place,
        tables,
        gene_in,
        class_in,
        gene_cot,
        class_cot,
        w_out,
        row(ln2_gain),
        row(ln2_bias),
        w_up,
        row(b_up),
        w_down,
        row(b_down),
    )
    gene_grad, class_grad, slab, vec = finish(
        slab, vec, gene_in, class_in, gm, gmc, dq, dqc, dkv, dkvc, gain1, bias1, w_qkv
    )
    (
        gene_grad,
        g_up,
        g_down,
        g_out,
        g_qkv,
        class_grad,
        g_b_up,
        g_gain2,
        g_bias2,
        g_b_down,
        g_gain1,
        g_bias1,
    ) = unpack(slab, vec, gain1, bias1, w_qkv, gene_grad, class_grad, w_up.shape[1])
    return (
        gene_out,
        class_out,
        gene_grad,
        class_grad,
        g_gain1[0],
        g_bias1[0],
        g_qkv,
        g_out,
        g_gain2[0],
        g_bias2[0],
        g_up,
        g_b_up[0],
        g_down,
        g_b_down[0],
    )


def solution(mesh):
    genes, cells, whole = P("cell", "gene", None), P("cell", None, None), P()
    return jax.shard_map(
        shards,
        mesh=mesh,
        in_specs=(genes, cells, P("cell")) + (whole,) * 10 + (genes, cells),
        out_specs=(genes, cells, genes, cells) + (whole,) * 10,
        check_vma=False,
    )
```

```python
import functools

import jax
import jax.numpy as jnp
from jax import lax
from jax.experimental import pallas as pl
from jax.experimental.pallas import tpu as pltpu
from jax.sharding import PartitionSpec as P

HEADS = 4
EPS = 1e-05
LOG2E = 1.4426950408889634
SAFE = 40.0
KB = 256
PIECE = 512
FF_STEP = 512
FEED_AHEAD = 2
AHEAD = 2
MARKS = 3
VECTOR_ROWS = 32
CUTS = 2
STAGES = (0, 1, 4, 7)
VMEM = 63 * 2**20
F32 = jnp.float32
BF16 = jnp.bfloat16
MESH = pl.DeviceIdType.MESH


def dot(left, right):
    return jnp.dot(left, right, preferred_element_type=F32)


def dot_nt(left, right):
    return lax.dot_general(left, right, (((1,), (1,)), ((), ())), preferred_element_type=F32)


def dot_tn(left, right):
    return lax.dot_general(left, right, (((0,), (0,)), ((), ())), preferred_element_type=F32)


def spread_column(row):
    return jnp.broadcast_to(row, (128, row.shape[1])).T


def widen(column, lanes):
    return jnp.concatenate([column] * (lanes // 128), axis=1)


def fold_lanes(values):
    total = values[:, :128]
    for start in range(128, values.shape[1], 128):
        total = total + values[:, start : start + 128]
    return total


def paired_loop(count, body, carried):
    carried = lax.fori_loop(
        0, count // 2, lambda i, value: body(2 * i + 1, body(2 * i, value)), carried
    )
    return lax.fori_loop(count // 2 * 2, count, body, carried)


def norm_rows(values):
    centered = values - jnp.mean(values, -1, keepdims=True)
    inverse = lax.rsqrt(jnp.mean(centered * centered, -1, keepdims=True) + EPS)
    return centered * inverse, inverse


def norm_columns(values):
    scale = 1.0 / values.shape[0]
    centered = values - jnp.sum(values, 0, keepdims=True) * scale
    inverse = lax.rsqrt(jnp.sum(centered * centered, 0, keepdims=True) * scale + EPS)
    return centered * inverse, inverse


def greet(partners):
    barrier = pltpu.get_barrier_semaphore()
    for partner in partners:
        pl.semaphore_signal(barrier, inc=1, device_id=partner, device_id_type=MESH)
    pl.semaphore_wait(barrier, len(partners))


def project_kernel(
    counts,
    x,
    x_hbm,
    xc,
    gain,
    bias,
    w,
    qt,
    kr,
    va,
    ut,
    stat,
    pc,
    w_t,
    gain_c,
    bias_c,
    other,
    sent,
    received,
):
    cell = pl.program_id(0)
    cells = x_hbm.shape[0]
    genes, width = x.shape[1:]
    head = width // HEADS
    place = lax.axis_index("gene")
    partner = {"cell": lax.axis_index("cell"), "gene": 1 - place}

    def swap(index):
        return pltpu.make_async_remote_copy(
            src_ref=x_hbm.at[index],
            dst_ref=other.at[index],
            send_sem=sent.at[index],
            recv_sem=received.at[index],
            device_id=partner,
            device_id_type=MESH,
        )

    @pl.when(cell == 0)
    def _():
        greet([partner])
        for index in range(cells):
            swap(index).start()
        w_t[...] = w[...].T
        gain_c[...] = spread_column(gain[...])
        bias_c[...] = spread_column(bias[...])

    def norms(columns, row, line):
        for h in range(HEADS):
            part = columns[h * head : (h + 1) * head]
            size = jnp.sum(part * part, 0, keepdims=True)
            best = size[:, :128]
            for start in range(128, columns.shape[1], 128):
                best = jnp.maximum(best, size[:, start : start + 128])
            stat[0, row, line + h : line + h + 1, :] = best

    def tables(values, half, origin):
        lows = []
        for first in range(0, genes, PIECE):
            span = slice(half * genes + first, half * genes + first + PIECE)
            unit, _ = norm_columns(values[first : first + PIECE].T.astype(F32))
            ut[0, :, span] = unit.astype(BF16)
            low = unit * widen(gain_c[...], PIECE) + widen(bias_c[...], PIECE)
            spot = origin + first + lax.broadcasted_iota(jnp.int32, (1, PIECE), 1)
            valid = spot < counts[cell]
            kept = jnp.where(valid, low, 0.0).astype(BF16)
            lows.append(low.astype(BF16))
            packed_t = dot(w_t[width:, :], kept)
            mark = jnp.where(
                (lax.broadcasted_iota(jnp.int32, (16, PIECE), 0) < MARKS) & valid, 1.0, 0.0
            ).astype(BF16)
            for h in range(HEADS):
                rows = slice(width + h * head, width + (h + 1) * head)
                va[0, h, :head, span] = packed_t[rows].astype(BF16)
                va[0, h, head:, span] = mark
            kr[0, span, :] = packed_t[:width].astype(BF16).T
            norms(packed_t[:width], half * (genes // PIECE) + first // PIECE, 0)
        return lows

    stat[...] = jnp.zeros_like(stat)
    for i, low in enumerate(tables(x[0], 0, place * genes)):
        query_t = dot(w_t[:width, :], low).astype(BF16) * (head**-0.5)
        qt[0, :, i * PIECE : (i + 1) * PIECE] = query_t
        norms(query_t.astype(F32), i, HEADS)
    unit, _ = norm_rows(xc[0].astype(F32))
    class_low = (unit * gain[...] + bias[...]).astype(BF16)
    pc[0] = dot(class_low, w[...]).astype(BF16).astype(F32)
    swap(cell).wait_recv()
    tables(other[cell], 1, (1 - place) * genes)

    @pl.when(cell == cells - 1)
    def _():
        for index in range(cells):
            swap(index).wait_send()


def project(counts, x, xc, gain, bias, w):
    cells, genes, width = x.shape
    total = 2 * genes
    classes = xc.shape[1]
    head = width // HEADS
    pieces = total // PIECE
    whole = lambda shape: pl.BlockSpec(shape, lambda c: (0,) * len(shape))
    per_cell = lambda *shape: pl.BlockSpec((1,) + shape, lambda c: (c,) + (0,) * len(shape))
    out = lambda shape, kind=BF16: jax.ShapeDtypeStruct(shape, kind)
    return pl.pallas_call(
        project_kernel,
        grid=(cells,),
        in_specs=[
            pl.BlockSpec(memory_space=pltpu.SMEM),
            per_cell(genes, width),
            pl.BlockSpec(memory_space=pl.ANY),
            per_cell(classes, width),
            whole((1, width)),
            whole((1, width)),
            whole((width, 3 * width)),
        ],
        out_specs=[
            per_cell(width, genes),
            per_cell(total, width),
            per_cell(HEADS, head + 16, total),
            per_cell(width, total),
            per_cell(pieces, 8, 128),
            per_cell(classes, 3 * width),
        ],
        out_shape=[
            out((cells, width, genes)),
            out((cells, total, width)),
            out((cells, HEADS, head + 16, total)),
            out((cells, width, total)),
            out((cells, pieces, 8, 128), F32),
            out((cells, classes, 3 * width), F32),
        ],
        scratch_shapes=[
            pltpu.VMEM((3 * width, width), BF16),
            pltpu.VMEM((width, 128), F32),
            pltpu.VMEM((width, 128), F32),
            pltpu.VMEM((cells, genes, width), BF16),
            pltpu.SemaphoreType.DMA((cells,)),
            pltpu.SemaphoreType.DMA((cells,)),
        ],
        compiler_params=pltpu.CompilerParams(
            vmem_limit_bytes=VMEM, collective_id=0, has_side_effects=True
        ),
        name="project",
    )(counts, x, x, xc, gain, bias, w)


def gelu_parts(u):
    phi = 0.5 + 0.5 * lax.erf(u * 0.7071067811865476)
    bell = jnp.exp2((u * u) * (-0.5 * LOG2E))
    return u * phi, phi + (u * 0.3989422804014327) * bell


def layer_kernel(
    counts,
    place,
    qt,
    kr,
    va,
    ut,
    stat,
    pc,
    x,
    xc,
    cot,
    cotc,
    w_out,
    gain,
    bias,
    w_up,
    b_up,
    w_down,
    b_down,
    y,
    yc,
    dq,
    dqc,
    dkv,
    dkvc,
    gm,
    gmc,
    slab,
    g_vec,
    w_out_t,
    w_up_t,
    w_down_t,
    gain_c,
    bias_c,
    b_up_c,
    b_down_c,
    probs,
    probs_ck,
    probs_cq,
    mix,
    shift,
    shift_q,
    inv_sum,
    qz,
    da,
    delta,
    att,
    datt,
    dq_t,
    grads_t,
    up_acc,
    g_down,
    g_out,
    qkv_acc,
    up_bias_acc,
    gain_acc,
    bias_acc,
    down_bias_acc,
    packed_sum,
    packed_cols,
    class_units,
    class_packs,
    class_kept,
):
    cell = pl.program_id(0)
    cells = pl.num_programs(0)
    genes, width = x.shape[1:]
    classes = xc.shape[1]
    head = width // HEADS
    ff = w_up.shape[1]
    stack = HEADS * classes
    factor = head**-0.5
    count = counts[cell]
    own_count = jnp.clip(count - place[0] * genes, 0, genes)
    other_count = jnp.clip(count - (1 - place[0]) * genes, 0, genes)
    own_blocks = (own_count + (KB - 1)) // KB
    other_blocks = (other_count + (KB - 1)) // KB
    half_blocks = genes // KB
    blocks = own_blocks + other_blocks

    def nth_block(index):
        block = jnp.where(index < own_blocks, index, index - own_blocks + half_blocks)
        return pl.multiple_of(block * KB, KB)

    @pl.when(cell == 0)
    def _():
        w_out_t[...] = w_out[...].T
        w_up_t[...] = w_up[...].T
        w_down_t[...] = w_down[...].T
        gain_c[...] = spread_column(gain[...])
        bias_c[...] = spread_column(bias[...])
        b_up_c[...] = spread_column(b_up[...])
        b_down_c[...] = spread_column(b_down[...])
        up_acc[...] = jnp.zeros_like(up_acc)
        up_bias_acc[...] = jnp.zeros_like(up_bias_acc)
        gain_acc[...] = jnp.zeros_like(gain_acc)
        bias_acc[...] = jnp.zeros_like(bias_acc)
        down_bias_acc[...] = jnp.zeros_like(down_bias_acc)
        g_down[...] = jnp.zeros_like(g_down)
        g_out[...] = jnp.zeros_like(g_out)
        qkv_acc[...] = jnp.zeros_like(qkv_acc)
        packed_sum[...] = jnp.zeros_like(packed_sum)
        packed_cols[...] = jnp.zeros_like(packed_cols)

    head_mask = lax.broadcasted_iota(jnp.int32, (stack, width), 1) // head == (
        lax.broadcasted_iota(jnp.int32, (stack, width), 0) // classes
    )
    pair_mask = lax.broadcasted_iota(jnp.int32, (stack, stack), 1) // classes == (
        lax.broadcasted_iota(jnp.int32, (stack, stack), 0) // classes
    )

    def by_head(rows):
        return jnp.where(head_mask, jnp.concatenate([rows] * HEADS, 0), 0.0)

    def from_heads(rows):
        kept = jnp.where(head_mask, rows, 0.0)
        total = kept[:classes]
        for h in range(1, HEADS):
            total = total + kept[h * classes : (h + 1) * classes]
        return total

    class_lines = pl.ds(pl.multiple_of(cell * classes, classes), classes)
    packed_c = pc[0]
    query_c = by_head(packed_c[:, :width] * factor)
    key_c = by_head(packed_c[:, width : 2 * width])
    value_c = by_head(packed_c[:, 2 * width :])
    key_c_t = key_c.T.astype(BF16)
    value_c_t = value_c.T.astype(BF16)
    query_cb, key_cb, value_cb = query_c.astype(BF16), key_c.astype(BF16), value_c.astype(BF16)

    blank = jnp.zeros((head, genes), BF16)
    for h in range(HEADS):
        own = slice(h % 2 * head, (h % 2 + 1) * head)
        rest = slice((1 - h % 2) * head, (2 - h % 2) * head)
        qz[h, own, :] = qt[0, h * head : (h + 1) * head, :]
        qz[h, rest, :] = blank

    sizes = jnp.max(stat[0], 0)
    size_k, size_q = jnp.max(sizes[:HEADS]), jnp.max(sizes[HEADS:])
    size_k = jnp.maximum(size_k, jnp.max(jnp.sum(key_c * key_c, -1, keepdims=True)))
    size_q = jnp.maximum(size_q, jnp.max(jnp.sum(query_c * query_c, -1, keepdims=True)))
    safe = size_k * size_q < SAFE * SAFE

    def key_mask(start, shape, axis):
        limit = jnp.where(start < genes, own_count, genes + other_count)
        return start + lax.broadcasted_iota(jnp.int32, shape, axis) < limit

    shift[...] = jnp.zeros_like(shift)
    shift_q[...] = jnp.zeros_like(shift_q)

    @pl.when(jnp.logical_not(safe))
    def _():
        class_scores = dot(key_cb, qt[0])
        for h in range(HEADS):
            shift[h] = jnp.max(class_scores[h * classes : (h + 1) * classes], 0, keepdims=True)
        own_scores = jnp.where(pair_mask, dot(query_cb, key_c_t), -1e30)
        shift_q[...] = jnp.broadcast_to(jnp.max(own_scores, -1, keepdims=True), shift_q.shape)

        @pl.loop(0, blocks)
        def _(block):
            start = nth_block(block)
            for h in range(HEADS):
                scores = dot(
                    kr[0, pl.ds(start, KB), (h // 2) * 2 * head : (h // 2 + 1) * 2 * head], qz[h]
                )
                scores = jnp.where(key_mask(start, scores.shape, 0), scores, -1e30)
                shift[h] = jnp.maximum(shift[h], jnp.max(scores, 0, keepdims=True))
            scores = dot_nt(query_cb, kr[0, pl.ds(start, KB), :])
            scores = jnp.where(key_mask(start, scores.shape, 1), scores, -1e30)
            shift_q[...] = jnp.maximum(shift_q[...], jnp.max(scores, -1, keepdims=True))

        shift[...] = shift[...] * LOG2E
        shift_q[...] = shift_q[...] * LOG2E

    class_scores = dot(key_cb, qt[0])
    shift_rows = jnp.concatenate(
        [jnp.broadcast_to(shift[h], (classes, genes)) for h in range(HEADS)], 0
    )
    class_exp = jnp.exp2(class_scores * LOG2E - shift_rows).astype(BF16)
    probs_ck[...] = class_exp
    class_mix = dot(value_c_t, class_exp)
    for h in range(HEADS):
        mix[h, :head, :] = class_mix[h * head : (h + 1) * head]
        sums = jnp.sum(
            class_exp[h * classes : (h + 1) * classes].astype(F32), 0, keepdims=True
        )
        mix[h, head:, :] = jnp.where(
            lax.broadcasted_iota(jnp.int32, (16, genes), 0) == 0, sums, 0.0
        )
    shift_qc = shift_q[:, :1]
    own_exp = jnp.where(
        pair_mask, jnp.exp2(dot(query_cb, key_c_t) * LOG2E - shift_qc), 0.0
    ).astype(BF16)
    deep = head + 16

    def spread_heads(rows, extra):
        pieces = []
        for h in range(HEADS):
            pieces += [rows[:, h * head : (h + 1) * head], extra]
        return jnp.concatenate(pieces, 1)

    own_mix = spread_heads(
        dot(own_exp, value_cb),
        jnp.broadcast_to(jnp.sum(own_exp.astype(F32), -1, keepdims=True), (stack, 16)),
    )

    def forward_block(block, class_total, shifted):
        start = nth_block(block)
        keys = pl.ds(start, KB)
        scores = [
            dot(kr[0, keys, (h // 2) * 2 * head : (h // 2 + 1) * 2 * head], qz[h])
            for h in range(1)
        ]
        class_scores = dot_nt(query_cb, kr[0, keys, :]) * LOG2E - shift_qc
        all_values = va[0, :, :, keys].reshape(HEADS * deep, KB)
        for h in range(HEADS):
            if h + 1 < HEADS:
                g = h + 1
                scores.append(
                    dot(kr[0, keys, (g // 2) * 2 * head : (g // 2 + 1) * 2 * head], qz[g])
                )
            scaled = scores[h] * LOG2E
            if shifted:
                scaled = jnp.minimum(scaled - shift[h], 60.0)
            exps = jnp.exp2(scaled).astype(BF16)
            first = min(h * deep, HEADS * deep - 112)
            kept = slice(h * deep - first, (h + 1) * deep - first)
            mix[h] += dot(all_values[first : first + 112], exps)[kept]
            probs[h, :, keys] = exps.T
        class_exp = jnp.where(
            key_mask(start, class_scores.shape, 1), jnp.exp2(class_scores), 0.0
        ).astype(BF16)
        probs_cq[:, keys] = class_exp
        return class_total + dot_nt(class_exp, va[0, :, :, keys].reshape(HEADS * deep, KB))

    class_total = lax.cond(
        safe,
        lambda: paired_loop(blocks, functools.partial(forward_block, shifted=False), own_mix),
        lambda: lax.fori_loop(0, blocks, functools.partial(forward_block, shifted=True), own_mix),
    )
    class_sum = jnp.concatenate(
        [
            class_total[h * classes : (h + 1) * classes, h * deep + head : h * deep + head + 1]
            for h in range(HEADS)
        ],
        0,
    )
    class_total = jnp.concatenate(
        [class_total[:, h * deep : h * deep + head] for h in range(HEADS)], 1
    )
    class_inv = 1.0 / class_sum
    class_att = from_heads(class_total * class_inv)
    for h in range(HEADS):
        inverse = 1.0 / mix[h, head : head + 1, :]
        inv_sum[h] = inverse
        att[h * head : (h + 1) * head, :genes] = (mix[h, :head, :] * inverse).astype(BF16)

    def feed(start, lanes):
        span = pl.ds(start, lanes)
        wide_gain = widen(gain_c[...], lanes)
        cot_r = cot[0, span, :]
        cot_t = cot_r.T
        x_t = x[0, span, :].T
        parts = [slice(first, first + FF_STEP) for first in range(0, ff, FF_STEP)]
        held = {}

        def begin():
            held["att"] = att[:, span]
            middle = x_t.astype(F32) + dot(w_out_t[...], held["att"])
            held["unit"], held["inverse"] = norm_columns(middle)
            held["low"] = (held["unit"] * wide_gain + widen(bias_c[...], lanes)).astype(BF16)
            held["low_r"] = held["low"].T
            held["result"] = middle + widen(b_down_c[...], lanes)
            held["back"] = jnp.zeros((width, lanes), F32)

        def rise(part):
            up = dot(w_up_t[part, :], held["low"]) + widen(b_up_c[part, :], lanes)
            held[part.start] = up, dot(w_down[part, :], cot_t)

        def fall(part):
            up, grad_act = held.pop(part.start)
            active, slope = gelu_parts(up)
            active = active.astype(BF16)
            grad_up = slope * grad_act
            up_bias_acc[part, :] += fold_lanes(grad_up)
            grad_up = grad_up.astype(BF16)
            held["result"] += dot(w_down_t[:, part], active)
            held["back"] += dot(w_up[:, part], grad_up)
            g_down[part, :] += dot(active, cot_r)
            up_acc[part, :] += dot(grad_up, held["low_r"])

        def end():
            back, unit = held["back"], held["unit"]
            scaled = back * wide_gain
            scale = 1.0 / width
            grad_middle = cot_t.astype(F32) + held["inverse"] * (
                scaled
                - jnp.sum(scaled, 0, keepdims=True) * scale
                - unit * (jnp.sum(scaled * unit, 0, keepdims=True) * scale)
            )
            grad_middle = grad_middle.astype(BF16)
            datt[:, span] = dot(w_out[...], grad_middle).astype(BF16)
            gain_acc[...] += fold_lanes(back * unit)
            bias_acc[...] += fold_lanes(back)
            middle_r = grad_middle.T
            g_out[...] += dot(held["att"], middle_r)
            down_bias_acc[...] += jnp.sum(cot_r.astype(F32), 0, keepdims=True)
            y[0, span, :] = held["result"].T.astype(BF16)
            gm[0, span, :] = middle_r

        rises = [begin] + [functools.partial(rise, part) for part in parts]
        falls = [functools.partial(fall, part) for part in parts] + [end]
        return rises, falls

    feed_step = 512
    pieces = genes // feed_step
    rises, falls = [], []
    for piece in range(pieces):
        more_rises, more_falls = feed(piece * feed_step, feed_step)
        rises += more_rises
        falls += more_falls

    class_own = {}

    def keep(index, values):
        class_kept[index, class_lines, : values.shape[1]] = values.astype(F32)

    def class_begin():
        att_low = class_att.astype(BF16)
        keep(0, att_low)
        class_own["middle"] = xc[0].astype(F32) + dot(att_low, w_out[...])
        class_own["unit"], class_own["inverse"] = norm_rows(class_own["middle"])
        class_own["low"] = (class_own["unit"] * gain[...] + bias[...]).astype(BF16)
        keep(1, class_own["low"])

    def class_rise():
        class_own["up"] = dot(class_own["low"], w_up[...]) + b_up[...]
        class_own["grad_act"] = dot(cotc[0], w_down_t[...])

    def class_fall():
        active, slope = gelu_parts(class_own["up"])
        active, grad_up = active.astype(BF16), slope * class_own["grad_act"]
        keep(2, active)
        keep(3, grad_up)
        yc[0] = (class_own["middle"] + dot(active, w_down[...]) + b_down[...]).astype(BF16)
        class_own["back"] = dot(grad_up.astype(BF16), w_up_t[...])

    def class_end():
        back, unit = class_own["back"], class_own["unit"]
        keep(4, back * unit)
        keep(5, back)
        keep(6, cotc[0])
        scaled = back * gain[...]
        grad_middle = cotc[0].astype(F32) + class_own["inverse"] * (
            scaled
            - jnp.mean(scaled, -1, keepdims=True)
            - unit * jnp.mean(scaled * unit, -1, keepdims=True)
        )
        grad_middle = grad_middle.astype(BF16)
        keep(7, grad_middle)
        gmc[0] = grad_middle.astype(F32)
        class_own["datt"] = dot(grad_middle, w_out_t[...]).astype(BF16).astype(F32)

    class_steps = [class_begin, class_rise, class_fall, class_end]
    for i in range(len(rises) + FEED_AHEAD):
        if i < len(rises):
            rises[i]()
        if i < len(class_steps):
            class_steps[i]()
        if i >= FEED_AHEAD:
            falls[i - FEED_AHEAD]()

    for h in range(HEADS):
        own = slice(h * head, (h + 1) * head)
        inverse = inv_sum[h]
        grad = (datt[own, :genes].astype(F32) * inverse).astype(BF16)
        row_delta = jnp.sum(grad.astype(F32) * (mix[h, :head, :] * inverse), 0, keepdims=True)
        delta[h] = row_delta
        datt[own, :genes] = grad
        parts = jnp.zeros((16, genes), F32)
        rest = row_delta
        for i in range(MARKS):
            piece = rest.astype(BF16).astype(F32)
            rest = rest - piece
            parts = jnp.where(
                lax.broadcasted_iota(jnp.int32, (16, genes), 0) == i, -piece, parts
            )
        blank = jnp.zeros((2 * head - deep, genes), BF16)
        da[h] = jnp.concatenate([grad, parts.astype(BF16), blank], 0).T

    class_grad = by_head(class_own["datt"]) * class_inv
    class_grad_b = class_grad.astype(BF16)
    class_grad_h = (class_grad * 0.5).astype(BF16)
    query_ch = (query_c * 0.5).astype(BF16)
    class_delta = jnp.sum(
        class_grad_b.astype(F32) * (class_total * class_inv), -1, keepdims=True
    )

    class_dprob = dot(value_cb, datt[:, :genes])
    delta_rows = jnp.concatenate(
        [jnp.broadcast_to(delta[h], (classes, genes)) for h in range(HEADS)], 0
    )
    class_probs = probs_ck[...]
    class_dscore = (class_probs.astype(F32) * (class_dprob - delta_rows)).astype(BF16)
    dq_t[...] = dot(key_c_t, class_dscore)
    class_dkey = dot_nt(class_dscore, qt[0])
    class_dvalue = dot_nt(class_probs, datt[:, :genes])
    own_dprob = dot(class_grad_b, value_c_t)
    own_dscore = (own_exp.astype(F32) * (own_dprob - class_delta)).astype(BF16)
    class_dquery = dot(own_dscore, key_cb)
    class_dkey = class_dkey + dot(own_dscore.astype(F32).T.astype(BF16), query_ch)
    class_dvalue = class_dvalue + dot(own_exp.astype(F32).T.astype(BF16), class_grad_h)

    class_grad_s = spread_heads(class_grad_b, jnp.zeros((stack, 16), BF16))
    class_grad_ht = class_grad_h.T
    query_ct = query_ch.T

    def settle(start):
        keys = pl.ds(pl.multiple_of(start, KB), KB)
        grads = grads_t[...].T
        dkv[0, keys, :] = grads
        qkv_acc[:, width:] += dot(ut[0, :, keys], grads)

    def backward_block(block, carried):
        class_dquery, previous = carried
        start = nth_block(block)
        keys = pl.ds(start, KB)
        dprobs = [dot(da[h, :, :deep], va[0, h, :, keys]) for h in range(AHEAD)]
        settle(previous)
        class_weights = probs_cq[:, keys]
        class_dprob = dot(class_grad_s, va[0, :, :, keys].reshape(HEADS * deep, KB))
        class_dscore = (class_weights.astype(F32) * (class_dprob - class_delta)).astype(BF16)
        dkeys, dvalues, dscores = [], [], []
        key_t = kr[0, keys, :].T
        for h in range(HEADS + 1):
            if h + AHEAD < HEADS:
                dprobs.append(dot(da[h + AHEAD, :, :deep], va[0, h + AHEAD, :, keys]))
            if h < HEADS:
                weights = probs[h, :, keys]
                dscore = weights * dprobs[h].astype(BF16)
                dscores.append(dscore)
                spot = slice(h % 2 * 2, h % 2 * 2 + 2)
                qz[spot] = dscore.T.reshape(2, KB // 2, genes)
                own = slice(h * head, (h + 1) * head)
                pair = slice((h // 2) * 2 * head, (h // 2 + 1) * 2 * head)
                kept = slice(h % 2 * head, (h % 2 + 1) * head)
                dvalues.append(dot(datt[pair, :genes], weights)[kept])
                dkeys.append(dot(qt[0, pair, :], dscore)[kept])
            if h > 0:
                own = slice((h - 1) * head, h * head)
                spot = slice((h - 1) % 2 * 2, (h - 1) % 2 * 2 + 2)
                pair = slice(((h - 1) // 2) * 2 * head, ((h - 1) // 2 + 1) * 2 * head)
                kept = slice((h - 1) % 2 * head, ((h - 1) % 2 + 1) * head)
                dq_t[own, :] += dot(key_t[pair, :], qz[spot].reshape(KB, genes))[kept]
        class_dquery = class_dquery + dot(class_dscore, kr[0, keys, :])
        dkey = jnp.concatenate(dkeys, 0) + dot(query_ct, class_dscore)
        dvalue = jnp.concatenate(dvalues, 0) + dot(class_grad_ht, class_weights)
        valid = key_mask(start, (1, KB), 1)
        grads = jnp.where(valid, jnp.concatenate([dkey, dvalue], 0), 0.0)
        packed_cols[...] += fold_lanes(grads)
        grads_t[...] = grads.astype(BF16)
        return class_dquery, start

    grads_t[...] = jnp.zeros_like(grads_t)
    class_dquery, previous = paired_loop(
        blocks, backward_block, (class_dquery, nth_block(0))
    )
    settle(previous)

    def blank_rows(block):
        dkv[0, pl.ds(pl.multiple_of(block * KB, KB), KB), :] = jnp.zeros((KB, 2 * width), BF16)

    pl.loop(own_blocks, half_blocks)(blank_rows)
    pl.loop(half_blocks + other_blocks, 2 * half_blocks)(blank_rows)

    dquery_r = (dq_t[...] * factor).astype(BF16).T
    dq[0] = dquery_r
    qkv_acc[:, :width] += dot(ut[0, :, :genes], dquery_r)
    class_dquery = from_heads(class_dquery) * factor
    class_dkv = jnp.concatenate([from_heads(class_dkey), from_heads(class_dvalue)], 1)
    dqc[0] = class_dquery
    dkvc[0] = class_dkv
    class_packed = jnp.concatenate([class_dquery * 0.5, class_dkv], 1)
    class_unit, _ = norm_rows(xc[0].astype(F32))
    class_units[class_lines, :] = class_unit
    class_packs[class_lines, :] = class_packed
    packed_sum[:, :width] += jnp.sum(dquery_r.astype(F32), 0, keepdims=True)
    packed_sum[...] += jnp.sum(class_packed, 0, keepdims=True)

    @pl.when(cell == cells - 1)
    def _():
        first = 0

        def put(values):
            nonlocal first
            rows = values.shape[0]
            for start in range(0, values.shape[1], 128):
                slab[first : first + rows, :] = values[:, start : start + 128].astype(BF16)
                first += rows

        qkv_acc[...] += dot(
            class_units[...].T.astype(BF16), class_packs[...].astype(BF16)
        )
        att_low, low, active, grad_up, back_unit, back, cots, grad_middle = [
            class_kept[i, :, : (ff if i in (2, 3) else width)] for i in range(8)
        ]
        halved = lambda rows: (rows * 0.5).astype(BF16)
        half_sum = lambda rows: 0.5 * jnp.sum(rows, 0, keepdims=True)
        up_acc[...] += dot(grad_up.T.astype(BF16), halved(low))
        g_down[...] += dot(active.T.astype(BF16), halved(cots))
        g_out[...] += dot(att_low.T.astype(BF16), halved(grad_middle))
        put(up_acc[...].T)
        put(g_down[...])
        put(g_out[...])
        put(qkv_acc[...])
        if first < slab.shape[0]:
            slab[first:, :] = jnp.zeros((slab.shape[0] - first, 128), BF16)
        g_vec[...] = jnp.zeros_like(g_vec)
        line = 0
        for vector in (
            jnp.sum(up_bias_acc[...].T, 0, keepdims=True) + half_sum(grad_up),
            jnp.sum(gain_acc[...].T, 0, keepdims=True) + half_sum(back_unit),
            jnp.sum(bias_acc[...].T, 0, keepdims=True) + half_sum(back),
            down_bias_acc[...] + half_sum(cots),
            packed_sum[...]
            + jnp.concatenate(
                [jnp.zeros((1, width), F32), jnp.sum(packed_cols[...].T, 0, keepdims=True)], 1
            ),
        ):
            for start in range(0, vector.shape[1], 128):
                g_vec[line : line + 1, :] = vector[:, start : start + 128]
                line += 1


def layer(
    counts, place, tables, x, xc, cot, cotc, w_out, gain, bias, w_up, b_up, w_down, b_down
):
    cells, genes, width = x.shape
    classes = xc.shape[1]
    total = tables[1].shape[1]
    head = width // HEADS
    ff = w_up.shape[1]
    stack = HEADS * classes
    slab_rows = Reduction.padded((2 * ff + 4 * width) * width // 128, lax.axis_size("cell"))
    whole = lambda shape: pl.BlockSpec(
        shape, lambda c, *_: (0,) * len(shape), pipeline_mode=pl.Buffered(1)
    )
    per_cell = lambda *shape: pl.BlockSpec((1,) + shape, lambda c, *_: (c,) + (0,) * len(shape))
    kept = lambda *shape: whole(shape)
    out = lambda shape, kind=BF16: jax.ShapeDtypeStruct(shape, kind)
    vmem = lambda *shape, kind=BF16: pltpu.VMEM(shape, kind)
    f32 = functools.partial(vmem, kind=F32)
    return pl.pallas_call(
        layer_kernel,
        grid_spec=pltpu.PrefetchScalarGridSpec(
            num_scalar_prefetch=2,
            grid=(cells,),
            in_specs=[
                per_cell(width, genes),
                per_cell(total, width),
                per_cell(HEADS, head + 16, total),
                per_cell(width, total),
                per_cell(total // PIECE, 8, 128),
                per_cell(classes, 3 * width),
                per_cell(genes, width),
                per_cell(classes, width),
                per_cell(genes, width),
                per_cell(classes, width),
                whole((width, width)),
                whole((1, width)),
                whole((1, width)),
                whole((width, ff)),
                whole((1, ff)),
                whole((ff, width)),
                whole((1, width)),
            ],
            out_specs=[
                per_cell(genes, width),
                per_cell(classes, width),
                per_cell(genes, width),
                per_cell(classes, width),
                per_cell(total, 2 * width),
                per_cell(classes, 2 * width),
                per_cell(genes, width),
                per_cell(classes, width),
                kept(slab_rows, 128),
                kept(VECTOR_ROWS, 128),
            ],
            scratch_shapes=[
                vmem(width, width),
                vmem(ff, width),
                vmem(width, ff),
                f32(width, 128),
                f32(width, 128),
                f32(ff, 128),
                f32(width, 128),
                vmem(HEADS, genes, total),
                vmem(stack, genes),
                vmem(stack, total),
                f32(HEADS, head + 16, genes),
                f32(HEADS, 1, genes),
                f32(stack, 128),
                f32(HEADS, 1, genes),
                vmem(HEADS, 2 * head, genes),
                vmem(HEADS, genes, 2 * head),
                f32(HEADS, 1, genes),
                vmem(width, genes),
                vmem(width, genes),
                f32(width, genes),
                vmem(2 * width, KB),
                f32(ff, width),
                f32(ff, width),
                f32(width, width),
                f32(width, 3 * width),
                f32(ff, 128),
                f32(width, 128),
                f32(width, 128),
                f32(1, width),
                f32(1, 3 * width),
                f32(2 * width, 128),
                f32(cells * classes, width),
                f32(cells * classes, 3 * width),
                f32(8, cells * classes, ff),
            ],
        ),
        out_shape=[
            out((cells, genes, width)),
            out((cells, classes, width)),
            out((cells, genes, width)),
            out((cells, classes, width), F32),
            out((cells, total, 2 * width)),
            out((cells, classes, 2 * width), F32),
            out((cells, genes, width)),
            out((cells, classes, width), F32),
            out((slab_rows, 128)),
            out((VECTOR_ROWS, 128), F32),
        ],
        compiler_params=pltpu.CompilerParams(vmem_limit_bytes=VMEM),
        name="layer",
    )(counts, place, *tables, x, xc, cot, cotc, w_out, gain, bias, w_up, b_up, w_down, b_down)


class Reduction:
    @staticmethod
    def groups(cells):
        bits = (cells - 1).bit_length()
        return [(shift, min(2, bits - shift)) for shift in range(0, bits, 2)]

    @staticmethod
    def streams(rows, cells):
        groups = Reduction.groups(cells)
        unit = 2 * 16 * cells
        units = -(-rows // unit)
        kinds = min(len(groups), units)
        shares = [units // kinds] * kinds
        if kinds == 2:
            shares[1] = max(1, units // 3)
        shares[0] = units - sum(shares[1:])
        result, first = [], 0
        for turn in range(CUTS):
            for i, share in enumerate(shares):
                share = share * (turn + 1) // CUTS - share * turn // CUTS
                if share:
                    result.append((first, share * unit, groups[i:] + groups[:i]))
                    first += share * unit
        return result

    @staticmethod
    def padded(rows, cells):
        first, size, _ = Reduction.streams(rows, cells)[-1]
        return first + size

    @staticmethod
    def scratch(rows, cells):
        rows = Reduction.padded(rows, cells)
        hops = 2 + 2 * sum((1 << bits) - 1 for _, bits in Reduction.groups(cells))
        sems = (len(Reduction.streams(rows, cells)), hops)
        return [
            pltpu.VMEM((rows // 2, 128), BF16),
            pltpu.VMEM((rows, 128), BF16),
            pltpu.VMEM((rows, 128), BF16),
            pltpu.SemaphoreType.DMA(sems),
            pltpu.SemaphoreType.DMA(sems),
        ]

    def __init__(self, source, cells, work, inbox, total, sent, received):
        self.source, self.work, self.inbox, self.total = source, work, inbox, total
        self.sent, self.received = sent, received
        self.plan = self.streams(source.shape[0], cells)
        self.depth = len(self.groups(cells))
        self.stages = 2 * self.depth + 3
        self.me, self.place = lax.axis_index("cell"), lax.axis_index("gene")

    def peer(self, group, ahead):
        shift, bits = group
        radix = 1 << bits
        digit = (self.me // (1 << shift)) % radix
        there = (digit + ahead) % radix
        return {"cell": self.me + (there - digit) * (1 << shift), "gene": self.place}, there

    def digit(self, group):
        return (self.me // (1 << group[0])) % (1 << group[1])

    def held(self, stream, level):
        _, rows, order = self.plan[stream]
        first, size = 0, rows // 2
        for group in order[:level]:
            size = size >> group[1]
            first = first + self.digit(group) * size
        return first, size

    def slot(self, stream, level):
        first, rows, order = self.plan[stream]
        size = rows // 2
        spot = first
        for i in range(level):
            spot += size if i == 0 else ((1 << order[i - 1][1]) - 1) * size
            size = size >> order[i][1] if i < len(order) else size
        return spot

    def copy(self, source, target, stream, hop, ahead, device):
        return pltpu.make_async_remote_copy(
            src_ref=source,
            dst_ref=target,
            send_sem=self.sent.at[stream, hop + ahead - 1],
            recv_sem=self.received.at[stream, hop + ahead - 1],
            device_id=device,
            device_id_type=MESH,
        )

    def hop(self, stream, index):
        peers = [1] + [(1 << bits) - 1 for _, bits in self.plan[stream][2]]
        return sum((peers + peers[::-1])[:index])

    def rows(self, first, size):
        return pl.ds(pl.multiple_of(first, 16), size)

    def scatter(self, stream, level):
        first, rows, order = self.plan[stream]
        half = rows // 2
        if level == 0:
            mate = {"cell": self.me, "gene": 1 - self.place}
            source = self.source.at[self.rows(first + (1 - self.place) * half, half), :]
            target = self.inbox.at[pl.ds(first, half), :]
            return [self.copy(source, target, stream, 0, 1, mate)]
        group = order[level - 1]
        start, size = self.held(stream, level - 1)
        size = size >> group[1]
        copies = []
        for ahead in range(1, 1 << group[1]):
            device, there = self.peer(group, ahead)
            source = self.work.at[self.rows(first // 2 + start + there * size, size), :]
            target = self.inbox.at[pl.ds(self.slot(stream, level) + (ahead - 1) * size, size), :]
            copies.append(self.copy(source, target, stream, self.hop(stream, level), ahead, device))
        return copies

    def add(self, stream, level):
        first, rows, order = self.plan[stream]
        half = rows // 2
        start, size = self.held(stream, level)
        if level == 0:
            value = self.source[self.rows(first + self.place * half, half), :].astype(F32)
            count = 1
        else:
            value = self.work[self.rows(first // 2 + start, size), :].astype(F32)
            count = (1 << order[level - 1][1]) - 1
        for i in range(count):
            value += self.inbox[pl.ds(self.slot(stream, level) + i * size, size), :].astype(F32)
        if level == self.depth:
            self.total[self.rows(first + self.place * half + start, size), :] = value.astype(BF16)
        else:
            self.work[self.rows(first // 2 + start, size), :] = value.astype(BF16)

    def gather(self, stream, level):
        first, rows, order = self.plan[stream]
        half = rows // 2
        start, size = self.held(stream, level)
        span = self.total.at[self.rows(first + self.place * half + start, size), :]
        hop = self.hop(stream, 2 * self.depth + 1 - level)
        if level == 0:
            mate = {"cell": self.me, "gene": 1 - self.place}
            return [self.copy(span, span, stream, hop, 1, mate)]
        group = order[level - 1]
        return [
            self.copy(span, span, stream, hop, ahead, self.peer(group, ahead)[0])
            for ahead in range(1, 1 << group[1])
        ]

    def copies(self, stream, index):
        if index <= self.depth:
            return self.scatter(stream, index)
        return self.gather(stream, 2 * self.depth + 1 - index)

    def stage(self, index):
        for stream in range(len(self.plan)):
            if index > 0:
                for copy in self.copies(stream, index - 1):
                    copy.wait()
                if index - 1 <= self.depth:
                    self.add(stream, index - 1)
            if index < self.stages - 1:
                for copy in self.copies(stream, index):
                    copy.start()


class VectorSum:
    @staticmethod
    def scratch(shape, cells):
        groups = Reduction.groups(cells)
        return [
            pltpu.VMEM((2 + sum(1 << bits for _, bits in groups),) + shape, F32),
            pltpu.SemaphoreType.DMA((len(groups) + 1, 3)),
            pltpu.SemaphoreType.DMA((len(groups) + 1, 3)),
        ]

    def __init__(self, cells, reduction, slots, sent, received):
        self.reduction, self.slots, self.sent, self.received = reduction, slots, sent, received
        self.groups = reduction.groups(cells)

    def first(self, level):
        return 0 if level == 0 else 2 + sum(1 << bits for _, bits in self.groups[: level - 1])

    def size(self, level):
        return 2 if level == 0 else 1 << self.groups[level - 1][1]

    def copies(self, level):
        r = self.reduction
        if level == 0:
            mine = r.place
            devices = [{"cell": r.me, "gene": 1 - r.place}]
        else:
            group = self.groups[level - 1]
            mine = r.digit(group)
            devices = [r.peer(group, ahead)[0] for ahead in range(1, self.size(level))]
        spot = self.slots.at[self.first(level) + mine]
        return mine, [
            pltpu.make_async_remote_copy(
                src_ref=spot,
                dst_ref=spot,
                send_sem=self.sent.at[level, i],
                recv_sem=self.received.at[level, i],
                device_id=device,
                device_id_type=MESH,
            )
            for i, device in enumerate(devices)
        ]

    def start(self, level, value):
        mine, copies = self.copies(level)
        self.slots[self.first(level) + mine] = value
        for copy in copies:
            copy.start()

    def finish(self, level):
        for copy in self.copies(level)[1]:
            copy.wait()
        first = self.first(level)
        total = self.slots[first]
        for i in range(1, self.size(level)):
            total = total + self.slots[first + i]
        return total

    def stage(self, index, value):
        levels = len(self.groups)
        if 0 < index <= levels + 1:
            value = self.finish(index - 1)
        if index <= levels:
            self.start(index, value)
        return value if index == levels + 1 else None


def finish_kernel(
    slab,
    vec,
    x,
    gm,
    dq,
    dkv,
    dkv_hbm,
    xc,
    gmc,
    dqc,
    dkvc,
    gain,
    bias,
    w,
    g_x,
    g_xc,
    slab_out,
    vec_out,
    w_t,
    other,
    other_c,
    swap_send,
    swap_recv,
    class_send,
    class_recv,
    *reduction_scratch,
):
    step, steps = pl.program_id(0), pl.num_programs(0)
    cells = dkv_hbm.shape[0]
    genes = dkv_hbm.shape[1] // 2
    rows, width = x.shape[1:]
    classes = xc.shape[1]
    per_cell = genes // rows
    all_cells = lax.axis_size("cell")
    sums = Reduction(slab, all_cells, *reduction_scratch[:5])
    vectors = VectorSum(all_cells, sums, *reduction_scratch[5:])
    mate = {"cell": sums.me, "gene": 1 - sums.place}

    def swap(cell):
        return pltpu.make_async_remote_copy(
            src_ref=dkv_hbm.at[cell, pl.ds(genes, genes), :],
            dst_ref=other.at[cell],
            send_sem=swap_send.at[cell],
            recv_sem=swap_recv.at[cell],
            device_id=mate,
            device_id_type=MESH,
        )

    def swap_class():
        return pltpu.make_async_remote_copy(
            src_ref=dkvc,
            dst_ref=other_c,
            send_sem=class_send,
            recv_sem=class_recv,
            device_id=mate,
            device_id_type=MESH,
        )

    def stage(index):
        sums.stage(index)
        done = vectors.stage(index, vec[...] if index == 0 else None)
        if done is not None:
            vec_out[...] = done

    def rows_back(values, grads, packed):
        unit, inverse = norm_rows(values)
        scaled = dot(packed, w_t[...]) * gain[...]
        return grads + inverse * (
            scaled
            - jnp.mean(scaled, -1, keepdims=True)
            - unit * jnp.mean(scaled * unit, -1, keepdims=True)
        )

    for index, at in enumerate(STAGES):

        @pl.when(step == at)
        def _(index=index):
            if index == 0:
                partners = [mate]
                for group in sums.groups(all_cells):
                    for ahead in range(1, 1 << group[1]):
                        partners.append(sums.peer(group, ahead)[0])
                greet(partners)
            stage(index)
            if index == 0:
                for cell in range(cells):
                    swap(cell).start()
                swap_class().start()
                w_t[...] = w[...].T

    cell = step // per_cell

    @pl.when(step % per_cell == 0)
    def _():
        swap(cell).wait()

    grads = dkv[0].astype(F32) + other[
        cell, pl.ds(pl.multiple_of((step % per_cell) * rows, 16), rows), :
    ].astype(F32)
    packed = jnp.concatenate([dq[0], grads.astype(BF16)], 1)
    g_x[0] = rows_back(x[0].astype(F32), gm[0].astype(F32), packed).astype(BF16)

    @pl.when(step == steps - 1)
    def _():
        swap_class().wait()
        class_grads = dkvc[...] + other_c[...]
        stack = cells * classes
        packed = jnp.concatenate([dqc[...], class_grads], 2).reshape(stack, 3 * width)
        values = xc[...].astype(F32).reshape(stack, width)
        result = rows_back(values, gmc[...].reshape(stack, width), packed.astype(BF16))
        g_xc[...] = result.reshape(cells, classes, width)
        for index in range(len(STAGES), sums.stages):
            stage(index)
        slab_out[...] = sums.total[...]


def finish(slab, vec, x, xc, gm, gmc, dq, dqc, dkv, dkvc, gain, bias, w):
    cells, genes, width = x.shape
    classes = xc.shape[1]
    rows = genes // 2
    per_cell = genes // rows
    all_cells = lax.axis_size("cell")
    whole = lambda array: pl.BlockSpec(array.shape, lambda i: (0,) * array.ndim)
    piece = lambda lanes: pl.BlockSpec((1, rows, lanes), lambda i: (i // per_cell, i % per_cell, 0))
    out = lambda shape, kind=BF16: jax.ShapeDtypeStruct(shape, kind)
    dma = lambda *shape: pltpu.SemaphoreType.DMA(shape)
    outs = [
        out((cells, genes, width)),
        out((cells, classes, width), F32),
        out(slab.shape),
        out(vec.shape, F32),
    ]
    return pl.pallas_call(
        finish_kernel,
        grid=(cells * per_cell,),
        in_specs=[
            whole(slab),
            whole(vec),
            piece(width),
            piece(width),
            piece(width),
            piece(2 * width),
            pl.BlockSpec(memory_space=pl.ANY),
            whole(xc),
            whole(gmc),
            whole(dqc),
            whole(dkvc),
            whole(gain),
            whole(bias),
            whole(w),
        ],
        out_specs=[piece(width)] + [whole(o) for o in outs[1:]],
        out_shape=outs,
        scratch_shapes=[
            pltpu.VMEM((3 * width, width), BF16),
            pltpu.VMEM((cells, genes, 2 * width), BF16),
            pltpu.VMEM(dkvc.shape, F32),
            dma(cells),
            dma(cells),
            dma(),
            dma(),
        ]
        + Reduction.scratch(slab.shape[0], all_cells)
        + VectorSum.scratch(vec.shape, all_cells),
        compiler_params=pltpu.CompilerParams(
            vmem_limit_bytes=VMEM, collective_id=1, has_side_effects=True
        ),
        name="finish",
    )(slab, vec, x, gm, dq, dkv, dkv, xc, gmc, dqc, dkvc, gain, bias, w)


def unpack_kernel(slab, vec, gain, bias, w, x, xc, g_x, g_up, g_down, g_out, g_qkv, g_xc, *rest):
    *vectors, up, down, out, qkv, passing, sems = rest
    width, ff = up.shape
    copies = [
        pltpu.make_async_copy(source, target, sems.at[i])
        for i, (source, target) in enumerate(
            [(x, passing), (up, g_up), (down, g_down), (out, g_out), (qkv, g_qkv), (passing, g_x)]
        )
    ]
    copies[0].start()
    first = 0

    def take(target):
        nonlocal first
        rows = target.shape[0]
        for start in range(0, target.shape[1], 128):
            target[:, start : start + 128] = slab[first : first + rows, :].astype(F32)
            first += rows

    for copy, target in zip(copies[1:4], (up, down, out)):
        take(target)
        copy.start()
    copies[0].wait()
    copies[5].start()
    take(qkv)
    line = 0

    def lines(count):
        nonlocal line
        line += count
        return jnp.concatenate([vec[i : i + 1, :] for i in range(line - count, line)], 1)

    up_bias, ln2_gain, ln2_bias, down_bias, ln1_gain, ln1_bias = vectors
    up_bias[...] = lines(ff // 128)
    ln2_gain[...] = lines(width // 128)
    ln2_bias[...] = lines(width // 128)
    down_bias[...] = lines(width // 128)
    packed_sum = lines(3 * width // 128)
    weights = w[...].astype(F32)
    sums = qkv[...]
    qkv[...] = (
        widen(spread_column(gain[...]), 3 * width) * sums
        + widen(spread_column(bias[...]), 3 * width) * packed_sum
    )
    copies[4].start()
    ln1_gain[...] = jnp.sum((weights * sums).T, 0, keepdims=True)
    ln1_bias[...] = jnp.sum((weights * packed_sum).T, 0, keepdims=True)
    g_xc[...] = xc[...].astype(BF16)
    for copy in copies[1:]:
        copy.wait()


def unpack(slab, vec, gain, bias, w, x, xc, ff):
    width = w.shape[0]
    out = lambda *shape: jax.ShapeDtypeStruct(shape, F32)
    row = out(1, width)
    sums = [(width, ff), (ff, width), (width, width), (width, 3 * width)]
    anywhere = pl.BlockSpec(memory_space=pl.ANY)
    local = pl.BlockSpec(memory_space=pltpu.VMEM)
    return pl.pallas_call(
        unpack_kernel,
        in_specs=[local] * 5 + [anywhere, local],
        out_specs=[anywhere] * 5 + [local] * 7,
        out_shape=[jax.ShapeDtypeStruct(x.shape, BF16)]
        + [out(*shape) for shape in sums]
        + [jax.ShapeDtypeStruct(xc.shape, BF16), out(1, ff), row, row, row, row, row],
        scratch_shapes=[pltpu.VMEM(shape, F32) for shape in sums]
        + [pltpu.VMEM(x.shape, BF16), pltpu.SemaphoreType.DMA((6,))],
        compiler_params=pltpu.CompilerParams(vmem_limit_bytes=VMEM),
        name="unpack",
    )(slab, vec, gain, bias, w, x, xc)


def shards(
    gene_in,
    class_in,
    expressed,
    ln1_gain,
    ln1_bias,
    w_qkv,
    w_out,
    ln2_gain,
    ln2_bias,
    w_up,
    b_up,
    w_down,
    b_down,
    gene_cot,
    class_cot,
):
    row = lambda vector: vector.reshape(1, -1)
    place = lax.axis_index("gene").reshape(1)
    gain1, bias1 = row(ln1_gain), row(ln1_bias)
    tables = project(expressed, gene_in, class_in, gain1, bias1, w_qkv)
    gene_out, class_out, dq, dqc, dkv, dkvc, gm, gmc, slab, vec = layer(
        expressed,
        place,
        tables,
        gene_in,
        class_in,
        gene_cot,
        class_cot,
        w_out,
        row(ln2_gain),
        row(ln2_bias),
        w_up,
        row(b_up),
        w_down,
        row(b_down),
    )
    gene_grad, class_grad, slab, vec = finish(
        slab, vec, gene_in, class_in, gm, gmc, dq, dqc, dkv, dkvc, gain1, bias1, w_qkv
    )
    (
        gene_grad,
        g_up,
        g_down,
        g_out,
        g_qkv,
        class_grad,
        g_b_up,
        g_gain2,
        g_bias2,
        g_b_down,
        g_gain1,
        g_bias1,
    ) = unpack(slab, vec, gain1, bias1, w_qkv, gene_grad, class_grad, w_up.shape[1])
    return (
        gene_out,
        class_out,
        gene_grad,
        class_grad,
        g_gain1[0],
        g_bias1[0],
        g_qkv,
        g_out,
        g_gain2[0],
        g_bias2[0],
        g_up,
        g_b_up[0],
        g_down,
        g_b_down[0],
    )


def solution(mesh):
    genes, cells, whole = P("cell", "gene", None), P("cell", None, None), P()
    return jax.shard_map(
        shards,
        mesh=mesh,
        in_specs=(genes, cells, P("cell")) + (whole,) * 10 + (genes, cells),
        out_specs=(genes, cells, genes, cells) + (whole,) * 10,
        check_vma=False,
    )
```
